256 devices in a mesh: seq: 32 (over y, z_hi, core), blk: 8 (over z_lo, x).
Axes of the slice: x: 4, y: 4, z: 8 (z_hi: 4, z_lo: 2; z = z_hi * 2 + z_lo), core: 2. Of those that a mesh axis runs over, the one named last changes fastest.
Arguments:
- query_vectors: bfloat16 [12288, 4096], P(('seq', 'blk')), may hold values from -120 to 120
- key_vectors: bfloat16 [12288, 4096], P(('seq', 'blk')), may hold values from -9 to 9
- value_vectors: bfloat16 [12288, 4096], P(('seq', 'blk')), may hold values from -6 to 6
- weight_head: bfloat16 [4096, 64], replicated, may hold values from -0.5 to 0.5
- noisy_latent: float32 [4, 128, 96, 16], P(None, 'seq', 'blk'), may hold values from -6 to 6
- noise_level: float32 [1], replicated, may hold values from 0.5 to 1
- latent_mean: float32 [16], replicated, may hold values from -3 to 3
- latent_scale: float32 [16], replicated, may hold values from 0.5 to 2
- cache_in: bfloat16 [2, 128, 96, 16], P(None, 'seq', 'blk'), may hold values from -6 to 6
- weight_in: bfloat16 [3, 3, 3, 16, 384], replicated, may hold values from -0.3125 to 0.3125
- bias_in: float32 [384], replicated, may hold values from -3 to 3
- norm_gain: float32 [384], replicated, may hold values from 0.5 to 1.5
- cache_mid: bfloat16 [2, 128, 96, 384], P(None, 'seq', 'blk'), may hold values from -6 to 6
- weight_mid: bfloat16 [3, 3, 3, 384, 384], replicated, may hold values from -0.0625 to 0.0625
- bias_mid: float32 [384], replicated, may hold values from -3 to 3
Outputs:
- denoised: float32 [4, 128, 96, 16], P(None, 'seq', 'blk')
- features: bfloat16 [4, 128, 96, 384], P(None, 'seq', 'blk')
The draws below stay inside these ranges and needn't reach their ends.
All inputs are finite; a program needn't handle non-finite values.
Results may differ from the reference program's by a relative error of at most 0.011.
Values may be sent and summed in bfloat16 or wider, within the bound.
No kernel may reach another device: no remote copies, remote signals or barrier semaphores. Data moves between devices by JAX's collectives and lax.ppermute only.
A program may use at most 128 MiB of HBM per device.

```python
import math
import jax
import jax.numpy as jnp
from jax import lax

HEAD_DIM = 128
HEADS = 32
LAT = 16
PATCH = 64
C1 = 384
F = 4
TR = 2
WP = 48
ROWS = 128
COLS = 96
TOKENS = 12288
N_SEQ = 32


def shared_keys(key):
    base_draw = jax.random.normal(key, (TOKENS, HEADS * HEAD_DIM), jnp.float32) * 1.41
    return jnp.clip(base_draw, -8.5, 8.5)


def draw_key_vectors(key, part):
    base_draw = shared_keys(key)
    return base_draw.astype(jnp.bfloat16)


def draw_query_vectors(key, part):
    key = jax.random.fold_in(key, 5)
    base_draw = jax.random.normal(key, (TOKENS, HEADS * HEAD_DIM), jnp.float32) * 1.41
    return jnp.clip(base_draw, -8.5, 8.5).astype(jnp.bfloat16)


def block_levels(key, shape, cuts, smallest, largest):
    level = 1.0
    for position, shards_of in cuts:
        heights = jax.random.uniform(jax.random.fold_in(jax.random.fold_in(key, 6), position), (shards_of,), jnp.float32, smallest / len(cuts), largest / len(cuts))
        level = level * jnp.repeat(jnp.exp(heights), shape[position] // shards_of).reshape((-1,) + (1,) * (len(shape) - 1 - position))
    return level


def centred(own_key, extent, deviation, reach, pieces=(), kind=jnp.bfloat16):
    gain = block_levels(own_key, extent, pieces, -0.22, 0.18) if pieces else 1.0
    drawn = jax.random.normal(own_key, extent, jnp.float32) * deviation * gain
    return jnp.minimum(jnp.maximum(drawn, -reach), reach).astype(kind)


def setup_inputs(seed: int = 0) -> dict:
    key_of = jax.random.split(jax.random.key(seed), 16)
    return {
        "query_vectors": draw_query_vectors(jax.random.fold_in(key_of[15], 71), 0),
        "key_vectors": draw_key_vectors(jax.random.fold_in(key_of[15], 71), 0),
        "value_vectors": centred(key_of[2], (TOKENS, HEADS * HEAD_DIM), 1.0, 6.0, ((0, 256),)),
        "weight_head": centred(key_of[3], (HEADS * HEAD_DIM, PATCH), (6.0 / (HEADS * HEAD_DIM) ** 0.5), 0.5),
        "noisy_latent": centred(key_of[4], (F, ROWS, COLS, LAT), 1.0, 6.0, ((1, 32), (2, 8)), jnp.float32),
        "noise_level": jnp.clip(jax.random.uniform(key_of[5], (1,), jnp.float32, 0.5, 1.0), 0.5, 1.0),
        "latent_mean": centred(key_of[6], (LAT,), 0.5, 3.0, (), jnp.float32),
        "latent_scale": jnp.clip(jnp.exp(jax.random.uniform(key_of[7], (LAT,), jnp.float32, math.log(0.5), math.log(2.0))), 0.5, 2.0),
        "cache_in": centred(key_of[8], (2, ROWS, COLS, LAT), 1.0, 6.0, ((1, 32), (2, 8))),
        "weight_in": centred(key_of[9], (3, 3, 3, LAT, C1), (27 * LAT) ** -0.5, 0.3125),
        "bias_in": centred(key_of[10], (C1,), 0.5, 3.0, (), jnp.float32),
        "norm_gain": jnp.clip(1.0 + 0.1 * jax.random.normal(key_of[11], (C1,), jnp.float32), 0.5, 1.5),
        "cache_mid": centred(key_of[12], (2, ROWS, COLS, C1), 1.0, 6.0, ((1, 32), (2, 8))),
        "weight_mid": centred(key_of[13], (3, 3, 3, C1, C1), (27 * C1) ** -0.5, 0.0625),
        "bias_mid": centred(key_of[14], (C1,), 0.5, 3.0, (), jnp.float32),
    }


EPSILON = 1e-06

def head_attention(head_query, head_key, head_value):
    scaling = 1.0 / math.sqrt(HEAD_DIM)
    key_float = head_key.astype(jnp.float32)
    value_float = head_value.astype(jnp.float32)
    block_rows = math.gcd(TOKENS, 2048)
    query_blocks = head_query.astype(jnp.float32).reshape(TOKENS // block_rows, block_rows, HEAD_DIM)

    def one_block(query_block):
        scores = jnp.dot(query_block, key_float.T, precision=lax.Precision.HIGHEST) * scaling
        highest = lax.optimization_barrier(jnp.max(scores, axis=-1, keepdims=True))
        expd = jnp.exp(scores - highest)
        totals = lax.optimization_barrier(jnp.sum(expd, axis=-1, keepdims=True))
        rounded = lax.optimization_barrier(expd.astype(jnp.bfloat16)).astype(jnp.float32)
        mixed = jnp.dot(rounded, value_float, precision=lax.Precision.HIGHEST)
        return (mixed / totals).astype(jnp.bfloat16)
    return lax.map(one_block, query_blocks).reshape(TOKENS, HEAD_DIM)

def causal_conv(frames, cache, weight, bias_row):
    stacked = jnp.concatenate([cache, frames], axis=0)
    padded = jnp.pad(stacked, ((0, 0), (1, 1), (1, 1), (0, 0)))
    frame_count, row_count, col_count = (frames.shape[0], frames.shape[1], frames.shape[2])
    in_count = frames.shape[3]
    weight_float = weight.astype(jnp.float32)
    result = jnp.zeros((frame_count * row_count * col_count, weight.shape[-1]), jnp.float32)
    for shift_t in range(3):
        for shift_h in range(3):
            for shift_w in range(3):
                window = padded[shift_t:shift_t + frame_count, shift_h:shift_h + row_count, shift_w:shift_w + col_count]
                window = window.astype(jnp.float32).reshape(-1, in_count)
                result = result + jnp.dot(window, weight_float[shift_t, shift_h, shift_w], precision=lax.Precision.HIGHEST)
    return result.reshape(frame_count, row_count, col_count, -1) + bias_row

def reference(query_vectors, key_vectors, value_vectors, weight_head, noisy_latent, noise_level, latent_mean, latent_scale, cache_in, weight_in, bias_in, norm_gain, cache_mid, weight_mid, bias_mid):
    query_heads = query_vectors.reshape(TOKENS, HEADS, HEAD_DIM).transpose(1, 0, 2)
    key_heads = key_vectors.reshape(TOKENS, HEADS, HEAD_DIM).transpose(1, 0, 2)
    value_heads = value_vectors.reshape(TOKENS, HEADS, HEAD_DIM).transpose(1, 0, 2)

    def per_head(triple):
        return head_attention(triple[0], triple[1], triple[2])
    attended = lax.map(per_head, (query_heads, key_heads, value_heads))
    attended = attended.transpose(1, 0, 2).reshape(TOKENS, HEADS * HEAD_DIM)
    velocity = jnp.dot(attended, weight_head, preferred_element_type=jnp.float32)
    patch_grid = velocity.reshape(N_SEQ, F, TR, WP, 2, 2, LAT)
    patch_grid = patch_grid.transpose(1, 0, 2, 4, 3, 5, 6).reshape(F, ROWS, COLS, LAT)
    denoised = noisy_latent - noise_level[0] * patch_grid
    latent = (denoised * latent_scale + latent_mean).astype(jnp.bfloat16)
    first_conv = causal_conv(latent, cache_in, weight_in, bias_in)
    power = lax.optimization_barrier(jnp.mean(first_conv * first_conv, axis=-1, keepdims=True))
    active = jax.nn.silu(first_conv * lax.rsqrt(power + EPSILON) * norm_gain).astype(jnp.bfloat16)
    features = (first_conv + causal_conv(active, cache_mid, weight_mid, bias_mid)).astype(jnp.bfloat16)
    return (denoised, features)
```

```python
import functools
import math

import jax
import jax.numpy as jnp
from jax import lax
from jax.experimental import pallas as pl
from jax.experimental.pallas import tpu as pltpu
from jax.sharding import Mesh
from jax.sharding import PartitionSpec as P

HEAD_DIM = 128
LAT = 16
C1 = 384
F = 4
EPSILON = 1e-06

SEQ = ("y", "zh", "core")
BLK = ("zl", "x")
HEAD = ("y", "zh", "zl")
SHARD = SEQ + BLK

TILE = 512
SUB = 256
CHUNK = 768
NT = (((1,), (1,)), ((), ()))


def lane_max(s):
    t = s[:, :128]
    for j in range(1, s.shape[1] // 128):
        t = jnp.maximum(t, s[:, j * 128 : (j + 1) * 128])
    return jnp.max(t, axis=1, keepdims=True)


def flash_kernel(first, last, n_kv, half, *refs):
    qo_ref, qx_ref = refs[:2]
    kv_refs = refs[2 : 2 + n_kv]
    refs = refs[2 + n_kv :]
    if not first:
        st_ref, refs = refs[0], refs[1:]
    if last:
        w_ref, own_ref, oth_ref = refs
    else:
        (so_ref,) = refs
    i = pl.program_id(0)
    scale = math.log2(math.e) / math.sqrt(HEAD_DIM)
    qf = jnp.where(i < half, qo_ref[...], qx_ref[...]).astype(jnp.float32) * scale
    q_hi = qf.astype(jnp.bfloat16)
    q_lo = (qf - q_hi.astype(jnp.float32)).astype(jnp.bfloat16)
    q = jnp.concatenate([q_hi, q_lo], axis=1)
    subs = TILE // SUB
    tops, accs = [], []
    for r in range(subs):
        if first:
            tops.append(jnp.full((SUB, 128), -1e30, jnp.float32))
            accs.append(jnp.zeros((SUB, 256), jnp.float32))
        else:
            st = st_ref[pl.ds(r * SUB, SUB), :]
            acc_l = st[:, 128:]
            lane = lax.broadcasted_iota(jnp.int32, (SUB, 128), 1)
            total = jnp.max(jnp.where(lane < 64, acc_l, -1e30), axis=1, keepdims=True)
            top = jnp.max(jnp.where(lane < 64, -1e30, acc_l), axis=1, keepdims=True)
            tops.append(jnp.broadcast_to(top, (SUB, 128)))
            accs.append(
                jnp.concatenate([st[:, :128], jnp.broadcast_to(total, (SUB, 128))], axis=1)
            )
    items = [
        (r, b, c)
        for b in range(n_kv)
        for c in range(kv_refs[b].shape[0] // CHUNK)
        for r in range(subs)
    ]
    ones = jnp.ones((CHUNK, 128), jnp.bfloat16)

    def score(item):
        r, b, c = item
        k = kv_refs[b][pl.ds(c * CHUNK, CHUNK), :128]
        return lax.dot_general(
            q[r * SUB : (r + 1) * SUB],
            jnp.concatenate([k, k], axis=1),
            NT,
            preferred_element_type=jnp.float32,
        )

    s = score(items[0])
    for n, (r, b, c) in enumerate(items):
        following = score(items[n + 1]) if n + 1 < len(items) else None
        top = jnp.maximum(tops[r], lane_max(s))
        p = jnp.exp2(s - top[:, :1]).astype(jnp.bfloat16)
        fade = jnp.exp2(tops[r] - top)
        v = jnp.concatenate([kv_refs[b][pl.ds(c * CHUNK, CHUNK), 128:], ones], axis=1)
        accs[r] = accs[r] * jnp.concatenate([fade, fade], axis=1) + jnp.dot(
            p, v, preferred_element_type=jnp.float32
        )
        tops[r] = top
        s = following
    lane = lax.broadcasted_iota(jnp.int32, (SUB, 128), 1)
    outs = []
    for r in range(subs):
        if last:
            total = accs[r][:, 128:]
            mixed = (accs[r][:, :128] / total).astype(jnp.bfloat16)
            u = jnp.dot(mixed, w_ref[...], preferred_element_type=jnp.float32)
            outs.append(jnp.where(lane < 64, u, tops[r] + jnp.log2(total)))
        else:
            so_ref[pl.ds(r * SUB, SUB), :] = jnp.concatenate(
                [accs[r][:, :128], jnp.where(lane < 64, accs[r][:, 128:], tops[r])], axis=1
            )
    if last:

        @pl.when(i < half)
        def _():
            for r in range(subs):
                own_ref[pl.ds(r * SUB, SUB), :] = outs[r]

        @pl.when(i >= half)
        def _():
            for r in range(subs):
                oth_ref[pl.ds(r * SUB, SUB), :] = outs[r]


def flash(q_own, q_oth, kvs, state=None, weight=None):
    first, last = state is None, weight is not None
    rows = q_own.shape[0]
    half = rows // TILE
    keys = sum(kv.shape[0] for kv in kvs)

    def lower(i):
        return (jnp.minimum(i, half - 1), 0)

    def upper(i):
        return (jnp.maximum(i - half, 0), 0)

    in_specs = [pl.BlockSpec((TILE, 128), lower), pl.BlockSpec((TILE, 128), upper)]
    in_specs += [pl.BlockSpec(kv.shape, lambda i: (0, 0)) for kv in kvs]
    args = [q_own, q_oth, *kvs]
    if not first:
        in_specs.append(pl.BlockSpec((TILE, 256), lambda i: (i, 0)))
        args.append(state)
    if last:
        in_specs.append(pl.BlockSpec(weight.shape, lambda i: (0, 0)))
        args.append(weight)
        out_specs = [pl.BlockSpec((TILE, 128), lower), pl.BlockSpec((TILE, 128), upper)]
        out_shape = [jax.ShapeDtypeStruct((rows, 128), jnp.float32)] * 2
    else:
        out_specs = pl.BlockSpec((TILE, 256), lambda i: (i, 0))
        out_shape = jax.ShapeDtypeStruct((2 * rows, 256), jnp.float32)
    return pl.pallas_call(
        functools.partial(flash_kernel, first, last, len(kvs), half),
        grid=(2 * half,),
        in_specs=in_specs,
        out_specs=out_specs,
        out_shape=out_shape,
        compiler_params=pltpu.CompilerParams(vmem_limit_bytes=40 << 20),
        cost_estimate=pl.CostEstimate(
            flops=2 * rows * keys * 512 * 2,
            bytes_accessed=rows * 4096,
            transcendentals=2 * rows * keys,
        ),
    )(*args)


def conv_kernel(x_ref, w_ref, base_ref, out_ref, acc_ref):
    step = pl.program_id(0)
    t, u = step // 3, step % 3

    @pl.when(step == 0)
    def _():
        acc_ref[...] = base_ref[...]

    total = acc_ref[...]
    for v in range(3):
        rows = x_ref[v, pl.ds(t, 4), pl.ds(u, 4)].reshape(256, C1)
        total = total + jnp.dot(
            rows, w_ref[0, pl.ds(v * C1, C1), :], preferred_element_type=jnp.float32
        )
    acc_ref[...] = total

    @pl.when(step == 8)
    def _():
        out_ref[...] = total.astype(jnp.bfloat16)


def conv_mid(shifted, weight, base):
    return pl.pallas_call(
        conv_kernel,
        grid=(9,),
        in_specs=[
            pl.BlockSpec(shifted.shape, lambda i: (0, 0, 0, 0, 0)),
            pl.BlockSpec((1, 3 * C1, C1), lambda i: (i, 0, 0)),
            pl.BlockSpec((256, C1), lambda i: (0, 0)),
        ],
        out_specs=pl.BlockSpec((256, C1), lambda i: (0, 0)),
        out_shape=jax.ShapeDtypeStruct((256, C1), jnp.bfloat16),
        scratch_shapes=[pltpu.VMEM((256, C1), jnp.float32)],
        compiler_params=pltpu.CompilerParams(vmem_limit_bytes=32 << 20),
        cost_estimate=pl.CostEstimate(
            flops=2 * 256 * 27 * C1 * C1, bytes_accessed=10 << 20, transcendentals=0
        ),
    )(shifted, weight.reshape(9, 3 * C1, C1), base)


def along(axis, step):
    count = lax.axis_size(axis)
    return [(i, i + step) for i in range(count) if 0 <= i + step < count]


def with_halo(cells, sides, width):
    for axis, dim in sides:
        head = lax.slice_in_dim(cells, 0, width, axis=dim)
        tail = lax.slice_in_dim(cells, cells.shape[dim] - width, cells.shape[dim], axis=dim)
        cells = jnp.concatenate(
            [
                lax.ppermute(tail, axis, along(axis, 1)),
                cells,
                lax.ppermute(head, axis, along(axis, -1)),
            ],
            axis=dim,
        )
    return cells


def attention(query_vectors, key_vectors, value_vectors, weight_head):
    tokens = query_vectors.shape[0]
    heads = lax.axis_size(HEAD)
    packed = jnp.concatenate(
        [
            a.reshape(tokens, heads, HEAD_DIM)
            for a in (query_vectors, key_vectors, value_vectors)
        ],
        axis=2,
    ).transpose(1, 0, 2)
    moved = lax.all_to_all(packed, HEAD, split_axis=0, concat_axis=0, tiled=True)
    moved = moved.reshape(heads * tokens, 3 * HEAD_DIM)
    q_own, kv = moved[:, :128], moved[:, 128:]
    swap = [(0, 1), (1, 0)]
    right = [(i, (i + 1) % 4) for i in range(4)]
    left = [((i + 1) % 4, i) for i in range(4)]
    q_oth = lax.ppermute(q_own, "core", swap)
    mid = kv.shape[0] // 2
    a, b = kv[:mid], kv[mid:]
    left_a = lax.ppermute(a, "x", right)
    right_b = lax.ppermute(b, "x", left)
    state = flash(q_own, q_oth, [kv])
    left_b = lax.ppermute(b, "x", right)
    right_a = lax.ppermute(a, "x", left)
    state = flash(q_own, q_oth, [left_a, right_b], state)
    far_a = lax.ppermute(left_a, "x", right)
    far_b = lax.ppermute(right_b, "x", left)
    state = flash(q_own, q_oth, [left_b, right_a], state)
    head = lax.axis_index(HEAD)
    weight = lax.dynamic_slice_in_dim(weight_head, head * HEAD_DIM, HEAD_DIM, axis=0)
    weight = jnp.pad(weight, ((0, 0), (0, 64)))
    own, oth = flash(q_own, q_oth, [far_a, far_b], state, weight)
    oth = lax.ppermute(oth, "core", swap)
    share = 1.0 / (1.0 + jnp.exp2(oth[:, 64:] - own[:, 64:]))
    partial = own[:, :64] * share + oth[:, :64] * (1.0 - share)
    partial = partial.astype(jnp.bfloat16).reshape(heads, tokens, 64)
    parts = lax.all_to_all(partial, HEAD, split_axis=0, concat_axis=0, tiled=True)
    return jnp.sum(parts.astype(jnp.float32), axis=0)


def shards(
    query_vectors,
    key_vectors,
    value_vectors,
    weight_head,
    noisy_latent,
    noise_level,
    latent_mean,
    latent_scale,
    cache_in,
    weight_in,
    bias_in,
    norm_gain,
    cache_mid,
    weight_mid,
    bias_mid,
):
    sides = ((SEQ, 1), (BLK, 2))
    noisy = with_halo(noisy_latent, sides, 2)
    cache_first = with_halo(cache_in, sides, 2)
    cache_second = with_halo(cache_mid, sides, 1)

    velocity = attention(query_vectors, key_vectors, value_vectors, weight_head)

    tiles = lax.axis_size(BLK)
    cols = velocity.shape[0] // tiles
    wide = jnp.pad(velocity, ((1, 1), (0, 0)))
    pieces = jnp.stack([wide[k * cols : k * cols + cols + 2] for k in range(tiles)])
    patch = lax.all_to_all(pieces, BLK, split_axis=0, concat_axis=0, tiled=True)
    patch = patch.reshape(F, 2, cols + 2, 64)
    patch = jnp.concatenate(
        [
            lax.ppermute(patch[:, 1:], SEQ, along(SEQ, 1)),
            patch,
            lax.ppermute(patch[:, :1], SEQ, along(SEQ, -1)),
        ],
        axis=1,
    )
    grid = patch.reshape(F, 4, cols + 2, 2, 2, LAT).transpose(0, 1, 3, 2, 4, 5)
    grid = grid.reshape(F, 8, 2 * cols + 4, LAT)
    rows, width = noisy_latent.shape[1], noisy_latent.shape[2]
    denoised = noisy - noise_level[0] * grid
    row_at = lax.axis_index(SEQ) * rows - 2 + jnp.arange(rows + 4)
    col_at = lax.axis_index(BLK) * width - 2 + jnp.arange(width + 4)
    row_ok = (row_at >= 0) & (row_at < lax.axis_size(SEQ) * rows)
    col_ok = (col_at >= 0) & (col_at < tiles * width)
    inside = row_ok[:, None, None] & col_ok[None, :, None]
    latent = jnp.where(inside, denoised * latent_scale + latent_mean, 0.0).astype(jnp.bfloat16)

    stacked = jnp.concatenate([cache_first, latent], axis=0)
    taps = [
        stacked[t : t + F, u : u + rows + 2, v : v + width + 2]
        for t in range(3)
        for u in range(3)
        for v in range(3)
    ]
    gathered = jnp.concatenate(taps, axis=-1).reshape(F * (rows + 2) * (width + 2), -1)
    first = jnp.dot(
        gathered, weight_in.reshape(-1, C1), preferred_element_type=jnp.float32
    )
    first = (first + bias_in).reshape(F, rows + 2, width + 2, C1)
    power = jnp.mean(first * first, axis=-1, keepdims=True)
    active = jax.nn.silu(first * lax.rsqrt(power + EPSILON) * norm_gain)
    active = jnp.where(inside[1:-1, 1:-1], active, 0.0).astype(jnp.bfloat16)
    padded = jnp.concatenate([cache_second, active], axis=0)
    padded = jnp.pad(padded, ((0, 0), (0, 0), (0, 4), (0, 0)))
    shifted = jnp.stack([padded[:, :, v : v + 16] for v in range(3)])
    base = first[:, 1:-1, 1:-1] + bias_mid
    base = jnp.pad(base, ((0, 0), (0, 0), (0, 4), (0, 0))).reshape(256, C1)
    features = conv_mid(shifted, weight_mid, base)
    features = features.reshape(F, rows, 16, C1)[:, :, :width]
    return (denoised[:, 2:-2, 2:-2], features)


def solution(mesh):
    inner = Mesh(mesh.devices.reshape(4, 4, 2, 2, 4), SHARD)
    tokens, tile = P(SHARD, None), P(None, SEQ, BLK, None)
    in_specs = (
        tokens,
        tokens,
        tokens,
        P(),
        tile,
        P(),
        P(),
        P(),
        tile,
        P(),
        P(),
        P(),
        tile,
        P(),
        P(),
    )
    return jax.shard_map(
        shards, mesh=inner, in_specs=in_specs, out_specs=(tile, tile), check_vma=False
    )
```

```python
import functools
import math

import jax
import jax.numpy as jnp
from jax import lax
from jax.experimental import pallas as pl
from jax.experimental.pallas import tpu as pltpu
from jax.sharding import Mesh
from jax.sharding import PartitionSpec as P

HEAD_DIM = 128
LAT = 16
C1 = 384
F = 4
EPSILON = 1e-06

SEQ = ("y", "zh", "core")
BLK = ("zl", "x")
HEAD = ("y", "zl", "x")
SHARD = SEQ + BLK

TILE = 512
SUB = 256
CHUNK = 768
NT = (((1,), (1,)), ((), ()))


def lane_max(s):
    t = s[:, :128]
    for j in range(1, s.shape[1] // 128):
        t = jnp.maximum(t, s[:, j * 128 : (j + 1) * 128])
    return jnp.max(t, axis=1, keepdims=True)


def flash_kernel(first, last, n_kv, half, *refs):
    qo_ref, qx_ref = refs[:2]
    kv_refs = refs[2 : 2 + n_kv]
    refs = refs[2 + n_kv :]
    if not first:
        st_ref, refs = refs[0], refs[1:]
    if last:
        w_ref, own_ref, oth_ref = refs
    else:
        (so_ref,) = refs
    i = pl.program_id(0)
    scale = math.log2(math.e) / math.sqrt(HEAD_DIM)
    qf = jnp.where(i < half, qo_ref[...], qx_ref[...]).astype(jnp.float32) * scale
    q_hi = qf.astype(jnp.bfloat16)
    q_lo = (qf - q_hi.astype(jnp.float32)).astype(jnp.bfloat16)
    q = jnp.concatenate([q_hi, q_lo], axis=1)
    subs = TILE // SUB
    tops, accs = [], []
    for r in range(subs):
        if first:
            tops.append(jnp.full((SUB, 128), -1e30, jnp.float32))
            accs.append(jnp.zeros((SUB, 256), jnp.float32))
        else:
            st = st_ref[pl.ds(r * SUB, SUB), :]
            acc_l = st[:, 128:]
            lane = lax.broadcasted_iota(jnp.int32, (SUB, 128), 1)
            total = jnp.max(jnp.where(lane < 64, acc_l, -1e30), axis=1, keepdims=True)
            top = jnp.max(jnp.where(lane < 64, -1e30, acc_l), axis=1, keepdims=True)
            tops.append(jnp.broadcast_to(top, (SUB, 128)))
            accs.append(
                jnp.concatenate([st[:, :128], jnp.broadcast_to(total, (SUB, 128))], axis=1)
            )
    items = [
        (r, b, c)
        for b in range(n_kv)
        for c in range(kv_refs[b].shape[0] // CHUNK)
        for r in range(subs)
    ]
    ones = jnp.ones((CHUNK, 128), jnp.bfloat16)

    def score(item):
        r, b, c = item
        k = kv_refs[b][pl.ds(c * CHUNK, CHUNK), :128]
        return lax.dot_general(
            q[r * SUB : (r + 1) * SUB],
            jnp.concatenate([k, k], axis=1),
            NT,
            preferred_element_type=jnp.float32,
        )

    s = score(items[0])
    for n, (r, b, c) in enumerate(items):
        following = score(items[n + 1]) if n + 1 < len(items) else None
        top = jnp.maximum(tops[r], lane_max(s))
        p = jnp.exp2(s - top[:, :1]).astype(jnp.bfloat16)
        fade = jnp.exp2(tops[r] - top)
        v = jnp.concatenate([kv_refs[b][pl.ds(c * CHUNK, CHUNK), 128:], ones], axis=1)
        accs[r] = accs[r] * jnp.concatenate([fade, fade], axis=1) + jnp.dot(
            p, v, preferred_element_type=jnp.float32
        )
        tops[r] = top
        s = following
    lane = lax.broadcasted_iota(jnp.int32, (SUB, 128), 1)
    outs = []
    for r in range(subs):
        if last:
            total = accs[r][:, 128:]
            mixed = (accs[r][:, :128] / total).astype(jnp.bfloat16)
            u = jnp.dot(mixed, w_ref[...], preferred_element_type=jnp.float32)
            outs.append(jnp.where(lane < 64, u, tops[r] + jnp.log2(total)))
        else:
            so_ref[pl.ds(r * SUB, SUB), :] = jnp.concatenate(
                [accs[r][:, :128], jnp.where(lane < 64, accs[r][:, 128:], tops[r])], axis=1
            )
    if last:

        @pl.when(i < half)
        def _():
            for r in range(subs):
                own_ref[pl.ds(r * SUB, SUB), :] = outs[r]

        @pl.when(i >= half)
        def _():
            for r in range(subs):
                oth_ref[pl.ds(r * SUB, SUB), :] = outs[r]


def flash(q_own, q_oth, kvs, state=None, weight=None):
    first, last = state is None, weight is not None
    rows = q_own.shape[0]
    half = rows // TILE
    keys = sum(kv.shape[0] for kv in kvs)

    def lower(i):
        return (jnp.minimum(i, half - 1), 0)

    def upper(i):
        return (jnp.maximum(i - half, 0), 0)

    in_specs = [
        pl.BlockSpec((TILE, 128), lambda i: (jnp.minimum(i, half - 1), 2)),
        pl.BlockSpec((TILE, 128), upper),
    ]
    in_specs += [pl.BlockSpec((kv.shape[0], 256), lambda i: (0, 0)) for kv in kvs]
    args = [q_own, q_oth, *kvs]
    if not first:
        in_specs.append(pl.BlockSpec((TILE, 256), lambda i: (i, 0)))
        args.append(state)
    if last:
        in_specs.append(pl.BlockSpec(weight.shape, lambda i: (0, 0)))
        args.append(weight)
        out_specs = [pl.BlockSpec((TILE, 128), lower), pl.BlockSpec((TILE, 128), upper)]
        out_shape = [jax.ShapeDtypeStruct((rows, 128), jnp.float32)] * 2
    else:
        out_specs = pl.BlockSpec((TILE, 256), lambda i: (i, 0))
        out_shape = jax.ShapeDtypeStruct((2 * rows, 256), jnp.float32)
    return pl.pallas_call(
        functools.partial(flash_kernel, first, last, len(kvs), half),
        grid=(2 * half,),
        in_specs=in_specs,
        out_specs=out_specs,
        out_shape=out_shape,
        compiler_params=pltpu.CompilerParams(vmem_limit_bytes=40 << 20),
        cost_estimate=pl.CostEstimate(
            flops=2 * rows * keys * 512 * 2,
            bytes_accessed=rows * 4096,
            transcendentals=2 * rows * keys,
        ),
    )(*args)


def conv_kernel(x_ref, w_ref, base_ref, out_ref, acc_ref):
    step = pl.program_id(0)
    t, u = step // 3, step % 3

    @pl.when(step == 0)
    def _():
        acc_ref[...] = base_ref[...]

    total = acc_ref[...]
    for v in range(3):
        rows = x_ref[v, pl.ds(t, 4), pl.ds(u, 4)].reshape(256, C1)
        total = total + jnp.dot(
            rows, w_ref[0, pl.ds(v * C1, C1), :], preferred_element_type=jnp.float32
        )
    acc_ref[...] = total

    @pl.when(step == 8)
    def _():
        out_ref[...] = total.astype(jnp.bfloat16)


def conv_mid(shifted, weight, base):
    return pl.pallas_call(
        conv_kernel,
        grid=(9,),
        in_specs=[
            pl.BlockSpec(shifted.shape, lambda i: (0, 0, 0, 0, 0)),
            pl.BlockSpec((1, 3 * C1, C1), lambda i: (i, 0, 0)),
            pl.BlockSpec((256, C1), lambda i: (0, 0)),
        ],
        out_specs=pl.BlockSpec((256, C1), lambda i: (0, 0)),
        out_shape=jax.ShapeDtypeStruct((256, C1), jnp.bfloat16),
        scratch_shapes=[pltpu.VMEM((256, C1), jnp.float32)],
        compiler_params=pltpu.CompilerParams(vmem_limit_bytes=32 << 20),
        cost_estimate=pl.CostEstimate(
            flops=2 * 256 * 27 * C1 * C1, bytes_accessed=10 << 20, transcendentals=0
        ),
    )(shifted, weight.reshape(9, 3 * C1, C1), base)


def along(axis, step):
    count = lax.axis_size(axis)
    return [(i, i + step) for i in range(count) if 0 <= i + step < count]


def swap_edges(parts, axis, dims, widths):
    def cut(tail):
        flat = []
        for part, dim, width in zip(parts, dims, widths):
            size = part.shape[dim]
            start = size - width if tail else 0
            flat.append(lax.slice_in_dim(part, start, start + width, axis=dim).reshape(-1))
        return jnp.concatenate(flat).reshape(-1, 128)

    before = lax.ppermute(cut(True), axis, along(axis, 1)).reshape(-1)
    after = lax.ppermute(cut(False), axis, along(axis, -1)).reshape(-1)
    wider, at = [], 0
    for part, dim, width in zip(parts, dims, widths):
        shape = list(part.shape)
        shape[dim] = width
        size = math.prod(shape)
        wider.append(
            jnp.concatenate(
                [
                    before[at : at + size].reshape(shape),
                    part,
                    after[at : at + size].reshape(shape),
                ],
                axis=dim,
            )
        )
        at += size
    return wider


def input_halos(noisy, cache_in, cache_mid):
    both = jnp.concatenate([cache_in.astype(jnp.float32), noisy], axis=0)
    parts = [both, cache_mid.astype(jnp.float32)]
    parts = swap_edges(parts, SEQ, (1, 1), (2, 1))
    both, cache_mid = swap_edges(parts, BLK, (2, 2), (2, 1))
    return both[2:], both[:2].astype(jnp.bfloat16), cache_mid.astype(jnp.bfloat16)


def pack_kernel(q_ref, k_ref, v_ref, out_ref):
    for h in range(out_ref.shape[0]):
        lanes = pl.ds(h * HEAD_DIM, HEAD_DIM)
        out_ref[h, :, 0:128] = k_ref[:, lanes]
        out_ref[h, :, 128:256] = v_ref[:, lanes]
        out_ref[h, :, 256:384] = q_ref[:, lanes]


def pack(query_vectors, key_vectors, value_vectors):
    tokens, width = query_vectors.shape
    heads = width // HEAD_DIM
    block = pl.BlockSpec((tokens, width // 4), lambda i: (0, i))
    return pl.pallas_call(
        pack_kernel,
        grid=(4,),
        in_specs=[block] * 3,
        out_specs=pl.BlockSpec((heads // 4, tokens, 3 * HEAD_DIM), lambda i: (i, 0, 0)),
        out_shape=jax.ShapeDtypeStruct((heads, tokens, 3 * HEAD_DIM), jnp.bfloat16),
    )(query_vectors, key_vectors, value_vectors)


def merge_kernel(own_ref, oth_ref, out_ref, vel_ref, piece_ref):
    own, oth = own_ref[...], oth_ref[...]
    gap = pltpu.roll(oth - own, 64, axis=1)
    share = 1.0 / (1.0 + jnp.exp2(gap))
    vel = own * share + oth * (1.0 - share)
    lane = lax.broadcasted_iota(jnp.int32, vel.shape, 1)
    vel_ref[...] = jnp.where(lane < 64, vel, pltpu.roll(vel, 64, axis=1))
    low = lax.broadcasted_iota(jnp.int32, (16, 128), 1) < 64
    zero = jnp.zeros((16, 128), jnp.float32)

    def column(r, at):
        if at < 0 or at >= 48:
            return zero
        return vel_ref[pl.ds(r * 48 + at, 16, stride=96), :]

    for b in range(8):
        for r in range(2):
            for c in range(4):
                at = 6 * b - 1 + c
                both = jnp.where(low, column(r, at), column(r, at + 4))
                for y in range(4):
                    piece_ref[y, b, pl.ds(r * 16 + c * 4, 4), :] = both[y * 4 : y * 4 + 4]
    out_ref[...] = piece_ref[...].astype(jnp.bfloat16)


def merge(own, oth):
    rows = own.shape[0]
    whole = pl.BlockSpec((rows, 128), lambda: (0, 0))
    shape = (4, 8, 32, 128)
    return pl.pallas_call(
        merge_kernel,
        in_specs=[whole, whole],
        out_specs=pl.BlockSpec(shape, lambda: (0, 0, 0, 0)),
        out_shape=jax.ShapeDtypeStruct(shape, jnp.bfloat16),
        scratch_shapes=[
            pltpu.VMEM((rows, 128), jnp.float32),
            pltpu.VMEM(shape, jnp.float32),
        ],
        compiler_params=pltpu.CompilerParams(vmem_limit_bytes=24 << 20),
    )(own, oth)


def attention(query_vectors, key_vectors, value_vectors, weight_head, work):
    packed = pack(query_vectors, key_vectors, value_vectors)
    heads, tokens = packed.shape[:2]
    moved = lax.all_to_all(packed, HEAD, split_axis=0, concat_axis=0, tiled=True)
    moved = moved.reshape(heads * tokens, 3 * HEAD_DIM)
    swap = [(0, 1), (1, 0)]
    right = [(i, (i + 1) % 4) for i in range(4)]
    left = [((i + 1) % 4, i) for i in range(4)]
    mid = moved.shape[0] // 2
    a, b = moved[:mid, :256], moved[mid:, :256]
    left_a = lax.ppermute(a, "zh", right)
    right_b = lax.ppermute(b, "zh", left)
    q_oth = lax.ppermute(moved[:, 256:], "core", swap)
    state = flash(moved, q_oth, [moved])
    left_b = lax.ppermute(b, "zh", right)
    right_a = lax.ppermute(a, "zh", left)
    state = flash(moved, q_oth, [left_a, right_b], state)
    far_a = lax.ppermute(left_a, "zh", right)
    far_b = lax.ppermute(right_b, "zh", left)
    state = flash(moved, q_oth, [left_b, right_a], state)
    state, work = lax.optimization_barrier((state, work))
    head = lax.axis_index(HEAD)
    weight = lax.dynamic_slice_in_dim(weight_head, head * HEAD_DIM, HEAD_DIM, axis=0)
    weight = jnp.pad(weight, ((0, 0), (0, 64)))
    own, oth = flash(moved, q_oth, [far_a, far_b], state, weight)
    oth = lax.ppermute(oth, "core", swap)
    partial = merge(own, oth).reshape(heads, 32, 128)
    parts = lax.all_to_all(partial, HEAD, split_axis=0, concat_axis=0, tiled=True)
    return jnp.sum(parts.astype(jnp.float32), axis=0), work


def shards(
    query_vectors,
    key_vectors,
    value_vectors,
    weight_head,
    noisy_latent,
    noise_level,
    latent_mean,
    latent_scale,
    cache_in,
    weight_in,
    bias_in,
    norm_gain,
    cache_mid,
    weight_mid,
    bias_mid,
):
    work = input_halos(noisy_latent, cache_in, cache_mid)
    mine, work = attention(query_vectors, key_vectors, value_vectors, weight_head, work)
    noisy, cache_first, cache_second = work

    above = lax.ppermute(mine[16:], SEQ, along(SEQ, 1))
    below = lax.ppermute(mine[:16], SEQ, along(SEQ, -1))
    patch = jnp.concatenate([above, mine, below], axis=0)
    patch = patch.reshape(4, 4, F, 2, 64)
    patch = patch.transpose(2, 0, 3, 1, 4).reshape(F, 4, 8, 64)
    tiles, cols = lax.axis_size(BLK), 6
    grid = patch.reshape(F, 4, cols + 2, 2, 2, LAT).transpose(0, 1, 3, 2, 4, 5)
    grid = grid.reshape(F, 8, 2 * cols + 4, LAT)
    rows, width = noisy_latent.shape[1], noisy_latent.shape[2]
    denoised = noisy - noise_level[0] * grid
    row_at = lax.axis_index(SEQ) * rows - 2 + jnp.arange(rows + 4)
    col_at = lax.axis_index(BLK) * width - 2 + jnp.arange(width + 4)
    row_ok = (row_at >= 0) & (row_at < lax.axis_size(SEQ) * rows)
    col_ok = (col_at >= 0) & (col_at < tiles * width)
    inside = row_ok[:, None, None] & col_ok[None, :, None]
    latent = jnp.where(inside, denoised * latent_scale + latent_mean, 0.0).astype(jnp.bfloat16)

    stacked = jnp.concatenate([cache_first, latent], axis=0)
    taps = [
        stacked[t : t + F, u : u + rows + 2, v : v + width + 2]
        for t in range(3)
        for u in range(3)
        for v in range(3)
    ]
    gathered = jnp.concatenate(taps, axis=-1).reshape(F * (rows + 2) * (width + 2), -1)
    first = jnp.dot(
        gathered, weight_in.reshape(-1, C1), preferred_element_type=jnp.float32
    )
    first = (first + bias_in).reshape(F, rows + 2, width + 2, C1)
    power = jnp.mean(first * first, axis=-1, keepdims=True)
    active = jax.nn.silu(first * lax.rsqrt(power + EPSILON) * norm_gain)
    active = jnp.where(inside[1:-1, 1:-1], active, 0.0).astype(jnp.bfloat16)
    padded = jnp.concatenate([cache_second, active], axis=0)
    padded = jnp.pad(padded, ((0, 0), (0, 0), (0, 4), (0, 0)))
    shifted = jnp.stack([padded[:, :, v : v + 16] for v in range(3)])
    base = first[:, 1:-1, 1:-1] + bias_mid
    base = jnp.pad(base, ((0, 0), (0, 0), (0, 4), (0, 0))).reshape(256, C1)
    features = conv_mid(shifted, weight_mid, base)
    features = features.reshape(F, rows, 16, C1)[:, :, :width]
    return (denoised[:, 2:-2, 2:-2], features)


def solution(mesh):
    inner = Mesh(mesh.devices.reshape(4, 4, 2, 2, 4), SHARD)
    tokens, tile = P(SHARD, None), P(None, SEQ, BLK, None)
    in_specs = (
        tokens,
        tokens,
        tokens,
        P(),
        tile,
        P(),
        P(),
        P(),
        tile,
        P(),
        P(),
        P(),
        tile,
        P(),
        P(),
    )
    return jax.shard_map(
        shards, mesh=inner, in_specs=in_specs, out_specs=(tile, tile), check_vma=False
    )
```

```python
import functools
import math

import jax
import jax.numpy as jnp
from jax import lax
from jax.experimental import pallas as pl
from jax.experimental.pallas import tpu as pltpu
from jax.sharding import Mesh
from jax.sharding import PartitionSpec as P

HEAD_DIM = 128
LAT = 16
C1 = 384
F = 4
EPSILON = 1e-06

SEQ = ("y", "zh", "core")
BLK = ("zl", "x")
HEAD = ("zh", "zl", "x")
SHARD = SEQ + BLK

TILE = 512
SUB = 256
CHUNK = 768
NT = (((1,), (1,)), ((), ()))


def lane_max(s):
    t = s[:, :128]
    for j in range(1, s.shape[1] // 128):
        t = jnp.maximum(t, s[:, j * 128 : (j + 1) * 128])
    return jnp.max(t, axis=1, keepdims=True)


def flash_kernel(first, last, n_kv, half, *refs):
    qo_ref, qx_ref = refs[:2]
    kv_refs = refs[2 : 2 + n_kv]
    refs = refs[2 + n_kv :]
    if not first:
        st_ref, refs = refs[0], refs[1:]
    if last:
        w_ref, own_ref, oth_ref = refs
    else:
        (so_ref,) = refs
    i = pl.program_id(0)
    scale = math.log2(math.e) / math.sqrt(HEAD_DIM)
    qf = jnp.where(i < half, qo_ref[...], qx_ref[...]).astype(jnp.float32) * scale
    q_hi = qf.astype(jnp.bfloat16)
    q_lo = (qf - q_hi.astype(jnp.float32)).astype(jnp.bfloat16)
    q = jnp.concatenate([q_hi, q_lo], axis=1)
    subs = TILE // SUB
    tops, accs = [], []
    for r in range(subs):
        if first:
            tops.append(jnp.full((SUB, 128), -1e30, jnp.float32))
            accs.append(jnp.zeros((SUB, 256), jnp.float32))
        else:
            st = st_ref[pl.ds(r * SUB, SUB), :]
            acc_l = st[:, 128:]
            lane = lax.broadcasted_iota(jnp.int32, (SUB, 128), 1)
            total = jnp.max(jnp.where(lane < 64, acc_l, -1e30), axis=1, keepdims=True)
            top = jnp.max(jnp.where(lane < 64, -1e30, acc_l), axis=1, keepdims=True)
            tops.append(jnp.broadcast_to(top, (SUB, 128)))
            accs.append(
                jnp.concatenate([st[:, :128], jnp.broadcast_to(total, (SUB, 128))], axis=1)
            )
    items = [
        (r, b, c)
        for b in range(n_kv)
        for c in range(kv_refs[b].shape[0] // CHUNK)
        for r in range(subs)
    ]
    ones = jnp.ones((CHUNK, 128), jnp.bfloat16)

    def score(item):
        r, b, c = item
        k = kv_refs[b][pl.ds(c * CHUNK, CHUNK), :128]
        return lax.dot_general(
            q[r * SUB : (r + 1) * SUB],
            jnp.concatenate([k, k], axis=1),
            NT,
            preferred_element_type=jnp.float32,
        )

    s = score(items[0])
    for n, (r, b, c) in enumerate(items):
        following = score(items[n + 1]) if n + 1 < len(items) else None
        top = jnp.maximum(tops[r], lane_max(s))
        p = jnp.exp2(s - top[:, :1]).astype(jnp.bfloat16)
        fade = jnp.exp2(tops[r] - top)
        v = jnp.concatenate([kv_refs[b][pl.ds(c * CHUNK, CHUNK), 128:], ones], axis=1)
        accs[r] = accs[r] * jnp.concatenate([fade, fade], axis=1) + jnp.dot(
            p, v, preferred_element_type=jnp.float32
        )
        tops[r] = top
        s = following
    lane = lax.broadcasted_iota(jnp.int32, (SUB, 128), 1)
    outs = []
    for r in range(subs):
        if last:
            total = accs[r][:, 128:]
            mixed = (accs[r][:, :128] / total).astype(jnp.bfloat16)
            u = jnp.dot(mixed, w_ref[...], preferred_element_type=jnp.float32)
            outs.append(jnp.where(lane < 64, u, tops[r] + jnp.log2(total)))
        else:
            so_ref[pl.ds(r * SUB, SUB), :] = jnp.concatenate(
                [accs[r][:, :128], jnp.where(lane < 64, accs[r][:, 128:], tops[r])], axis=1
            )
    if last:

        @pl.when(i < half)
        def _():
            for r in range(subs):
                own_ref[pl.ds(r * SUB, SUB), :] = outs[r]

        @pl.when(i >= half)
        def _():
            for r in range(subs):
                oth_ref[pl.ds(r * SUB, SUB), :] = outs[r]


def flash(q_own, q_oth, kvs, state=None, weight=None):
    first, last = state is None, weight is not None
    rows = q_own.shape[0]
    half = rows // TILE
    keys = sum(kv.shape[0] for kv in kvs)

    def lower(i):
        return (jnp.minimum(i, half - 1), 0)

    def upper(i):
        return (jnp.maximum(i - half, 0), 0)

    in_specs = [
        pl.BlockSpec((TILE, 128), lambda i: (jnp.minimum(i, half - 1), 2)),
        pl.BlockSpec((TILE, 128), upper),
    ]
    in_specs += [pl.BlockSpec((kv.shape[0], 256), lambda i: (0, 0)) for kv in kvs]
    args = [q_own, q_oth, *kvs]
    if not first:
        in_specs.append(pl.BlockSpec((TILE, 256), lambda i: (i, 0)))
        args.append(state)
    if last:
        in_specs.append(pl.BlockSpec(weight.shape, lambda i: (0, 0)))
        args.append(weight)
        out_specs = [pl.BlockSpec((TILE, 128), lower), pl.BlockSpec((TILE, 128), upper)]
        out_shape = [jax.ShapeDtypeStruct((rows, 128), jnp.float32)] * 2
    else:
        out_specs = pl.BlockSpec((TILE, 256), lambda i: (i, 0))
        out_shape = jax.ShapeDtypeStruct((2 * rows, 256), jnp.float32)
    return pl.pallas_call(
        functools.partial(flash_kernel, first, last, len(kvs), half),
        grid=(2 * half,),
        in_specs=in_specs,
        out_specs=out_specs,
        out_shape=out_shape,
        compiler_params=pltpu.CompilerParams(vmem_limit_bytes=40 << 20),
        cost_estimate=pl.CostEstimate(
            flops=2 * rows * keys * 512 * 2,
            bytes_accessed=rows * 4096,
            transcendentals=2 * rows * keys,
        ),
    )(*args)


def tail_kernel(
    above_ref,
    mine_ref,
    below_ref,
    noisy_ref,
    cache_ref,
    affine_ref,
    token_ok_ref,
    cell_ok_ref,
    w1_ref,
    b1_ref,
    gain_ref,
    mid_ref,
    w2_ref,
    b2_ref,
    den_ref,
    out_ref,
    w2_buf,
    sems,
    vel,
    lat,
    first,
    act,
    wide,
):
    for tap in range(9):
        pltpu.make_async_copy(w2_ref.at[tap], w2_buf.at[tap], sems.at[tap]).start()
    for at, rows in enumerate(
        (above_ref[...], mine_ref[0:16, :], mine_ref[16:32, :], below_ref[...])
    ):
        turned = pltpu.roll(rows, 64, axis=1)
        for f in range(F):
            vel[f, at, 0:4, :] = rows[f * 4 : f * 4 + 4]
            vel[f, at, 4:8, :] = turned[f * 4 : f * 4 + 4]
    level, scale, mean = affine_ref[0:1, :], affine_ref[1:2, :], affine_ref[2:3, :]
    denoised = noisy_ref[...] - level * vel[:, :, :, 0:64]
    den_ref[...] = denoised
    latent = jnp.where(token_ok_ref[...] > 0, denoised * scale + mean, 0.0)
    lat[...] = jnp.zeros(lat.shape, jnp.float32)
    lat[0:2, :, 0:8, 0:64] = cache_ref[...]
    lat[2:6, :, 0:8, 0:64] = latent.astype(jnp.bfloat16).astype(jnp.float32)
    here = lat[:, :, 0:8, :].reshape(192, 128)
    right = pltpu.roll(lat[:, :, 1:9, :].reshape(192, 128), 64, axis=1)
    lane = lax.broadcasted_iota(jnp.int32, (192, 128), 1)
    pair = jnp.where(lane < 64, here, right).reshape(6, 4, 8, 128)
    lower = jnp.concatenate([pair[:, 1:4], pair[:, 3:4]], axis=1)
    window = jnp.concatenate([pair, lower], axis=3).reshape(192, 256).astype(jnp.bfloat16)
    parts = C1 // 128
    for k in range(parts):
        act[k, 0:2, :, 0:14, :] = mid_ref[:, :, :, pl.ds(k * 128, 128)]
    gain = gain_ref[...]
    for p in range(2):
        for q in range(2):
            lanes = pl.ds((2 * p + q) * C1, C1)
            value = b1_ref[...]
            for t in range(3):
                value = value + jnp.dot(
                    window[t * 32 : t * 32 + 128],
                    w1_ref[t, :, lanes],
                    preferred_element_type=jnp.float32,
                )
            power = jnp.mean(value * value, axis=1, keepdims=True)
            normed = value * lax.rsqrt(power + EPSILON) * gain
            active = (normed / (1.0 + jnp.exp(-normed))).reshape(F, 32, C1)
            active = active * cell_ok_ref[2 * p + q, :, 0:1]
            value = value.reshape(F, 4, 8, C1)
            active = active.reshape(F, 4, 8, C1)
            for r in range(3):
                cols = pl.ds(q, 8, stride=2)
                for k in range(parts):
                    part = slice(k * 128, k * 128 + 128)
                    for f in range(F):
                        first[k, f, 2 * r + p, cols, :] = value[f, r, :, part]
                        act[k, f + 2, 2 * r + p, cols, :] = active[f, r, :, part]
    for v in range(3):
        for k in range(parts):
            wide[:, :, :, pl.ds(v * C1 + k * 128, 128)] = act[k, :, :, pl.ds(v, 16), :].astype(
                jnp.bfloat16
            )
    middle = [first[k, :, 1:5, pl.ds(1, 16), :].reshape(256, 128) for k in range(parts)]
    total = jnp.concatenate(middle, axis=1) + b2_ref[...]
    for tap in range(9):
        t, u = divmod(tap, 3)
        pltpu.make_async_copy(w2_ref.at[tap], w2_buf.at[tap], sems.at[tap]).wait()
        rows = wide[t : t + 4, u : u + 4].reshape(256, 3 * C1)
        total = total + jnp.dot(rows, w2_buf[tap], preferred_element_type=jnp.float32)
    out_ref[...] = total.reshape(F, 4, 16, C1)[:, :, 0:12].astype(jnp.bfloat16)


def tail(*args):
    specs = [pl.BlockSpec(memory_space=pltpu.VMEM)] * len(args)
    specs[12] = pl.BlockSpec(memory_space=pl.ANY)
    return pl.pallas_call(
        tail_kernel,
        in_specs=specs,
        out_specs=[pl.BlockSpec(memory_space=pltpu.VMEM)] * 2,
        out_shape=[
            jax.ShapeDtypeStruct((F, 4, 8, 64), jnp.float32),
            jax.ShapeDtypeStruct((F, 4, 12, C1), jnp.bfloat16),
        ],
        scratch_shapes=[
            pltpu.VMEM((9, 3 * C1, C1), jnp.bfloat16),
            pltpu.SemaphoreType.DMA((9,)),
            pltpu.VMEM((F, 4, 8, 128), jnp.float32),
            pltpu.VMEM((6, 4, 16, 128), jnp.float32),
            pltpu.VMEM((C1 // 128, F, 6, 24, 128), jnp.float32),
            pltpu.VMEM((C1 // 128, 6, 6, 24, 128), jnp.float32),
            pltpu.VMEM((6, 6, 16, 3 * C1), jnp.bfloat16),
        ],
        compiler_params=pltpu.CompilerParams(vmem_limit_bytes=32 << 20),
    )(*args)


def window_weights(weight):
    cells = [
        jnp.pad(weight, ((0, 0), (p, 1 - p), (q, 1 - q), (0, 0), (0, 0)))
        for p in range(2)
        for q in range(2)
    ]
    joined = jnp.stack(cells, axis=4).reshape(3, 2, 2, 2, 2, LAT, 4, C1)
    return joined.transpose(0, 1, 3, 2, 4, 5, 6, 7).reshape(3, 16 * LAT, 4 * C1)


def by_token(cells):
    frames = cells.shape[0]
    split = cells.reshape(frames, 4, 2, 8, 2, LAT).transpose(0, 1, 3, 2, 4, 5)
    return split.reshape(frames, 4, 8, 4 * LAT)


def along(axis, step):
    count = lax.axis_size(axis)
    return [(i, i + step) for i in range(count) if 0 <= i + step < count]


def swap_edges(parts, axis, dims, widths):
    def cut(tail):
        flat = []
        for part, dim, width in zip(parts, dims, widths):
            size = part.shape[dim]
            start = size - width if tail else 0
            flat.append(lax.slice_in_dim(part, start, start + width, axis=dim).reshape(-1))
        return jnp.concatenate(flat).reshape(-1, 128)

    before = lax.ppermute(cut(True), axis, along(axis, 1)).reshape(-1)
    after = lax.ppermute(cut(False), axis, along(axis, -1)).reshape(-1)
    wider, at = [], 0
    for part, dim, width in zip(parts, dims, widths):
        shape = list(part.shape)
        shape[dim] = width
        size = math.prod(shape)
        wider.append(
            jnp.concatenate(
                [
                    before[at : at + size].reshape(shape),
                    part,
                    after[at : at + size].reshape(shape),
                ],
                axis=dim,
            )
        )
        at += size
    return wider


def input_halos(noisy, cache_in, cache_mid):
    both = jnp.concatenate([cache_in.astype(jnp.float32), noisy], axis=0)
    parts = [both, cache_mid.astype(jnp.float32)]
    parts = swap_edges(parts, SEQ, (1, 1), (2, 1))
    both, cache_mid = swap_edges(parts, BLK, (2, 2), (2, 1))
    both = by_token(both)
    return both[2:], both[:2], cache_mid


def pack_kernel(q_ref, k_ref, v_ref, out_ref):
    for h in range(out_ref.shape[0]):
        lanes = pl.ds(h * HEAD_DIM, HEAD_DIM)
        out_ref[h, :, 0:128] = k_ref[:, lanes]
        out_ref[h, :, 128:256] = v_ref[:, lanes]
        out_ref[h, :, 256:384] = q_ref[:, lanes]


def pack(query_vectors, key_vectors, value_vectors):
    tokens, width = query_vectors.shape
    heads = width // HEAD_DIM
    block = pl.BlockSpec((tokens, width // 2), lambda i: (0, i))
    return pl.pallas_call(
        pack_kernel,
        grid=(2,),
        in_specs=[block] * 3,
        out_specs=pl.BlockSpec((heads // 2, tokens, 3 * HEAD_DIM), lambda i: (i, 0, 0)),
        out_shape=jax.ShapeDtypeStruct((heads, tokens, 3 * HEAD_DIM), jnp.bfloat16),
    )(query_vectors, key_vectors, value_vectors)


def merge_kernel(own_ref, oth_ref, out_ref, vel_ref, piece_ref):
    own, oth = own_ref[...], oth_ref[...]
    gap = pltpu.roll(oth - own, 64, axis=1)
    share = 1.0 / (1.0 + jnp.exp2(gap))
    vel = own * share + oth * (1.0 - share)
    lane = lax.broadcasted_iota(jnp.int32, vel.shape, 1)
    vel_ref[...] = jnp.where(lane < 64, vel, pltpu.roll(vel, 64, axis=1))
    low = lax.broadcasted_iota(jnp.int32, (16, 128), 1) < 64
    zero = jnp.zeros((16, 128), jnp.float32)

    def column(r, at):
        if at < 0 or at >= 48:
            return zero
        return vel_ref[pl.ds(r * 48 + at, 16, stride=96), :]

    for b in range(8):
        for r in range(2):
            for c in range(4):
                at = 6 * b - 1 + c
                both = jnp.where(low, column(r, at), column(r, at + 4))
                for y in range(4):
                    piece_ref[y, b, pl.ds(r * 16 + c, 4, stride=4), :] = both[y * 4 : y * 4 + 4]
    out_ref[...] = piece_ref[...].astype(jnp.bfloat16)


def merge(own, oth):
    rows = own.shape[0]
    whole = pl.BlockSpec((rows, 128), lambda: (0, 0))
    shape = (4, 8, 32, 128)
    return pl.pallas_call(
        merge_kernel,
        in_specs=[whole, whole],
        out_specs=pl.BlockSpec(shape, lambda: (0, 0, 0, 0)),
        out_shape=jax.ShapeDtypeStruct(shape, jnp.bfloat16),
        scratch_shapes=[
            pltpu.VMEM((rows, 128), jnp.float32),
            pltpu.VMEM(shape, jnp.float32),
        ],
        compiler_params=pltpu.CompilerParams(vmem_limit_bytes=24 << 20),
    )(own, oth)


def attention(query_vectors, key_vectors, value_vectors, weight_head, work):
    packed = pack(query_vectors, key_vectors, value_vectors)
    heads, tokens = packed.shape[:2]
    moved = lax.all_to_all(packed, HEAD, split_axis=0, concat_axis=0, tiled=True)
    moved, work = lax.optimization_barrier((moved, work))
    moved = moved.reshape(heads * tokens, 3 * HEAD_DIM)
    swap = [(0, 1), (1, 0)]
    right = [(i, (i + 1) % 4) for i in range(4)]
    left = [((i + 1) % 4, i) for i in range(4)]
    mid = moved.shape[0] // 2
    a, b = moved[:mid, :256], moved[mid:, :256]
    left_a = lax.ppermute(a, "y", right)
    right_b = lax.ppermute(b, "y", left)
    q_oth = lax.ppermute(moved[:, 256:], "core", swap)
    state = flash(moved, q_oth, [moved])
    left_b = lax.ppermute(b, "y", right)
    right_a = lax.ppermute(a, "y", left)
    state = flash(moved, q_oth, [left_a, right_b], state)
    far_a = lax.ppermute(left_a, "y", right)
    far_b = lax.ppermute(right_b, "y", left)
    state = flash(moved, q_oth, [left_b, right_a], state)
    head = lax.axis_index(HEAD)
    weight = lax.dynamic_slice_in_dim(weight_head, head * HEAD_DIM, HEAD_DIM, axis=0)
    weight = jnp.pad(weight, ((0, 0), (0, 64)))
    own, oth = flash(moved, q_oth, [far_a, far_b], state, weight)
    oth = lax.ppermute(oth, "core", swap)
    partial = merge(own, oth).reshape(heads, 32, 128)
    parts = lax.all_to_all(partial, HEAD, split_axis=0, concat_axis=0, tiled=True)
    return jnp.sum(parts.astype(jnp.float32), axis=0), work


def shards(
    query_vectors,
    key_vectors,
    value_vectors,
    weight_head,
    noisy_latent,
    noise_level,
    latent_mean,
    latent_scale,
    cache_in,
    weight_in,
    bias_in,
    norm_gain,
    cache_mid,
    weight_mid,
    bias_mid,
):
    row, col = lax.axis_index(SEQ), lax.axis_index(BLK)
    last_row, last_col = lax.axis_size(SEQ) - 1, lax.axis_size(BLK) - 1
    row_ok, col_ok = inside(8, row, last_row), inside(16, col, last_col)
    token_ok = (row_ok[::2, None] & col_ok[None, ::2]).astype(jnp.float32)
    token_ok = jnp.broadcast_to(token_ok[:, :, None], (4, 8, 4 * LAT))
    cell_ok = inside(8, row, last_row)[1:7, None] & jnp.pad(col_ok[1:15], (0, 2))[None, :]
    cell_ok = cell_ok.reshape(3, 2, 8, 2).transpose(1, 3, 0, 2).astype(jnp.float32)
    cell_ok = jnp.pad(cell_ok, ((0, 0), (0, 0), (0, 1), (0, 0))).reshape(4, 32, 1)
    cell_ok = jnp.broadcast_to(cell_ok, (4, 32, 128))
    level = jnp.broadcast_to(noise_level, (4 * LAT,))
    affine = jnp.stack([level, jnp.tile(latent_scale, 4), jnp.tile(latent_mean, 4)])

    halos = input_halos(noisy_latent, cache_in, cache_mid)
    work = (*halos, token_ok, cell_ok, affine, window_weights(weight_in))
    mine, work = attention(query_vectors, key_vectors, value_vectors, weight_head, work)
    noisy, cache_first, cache_second, token_ok, cell_ok, affine, weight_first = work

    above = lax.ppermute(mine[16:], SEQ, along(SEQ, 1))
    below = lax.ppermute(mine[:16], SEQ, along(SEQ, -1))
    denoised, features = tail(
        above,
        mine,
        below,
        noisy,
        cache_first,
        affine,
        token_ok,
        cell_ok,
        weight_first,
        bias_in.reshape(1, C1),
        norm_gain.reshape(1, C1),
        cache_second,
        weight_mid.reshape(9, 3 * C1, C1),
        bias_mid.reshape(1, C1),
    )
    denoised = denoised[:, 1:3, 1:7].reshape(F, 2, 6, 2, 2, LAT).transpose(0, 1, 3, 2, 4, 5)
    return denoised.reshape(F, 4, 12, LAT), features


def inside(count, index, last):
    at = jnp.arange(count)
    return ((at >= 2) | (index > 0)) & ((at < count - 2) | (index < last))


def solution(mesh):
    inner = Mesh(mesh.devices.reshape(4, 4, 2, 2, 4), SHARD)
    tokens, tile = P(SHARD, None), P(None, SEQ, BLK, None)
    in_specs = (
        tokens,
        tokens,
        tokens,
        P(),
        tile,
        P(),
        P(),
        P(),
        tile,
        P(),
        P(),
        P(),
        tile,
        P(),
        P(),
    )
    return jax.shard_map(
        shards, mesh=inner, in_specs=in_specs, out_specs=(tile, tile), check_vma=False
    )
```

```python
import functools
import math

import jax
import jax.numpy as jnp
from jax import lax
from jax.experimental import pallas as pl
from jax.experimental.pallas import tpu as pltpu
from jax.sharding import Mesh
from jax.sharding import PartitionSpec as P

HEAD_DIM = 128
LAT = 16
C1 = 384
F = 4
EPSILON = 1e-06

SEQ = ("y", "zh", "core")
BLK = ("zl", "x")
HEAD = ("zh", "zl", "x")
SHARD = SEQ + BLK

TILE = 512
SUB = 256
CHUNK = 768
NT = (((1,), (1,)), ((), ()))


def lane_max(s):
    t = s[:, :128]
    for j in range(1, s.shape[1] // 128):
        t = jnp.maximum(t, s[:, j * 128 : (j + 1) * 128])
    return jnp.max(t, axis=1, keepdims=True)


def flash_kernel(first, last, n_kv, half, *refs):
    qo_ref, qx_ref = refs[:2]
    kv_refs = refs[2 : 2 + n_kv]
    refs = refs[2 + n_kv :]
    if not first:
        st_ref, refs = refs[0], refs[1:]
    if last:
        w_ref, own_ref, oth_ref = refs
    else:
        (so_ref,) = refs
    i = pl.program_id(0)
    scale = math.log2(math.e) / math.sqrt(HEAD_DIM)
    qf = jnp.where(i < half, qo_ref[...], qx_ref[...]).astype(jnp.float32) * scale
    q_hi = qf.astype(jnp.bfloat16)
    q_lo = (qf - q_hi.astype(jnp.float32)).astype(jnp.bfloat16)
    q = jnp.concatenate([q_hi, q_lo], axis=1)
    subs = TILE // SUB
    tops, accs = [], []
    for r in range(subs):
        if first:
            tops.append(jnp.full((SUB, 128), -1e30, jnp.float32))
            accs.append(jnp.zeros((SUB, 256), jnp.float32))
        else:
            st = st_ref[pl.ds(r * SUB, SUB), :]
            acc_l = st[:, 128:]
            lane = lax.broadcasted_iota(jnp.int32, (SUB, 128), 1)
            total = jnp.max(jnp.where(lane < 64, acc_l, -1e30), axis=1, keepdims=True)
            top = jnp.max(jnp.where(lane < 64, -1e30, acc_l), axis=1, keepdims=True)
            tops.append(jnp.broadcast_to(top, (SUB, 128)))
            accs.append(
                jnp.concatenate([st[:, :128], jnp.broadcast_to(total, (SUB, 128))], axis=1)
            )
    items = [
        (r, b, c)
        for b in range(n_kv)
        for c in range(kv_refs[b].shape[0] // CHUNK)
        for r in range(subs)
    ]
    ones = jnp.ones((CHUNK, 128), jnp.bfloat16)

    def score(item):
        r, b, c = item
        k = kv_refs[b][pl.ds(c * CHUNK, CHUNK), :128]
        return lax.dot_general(
            q[r * SUB : (r + 1) * SUB],
            jnp.concatenate([k, k], axis=1),
            NT,
            preferred_element_type=jnp.float32,
        )

    s = score(items[0])
    for n, (r, b, c) in enumerate(items):
        following = score(items[n + 1]) if n + 1 < len(items) else None
        top = jnp.maximum(tops[r], lane_max(s))
        p = jnp.exp2(s - top[:, :1]).astype(jnp.bfloat16)
        fade = jnp.exp2(tops[r] - top)
        v = jnp.concatenate([kv_refs[b][pl.ds(c * CHUNK, CHUNK), 128:], ones], axis=1)
        accs[r] = accs[r] * jnp.concatenate([fade, fade], axis=1) + jnp.dot(
            p, v, preferred_element_type=jnp.float32
        )
        tops[r] = top
        s = following
    lane = lax.broadcasted_iota(jnp.int32, (SUB, 128), 1)
    outs = []
    for r in range(subs):
        if last:
            total = accs[r][:, 128:]
            mixed = (accs[r][:, :128] / total).astype(jnp.bfloat16)
            u = jnp.dot(mixed, w_ref[...], preferred_element_type=jnp.float32)
            outs.append(jnp.where(lane < 64, u, tops[r] + jnp.log2(total)))
        else:
            so_ref[pl.ds(r * SUB, SUB), :] = jnp.concatenate(
                [accs[r][:, :128], jnp.where(lane < 64, accs[r][:, 128:], tops[r])], axis=1
            )
    if last:

        @pl.when(i < half)
        def _():
            for r in range(subs):
                own_ref[pl.ds(r * SUB, SUB), :] = outs[r]

        @pl.when(i >= half)
        def _():
            for r in range(subs):
                oth_ref[pl.ds(r * SUB, SUB), :] = outs[r]


def flash(q_own, q_oth, kvs, state=None, weight=None):
    first, last = state is None, weight is not None
    rows = q_own.shape[0]
    half = rows // TILE
    keys = sum(kv.shape[0] for kv in kvs)

    def lower(i):
        return (jnp.minimum(i, half - 1), 0)

    def upper(i):
        return (jnp.maximum(i - half, 0), 0)

    in_specs = [
        pl.BlockSpec((TILE, 128), lambda i: (jnp.minimum(i, half - 1), 2)),
        pl.BlockSpec((TILE, 128), upper),
    ]
    in_specs += [pl.BlockSpec((kv.shape[0], 256), lambda i: (0, 0)) for kv in kvs]
    args = [q_own, q_oth, *kvs]
    if not first:
        in_specs.append(pl.BlockSpec((TILE, 256), lambda i: (i, 0)))
        args.append(state)
    if last:
        in_specs.append(pl.BlockSpec(weight.shape, lambda i: (0, 0)))
        args.append(weight)
        out_specs = [pl.BlockSpec((TILE, 128), lower), pl.BlockSpec((TILE, 128), upper)]
        out_shape = [jax.ShapeDtypeStruct((rows, 128), jnp.float32)] * 2
    else:
        out_specs = pl.BlockSpec((TILE, 256), lambda i: (i, 0))
        out_shape = jax.ShapeDtypeStruct((2 * rows, 256), jnp.float32)
    return pl.pallas_call(
        functools.partial(flash_kernel, first, last, len(kvs), half),
        grid=(2 * half,),
        in_specs=in_specs,
        out_specs=out_specs,
        out_shape=out_shape,
        compiler_params=pltpu.CompilerParams(vmem_limit_bytes=20 << 20),
        cost_estimate=pl.CostEstimate(
            flops=2 * rows * keys * 512 * 2,
            bytes_accessed=rows * 4096,
            transcendentals=2 * rows * keys,
        ),
    )(*args)


def inside(at, low, high, before, after):
    return ((at > low) | before) & ((at < high) | after)


def tail_kernel(
    above_ref,
    mine_ref,
    below_ref,
    cells_ref,
    affine_ref,
    beyond_ref,
    w1_ref,
    b1_ref,
    gain_ref,
    mid_ref,
    w2_ref,
    b2_ref,
    den_ref,
    out_ref,
    w2_buf,
    sems,
    vel,
    lat,
    den,
    first,
    act,
    wide,
):
    for tap in range(9):
        pltpu.make_async_copy(w2_ref.at[tap], w2_buf.at[tap], sems.at[tap]).start()
    for at, rows in enumerate(
        (above_ref[...], mine_ref[0:16, :], mine_ref[16:32, :], below_ref[...])
    ):
        turned = pltpu.roll(rows, 64, axis=1)
        for f in range(F):
            vel[f, at, 0:4, :] = rows[f * 4 : f * 4 + 4]
            vel[f, at, 4:8, :] = turned[f * 4 : f * 4 + 4]
    level, scale, mean = affine_ref[0:1, :], affine_ref[1:2, :], affine_ref[2:3, :]
    denoised = cells_ref[2:6, :, :, 0:64] - level * vel[:, :, :, 0:64]
    up, down, before, after = (beyond_ref[k] > 0 for k in range(4))
    row = lax.broadcasted_iota(jnp.int32, denoised.shape, 1)
    col = lax.broadcasted_iota(jnp.int32, denoised.shape, 2)
    kept = inside(row, 0, 3, up, down) & inside(col, 0, 7, before, after)
    latent = jnp.where(kept, denoised * scale + mean, 0.0)
    for k in range(4):
        part = jnp.concatenate([denoised, denoised], axis=3).reshape(F * 32, 128)
        part = pltpu.roll(part, 128 - LAT * k, axis=1) if k else part
        part = part.reshape(F, 4, 8, 128)
        for f in range(F):
            for r in range(2):
                den[f, 2 * r + k // 2, pl.ds(k % 2, 8, stride=2), :] = part[f, r + 1]
    den_ref[...] = den[:, :, 2:14, 0:LAT]
    lat[...] = jnp.zeros(lat.shape, jnp.float32)
    lat[0:2, :, 0:8, 0:64] = cells_ref[0:2, :, :, 0:64]
    lat[2:6, :, 0:8, 0:64] = latent.astype(jnp.bfloat16).astype(jnp.float32)
    here = lat[:, :, 0:8, :].reshape(192, 128)
    right = pltpu.roll(lat[:, :, 1:9, :].reshape(192, 128), 64, axis=1)
    lane = lax.broadcasted_iota(jnp.int32, (192, 128), 1)
    pair = jnp.where(lane < 64, here, right).reshape(6, 4, 8, 128)
    lower = jnp.concatenate([pair[:, 1:4], pair[:, 3:4]], axis=1)
    window = jnp.concatenate([pair, lower], axis=3).reshape(192, 256).astype(jnp.bfloat16)
    parts = C1 // 128
    for k in range(parts):
        act[k, 0:2, :, 0:16, :] = mid_ref[:, :, :, pl.ds(k * 128, 128)]
    gain = gain_ref[...]
    for p in range(2):
        for q in range(2):
            lanes = pl.ds((2 * p + q) * C1, C1)
            value = b1_ref[...]
            for t in range(3):
                value = value + jnp.dot(
                    window[t * 32 : t * 32 + 128],
                    w1_ref[t, :, lanes],
                    preferred_element_type=jnp.float32,
                )
            power = jnp.mean(value * value, axis=1, keepdims=True)
            normed = value * lax.rsqrt(power + EPSILON) * gain
            active = (normed / (1.0 + jnp.exp(-normed))).reshape(F, 32, C1)
            at = lax.broadcasted_iota(jnp.int32, (32, C1), 0)
            kept = inside(2 * (at // 8) + p, 0, 5, up, down)
            kept = kept & inside(2 * (at % 8) + q, 0, 13, before, after)
            active = jnp.where(kept, active, 0.0)
            value = value.reshape(F, 4, 8, C1)
            active = active.reshape(F, 4, 8, C1)
            for r in range(3):
                cols = pl.ds(q, 8, stride=2)
                for k in range(parts):
                    part = slice(k * 128, k * 128 + 128)
                    for f in range(F):
                        first[k, f, 2 * r + p, cols, :] = value[f, r, :, part]
                        act[k, f + 2, 2 * r + p, cols, :] = active[f, r, :, part]
    for v in range(3):
        for k in range(parts):
            wide[:, :, :, pl.ds(v * C1 + k * 128, 128)] = act[k, :, :, pl.ds(v, 16), :].astype(
                jnp.bfloat16
            )
    middle = [first[k, :, 1:5, pl.ds(1, 16), :].reshape(256, 128) for k in range(parts)]
    total = jnp.concatenate(middle, axis=1) + b2_ref[...]
    for tap in range(9):
        t, u = divmod(tap, 3)
        pltpu.make_async_copy(w2_ref.at[tap], w2_buf.at[tap], sems.at[tap]).wait()
        rows = wide[t : t + 4, u : u + 4].reshape(256, 3 * C1)
        total = total + jnp.dot(rows, w2_buf[tap], preferred_element_type=jnp.float32)
    out_ref[...] = total.reshape(F, 4, 16, C1)[:, :, 0:12].astype(jnp.bfloat16)


def tail(*args):
    specs = [pl.BlockSpec(memory_space=pltpu.VMEM)] * len(args)
    specs[5] = pl.BlockSpec(memory_space=pltpu.SMEM)
    specs[10] = pl.BlockSpec(memory_space=pl.ANY)
    return pl.pallas_call(
        tail_kernel,
        in_specs=specs,
        out_specs=[pl.BlockSpec(memory_space=pltpu.VMEM)] * 2,
        out_shape=[
            jax.ShapeDtypeStruct((F, 4, 12, LAT), jnp.float32),
            jax.ShapeDtypeStruct((F, 4, 12, C1), jnp.bfloat16),
        ],
        scratch_shapes=[
            pltpu.VMEM((9, 3 * C1, C1), jnp.bfloat16),
            pltpu.SemaphoreType.DMA((9,)),
            pltpu.VMEM((F, 4, 8, 128), jnp.float32),
            pltpu.VMEM((6, 4, 16, 128), jnp.float32),
            pltpu.VMEM((F, 4, 16, 128), jnp.float32),
            pltpu.VMEM((C1 // 128, F, 6, 24, 128), jnp.float32),
            pltpu.VMEM((C1 // 128, 6, 6, 24, 128), jnp.float32),
            pltpu.VMEM((6, 6, 16, 3 * C1), jnp.bfloat16),
        ],
        compiler_params=pltpu.CompilerParams(vmem_limit_bytes=32 << 20),
    )(*args)


def window_kernel(w_ref, out_ref):
    out_ref[...] = jnp.zeros(out_ref.shape, out_ref.dtype)
    for t in range(3):
        for u in range(3):
            for v in range(3):
                taps = w_ref[t, u, v]
                for p in range(2):
                    for q in range(2):
                        (dr, a), (dc, b) = divmod(p + u, 2), divmod(q + v, 2)
                        at = dr * 128 + dc * 64 + a * 32 + b * 16
                        out_ref[t, pl.ds(at, LAT), pl.ds((2 * p + q) * C1, C1)] = taps


def window_weights(weight):
    return pl.pallas_call(
        window_kernel,
        out_shape=jax.ShapeDtypeStruct((3, 16 * LAT, 4 * C1), jnp.bfloat16),
        compiler_params=pltpu.CompilerParams(vmem_limit_bytes=16 << 20),
    )(weight)


def put_frames(ref, rows, tokens):
    count = tokens[0].shape[0]
    low = lax.broadcasted_iota(jnp.int32, (count, 128), 1) < 64
    for i in range(2):
        for h in range(2):
            one = tokens[i + 2 * h]
            two = pltpu.roll(tokens[i + 4], 64, axis=1) if h == 0 else jnp.zeros_like(one)
            ref[i, pl.ds(rows + h * count, count), 384:512] = jnp.where(low, one, two)


def get_frames(ref, rows, count):
    out = {}
    for i in range(2):
        for h in range(2):
            both = ref[i, pl.ds(rows + h * count, count), 384:512]
            out[i + 2 * h] = both
            if h == 0:
                out[i + 4] = pltpu.roll(both, 64, axis=1)
    return [out[f] for f in range(6)]


def edge_rows_kernel(noisy_ref, cache_ref, mid_ref, tok_ref, down_ref, up_ref, cells):
    cells[...] = jnp.zeros(cells.shape, jnp.float32)
    cells[0:2, :, 0:12, 0:LAT] = cache_ref[...].astype(jnp.float32)
    cells[2:6, :, 0:12, 0:LAT] = noisy_ref[...]
    lane = lax.broadcasted_iota(jnp.int32, (8, 128), 1)
    tokens = {}
    for r in range(2):
        for f in range(6):
            token = jnp.zeros((8, 128), jnp.float32)
            for k in range(4):
                part = cells[f, 2 * r + k // 2, pl.ds(k % 2, 8, stride=2), :]
                part = pltpu.roll(part, LAT * k, axis=1) if k else part
                token = jnp.where((lane >= LAT * k) & (lane < LAT * k + LAT), part, token)
            tok_ref[f, r] = token
            tokens[f, r] = token
    for ref, row, r in ((down_ref, 3, 1), (up_ref, 0, 0)):
        ref[...] = jnp.zeros(ref.shape, jnp.float32)
        ref[:, 0:12, 0:C1] = mid_ref[:, row].astype(jnp.float32)
        put_frames(ref, 0, [tokens[f, r] for f in range(6)])


def edge_cols_kernel(tok_ref, mid_ref, above_ref, below_ref, toks, mids, right_ref, left_ref):
    above, below = get_frames(above_ref, 0, 8), get_frames(below_ref, 0, 8)
    for f in range(6):
        toks[f, 0] = above[f]
        toks[f, 1] = tok_ref[f, 0]
        toks[f, 2] = tok_ref[f, 1]
        toks[f, 3] = below[f]
    mids[...] = jnp.zeros(mids.shape, jnp.float32)
    mids[:, 0, 0:12, :] = above_ref[:, 0:12, 0:C1]
    mids[:, 1:5, 0:12, :] = mid_ref[...].astype(jnp.float32)
    mids[:, 5, 0:12, :] = below_ref[:, 0:12, 0:C1]
    for ref, token, col in ((right_ref, 5, 11), (left_ref, 0, 0)):
        ref[...] = jnp.zeros(ref.shape, jnp.float32)
        for i in range(2):
            for row in range(6):
                ref[i, pl.ds(row, 1), 0:C1] = mids[i, row, pl.ds(col, 1), :]
        for r in range(4):
            put_rows(ref, r, [toks[f, r, pl.ds(token, 1), :] for f in range(6)])


def put_rows(ref, r, tokens):
    low = lax.broadcasted_iota(jnp.int32, (1, 128), 1) < 64
    for i in range(2):
        for h in range(2):
            one = tokens[i + 2 * h]
            two = pltpu.roll(tokens[i + 4], 64, axis=1) if h == 0 else jnp.zeros_like(one)
            ref[i, pl.ds(4 * h + r, 1), 384:512] = jnp.where(low, one, two)


def place_kernel(toks, mids, left_ref, right_ref, cells_ref, cache_ref):
    cells_ref[...] = jnp.zeros(cells_ref.shape, jnp.float32)
    cache_ref[...] = jnp.zeros(cache_ref.shape, jnp.float32)
    for f in range(6):
        for r in range(4):
            cells_ref[f, r, 1:7, :] = toks[f, r, 0:6, :]
    cache_ref[:, :, 1:13, :] = mids[:, :, 0:12, :]
    for ref, token, col in ((left_ref, 0, 0), (right_ref, 7, 13)):
        frames = get_frames(ref, 0, 4)
        for f in range(6):
            for r in range(4):
                cells_ref[f, r, pl.ds(token, 1), :] = frames[f][r : r + 1]
        for i in range(2):
            for row in range(6):
                cache_ref[i, row, pl.ds(col, 1), :] = ref[i, pl.ds(row, 1), 0:C1]


def small_call(kernel, shapes, scratch=()):
    return pl.pallas_call(
        kernel,
        out_shape=[jax.ShapeDtypeStruct(shape, jnp.float32) for shape in shapes],
        scratch_shapes=[pltpu.VMEM(shape, jnp.float32) for shape in scratch],
        compiler_params=pltpu.CompilerParams(vmem_limit_bytes=8 << 20),
    )


def along(axis, step):
    count = lax.axis_size(axis)
    return [(i, i + step) for i in range(count) if 0 <= i + step < count]


def input_halos(noisy, cache_in, cache_mid):
    edge = (2, 16, 512)
    toks, down, up = small_call(
        edge_rows_kernel, [(6, 2, 8, 128), edge, edge], [(6, 4, 16, 128)]
    )(noisy, cache_in, cache_mid)
    above = lax.ppermute(down, SEQ, along(SEQ, 1))
    below = lax.ppermute(up, SEQ, along(SEQ, -1))
    side = (2, 8, 512)
    toks, mids, right, left = small_call(
        edge_cols_kernel, [(6, 4, 8, 128), (2, 6, 16, C1), side, side]
    )(toks, cache_mid, above, below)
    before = lax.ppermute(right, BLK, along(BLK, 1))
    after = lax.ppermute(left, BLK, along(BLK, -1))
    return small_call(place_kernel, [(6, 4, 8, 128), (2, 6, 16, C1)])(toks, mids, before, after)


def pack_kernel(q_ref, k_ref, v_ref, out_ref):
    for h in range(out_ref.shape[0]):
        lanes = pl.ds(h * HEAD_DIM, HEAD_DIM)
        out_ref[h, :, 0:128] = k_ref[:, lanes]
        out_ref[h, :, 128:256] = v_ref[:, lanes]
        out_ref[h, :, 256:384] = q_ref[:, lanes]


def pack(query_vectors, key_vectors, value_vectors):
    tokens, width = query_vectors.shape
    heads = width // HEAD_DIM
    block = pl.BlockSpec((tokens, width // 2), lambda i: (0, i))
    return pl.pallas_call(
        pack_kernel,
        grid=(2,),
        in_specs=[block] * 3,
        out_specs=pl.BlockSpec((heads // 2, tokens, 3 * HEAD_DIM), lambda i: (i, 0, 0)),
        out_shape=jax.ShapeDtypeStruct((heads, tokens, 3 * HEAD_DIM), jnp.bfloat16),
    )(query_vectors, key_vectors, value_vectors)


def merge_kernel(own_ref, oth_ref, out_ref, vel_ref, piece_ref):
    own, oth = own_ref[...], oth_ref[...]
    gap = pltpu.roll(oth - own, 64, axis=1)
    share = 1.0 / (1.0 + jnp.exp2(gap))
    vel = own * share + oth * (1.0 - share)
    lane = lax.broadcasted_iota(jnp.int32, vel.shape, 1)
    vel_ref[...] = jnp.where(lane < 64, vel, pltpu.roll(vel, 64, axis=1))
    low = lax.broadcasted_iota(jnp.int32, (16, 128), 1) < 64
    zero = jnp.zeros((16, 128), jnp.float32)

    def column(r, at):
        if at < 0 or at >= 48:
            return zero
        return vel_ref[pl.ds(r * 48 + at, 16, stride=96), :]

    for b in range(8):
        for r in range(2):
            for c in range(4):
                at = 6 * b - 1 + c
                both = jnp.where(low, column(r, at), column(r, at + 4))
                for y in range(4):
                    piece_ref[y, b, pl.ds(r * 16 + c, 4, stride=4), :] = both[y * 4 : y * 4 + 4]
    out_ref[...] = piece_ref[...].astype(jnp.bfloat16)


def merge(own, oth):
    rows = own.shape[0]
    whole = pl.BlockSpec((rows, 128), lambda: (0, 0))
    shape = (4, 8, 32, 128)
    return pl.pallas_call(
        merge_kernel,
        in_specs=[whole, whole],
        out_specs=pl.BlockSpec(shape, lambda: (0, 0, 0, 0)),
        out_shape=jax.ShapeDtypeStruct(shape, jnp.bfloat16),
        scratch_shapes=[
            pltpu.VMEM((rows, 128), jnp.float32),
            pltpu.VMEM(shape, jnp.float32),
        ],
        compiler_params=pltpu.CompilerParams(vmem_limit_bytes=24 << 20),
    )(own, oth)


def attention(query_vectors, key_vectors, value_vectors, weight_head, work, inputs):
    packed = pack(query_vectors, key_vectors, value_vectors)
    packed, inputs = lax.optimization_barrier((packed, inputs))
    work = work(*inputs)
    heads, tokens = packed.shape[:2]
    moved = lax.all_to_all(packed, HEAD, split_axis=0, concat_axis=0, tiled=True)
    moved, work = lax.optimization_barrier((moved, work))
    moved = moved.reshape(heads * tokens, 3 * HEAD_DIM)
    swap = [(0, 1), (1, 0)]
    right = [(i, (i + 1) % 4) for i in range(4)]
    left = [((i + 1) % 4, i) for i in range(4)]
    mid = moved.shape[0] // 2
    a, b = moved[:mid, :256], moved[mid:, :256]
    left_a = lax.ppermute(a, "y", right)
    right_b = lax.ppermute(b, "y", left)
    q_oth = lax.ppermute(moved[:, 256:], "core", swap)
    state = flash(moved, q_oth, [moved])
    left_b = lax.ppermute(b, "y", right)
    right_a = lax.ppermute(a, "y", left)
    state, left_a, right_b = lax.optimization_barrier((state, left_a, right_b))
    state = flash(moved, q_oth, [left_a, right_b], state)
    far_a = lax.ppermute(left_a, "y", right)
    far_b = lax.ppermute(right_b, "y", left)
    state = flash(moved, q_oth, [left_b, right_a], state)
    head = lax.axis_index(HEAD)
    weight = lax.dynamic_slice_in_dim(weight_head, head * HEAD_DIM, HEAD_DIM, axis=0)
    weight = jnp.pad(weight, ((0, 0), (0, 64)))
    own, oth = flash(moved, q_oth, [far_a, far_b], state, weight)
    oth = lax.ppermute(oth, "core", swap)
    partial = merge(own, oth).reshape(heads, 32, 128)
    parts = lax.all_to_all(partial, HEAD, split_axis=0, concat_axis=0, tiled=True)
    return jnp.sum(parts.astype(jnp.float32), axis=0), work


def shards(
    query_vectors,
    key_vectors,
    value_vectors,
    weight_head,
    noisy_latent,
    noise_level,
    latent_mean,
    latent_scale,
    cache_in,
    weight_in,
    bias_in,
    norm_gain,
    cache_mid,
    weight_mid,
    bias_mid,
):
    def work(noisy, cache_first, cache_second, weight_first):
        row, col = lax.axis_index(SEQ), lax.axis_index(BLK)
        last_row, last_col = lax.axis_size(SEQ) - 1, lax.axis_size(BLK) - 1
        beyond = jnp.stack([row > 0, row < last_row, col > 0, col < last_col])
        level = jnp.broadcast_to(noise_level, (4 * LAT,))
        affine = jnp.stack([level, jnp.tile(latent_scale, 4), jnp.tile(latent_mean, 4)])
        halos = input_halos(noisy, cache_first, cache_second)
        return (*halos, beyond.astype(jnp.int32), affine, window_weights(weight_first))

    mine, work = attention(
        query_vectors,
        key_vectors,
        value_vectors,
        weight_head,
        work,
        (noisy_latent, cache_in, cache_mid, weight_in),
    )
    cells, cache_second, beyond, affine, weight_first = work

    above = lax.ppermute(mine[16:], SEQ, along(SEQ, 1))
    below = lax.ppermute(mine[:16], SEQ, along(SEQ, -1))
    return tail(
        above,
        mine,
        below,
        cells,
        affine,
        beyond,
        weight_first,
        bias_in.reshape(1, C1),
        norm_gain.reshape(1, C1),
        cache_second,
        weight_mid.reshape(9, 3 * C1, C1),
        bias_mid.reshape(1, C1),
    )


def solution(mesh):
    inner = Mesh(mesh.devices.reshape(4, 4, 2, 2, 4), SHARD)
    tokens, tile = P(SHARD, None), P(None, SEQ, BLK, None)
    in_specs = (
        tokens,
        tokens,
        tokens,
        P(),
        tile,
        P(),
        P(),
        P(),
        tile,
        P(),
        P(),
        P(),
        tile,
        P(),
        P(),
    )
    return jax.shard_map(
        shards, mesh=inner, in_specs=in_specs, out_specs=(tile, tile), check_vma=False
    )
```

```python
import functools
import math

import jax
import jax.numpy as jnp
from jax import lax
from jax.experimental import pallas as pl
from jax.experimental.pallas import tpu as pltpu
from jax.sharding import Mesh
from jax.sharding import PartitionSpec as P

HEAD_DIM = 128
LAT = 16
C1 = 384
F = 4
EPSILON = 1e-06

SEQ = ("y", "zh", "core")
BLK = ("zl", "x")
HEAD = ("zh", "zl", "x")
SHARD = SEQ + BLK

TILE = 512
SUB = 256
CHUNK = 768
NT = (((1,), (1,)), ((), ()))


def lane_max(s):
    t = s[:, :128]
    for j in range(1, s.shape[1] // 128):
        t = jnp.maximum(t, s[:, j * 128 : (j + 1) * 128])
    return jnp.max(t, axis=1, keepdims=True)


def flash_kernel(first, last, n_kv, half, *refs):
    q_ref, refs = refs[0], refs[1:]
    if not last:
        qx_ref, refs = refs[0], refs[1:]
    kv_refs, refs = refs[:n_kv], refs[n_kv:]
    if not first:
        st_ref, refs = refs[0], refs[1:]
    if last:
        w_ref, u_ref = refs
        query = q_ref[...]
    else:
        (so_ref,) = refs
        query = jnp.where(pl.program_id(0) < half, q_ref[...], qx_ref[...])
    scale = math.log2(math.e) / math.sqrt(HEAD_DIM)
    qf = query.astype(jnp.float32) * scale
    q_hi = qf.astype(jnp.bfloat16)
    q_lo = (qf - q_hi.astype(jnp.float32)).astype(jnp.bfloat16)
    q = jnp.concatenate([q_hi, q_lo], axis=1)
    subs = TILE // SUB
    tops, accs = [], []
    for r in range(subs):
        if first:
            tops.append(jnp.full((SUB, 128), -1e30, jnp.float32))
            accs.append(jnp.zeros((SUB, 256), jnp.float32))
        else:
            st = st_ref[pl.ds(r * SUB, SUB), :]
            acc_l = st[:, 128:]
            lane = lax.broadcasted_iota(jnp.int32, (SUB, 128), 1)
            total = jnp.max(jnp.where(lane < 64, acc_l, -1e30), axis=1, keepdims=True)
            top = jnp.max(jnp.where(lane < 64, -1e30, acc_l), axis=1, keepdims=True)
            tops.append(jnp.broadcast_to(top, (SUB, 128)))
            accs.append(
                jnp.concatenate([st[:, :128], jnp.broadcast_to(total, (SUB, 128))], axis=1)
            )
    items = [
        (r, b, c)
        for b in range(n_kv)
        for c in range(kv_refs[b].shape[0] // CHUNK)
        for r in range(subs)
    ]
    ones = jnp.ones((CHUNK, 128), jnp.bfloat16)

    def score(item):
        r, b, c = item
        k = kv_refs[b][pl.ds(c * CHUNK, CHUNK), :128]
        return lax.dot_general(
            q[r * SUB : (r + 1) * SUB],
            jnp.concatenate([k, k], axis=1),
            NT,
            preferred_element_type=jnp.float32,
        )

    s = score(items[0])
    for n, (r, b, c) in enumerate(items):
        following = score(items[n + 1]) if n + 1 < len(items) else None
        top = jnp.maximum(tops[r], lane_max(s))
        p = jnp.exp2(s - top[:, :1]).astype(jnp.bfloat16)
        fade = jnp.exp2(tops[r] - top)
        v = jnp.concatenate([kv_refs[b][pl.ds(c * CHUNK, CHUNK), 128:], ones], axis=1)
        accs[r] = accs[r] * jnp.concatenate([fade, fade], axis=1) + jnp.dot(
            p, v, preferred_element_type=jnp.float32
        )
        tops[r] = top
        s = following
    lane = lax.broadcasted_iota(jnp.int32, (SUB, 128), 1)
    for r in range(subs):
        if last:
            total = accs[r][:, 128:]
            mixed = (accs[r][:, :128] / total).astype(jnp.bfloat16)
            u = jnp.dot(mixed, w_ref[...], preferred_element_type=jnp.float32)
            u_ref[pl.ds(r * SUB, SUB), :] = jnp.where(lane < 64, u, tops[r] + jnp.log2(total))
        else:
            so_ref[pl.ds(r * SUB, SUB), :] = jnp.concatenate(
                [accs[r][:, :128], jnp.where(lane < 64, accs[r][:, 128:], tops[r])], axis=1
            )


def flash(q_own, q_oth, kvs, state=None):
    rows = q_oth.shape[0]
    half = rows // TILE
    keys = sum(kv.shape[0] for kv in kvs)
    in_specs = [
        pl.BlockSpec((TILE, 128), lambda i: (jnp.minimum(i, half - 1), 2)),
        pl.BlockSpec((TILE, 128), lambda i: (jnp.maximum(i - half, 0), 0)),
    ]
    in_specs += [pl.BlockSpec((kv.shape[0], 256), lambda i: (0, 0)) for kv in kvs]
    args = [q_own, q_oth, *kvs]
    if state is not None:
        in_specs.append(pl.BlockSpec((TILE, 256), lambda i: (i, 0)))
        args.append(state)
    return pl.pallas_call(
        functools.partial(flash_kernel, state is None, False, len(kvs), half),
        grid=(2 * half,),
        in_specs=in_specs,
        out_specs=pl.BlockSpec((TILE, 256), lambda i: (i, 0)),
        out_shape=jax.ShapeDtypeStruct((2 * rows, 256), jnp.float32),
        compiler_params=pltpu.CompilerParams(vmem_limit_bytes=20 << 20),
        cost_estimate=flash_cost(2 * rows, keys),
    )(*args)


def flash_last(query, lane_block, kvs, state, half_at, weight):
    rows = query.shape[0]
    half = rows // TILE
    keys = sum(kv.shape[0] for kv in kvs)
    in_specs = [pl.BlockSpec((TILE, 128), lambda i: (i, lane_block))]
    in_specs += [pl.BlockSpec((kv.shape[0], 256), lambda i: (0, 0)) for kv in kvs]
    in_specs += [
        pl.BlockSpec((TILE, 256), lambda i: (i + half_at * half, 0)),
        pl.BlockSpec(weight.shape, lambda i: (0, 0)),
    ]
    return pl.pallas_call(
        functools.partial(flash_kernel, False, True, len(kvs), half),
        grid=(half,),
        in_specs=in_specs,
        out_specs=pl.BlockSpec((TILE, 128), lambda i: (i, 0)),
        out_shape=jax.ShapeDtypeStruct((rows, 128), jnp.float32),
        compiler_params=pltpu.CompilerParams(vmem_limit_bytes=20 << 20),
        cost_estimate=flash_cost(rows, keys),
    )(query, *kvs, state, weight)


def flash_cost(rows, keys):
    return pl.CostEstimate(
        flops=rows * keys * 1024, bytes_accessed=rows * 2048, transcendentals=rows * keys
    )


def inside(at, low, high, before, after):
    return ((at > low) | before) & ((at < high) | after)


def tail_kernel(
    near_ref,
    mine_ref,
    apart_ref,
    cells_ref,
    affine_ref,
    beyond_ref,
    w1_ref,
    b1_ref,
    gain_ref,
    mid_ref,
    w2_ref,
    b2_ref,
    den_ref,
    out_ref,
    vel,
    lat,
    den,
    first,
    act,
    wide,
    done,
):
    even = beyond_ref[4] > 0
    above = jnp.where(even, apart_ref[...], near_ref[...])
    below = jnp.where(even, near_ref[...], apart_ref[...])
    for at, rows in enumerate((above, mine_ref[0:16, :], mine_ref[16:32, :], below)):
        turned = pltpu.roll(rows, 64, axis=1)
        for f in range(F):
            vel[f, at, 0:4, :] = rows[f * 4 : f * 4 + 4]
            vel[f, at, 4:8, :] = turned[f * 4 : f * 4 + 4]
    level, scale, mean = affine_ref[0:1, :], affine_ref[1:2, :], affine_ref[2:3, :]
    denoised = cells_ref[2:6, :, :, 0:64] - level * vel[:, :, :, 0:64]
    up, down, before, after = (beyond_ref[k] > 0 for k in range(4))
    row = lax.broadcasted_iota(jnp.int32, denoised.shape, 1)
    col = lax.broadcasted_iota(jnp.int32, denoised.shape, 2)
    kept = inside(row, 0, 3, up, down) & inside(col, 0, 7, before, after)
    latent = jnp.where(kept, denoised * scale + mean, 0.0)
    for k in range(4):
        part = jnp.concatenate([denoised, denoised], axis=3).reshape(F * 32, 128)
        part = pltpu.roll(part, 128 - LAT * k, axis=1) if k else part
        part = part.reshape(F, 4, 8, 128)
        for f in range(F):
            for r in range(2):
                rows = pl.ds(8 * (k % 2) + 2 * r + k // 2, 8, stride=16)
                den[f, rows, :] = part[f, r + 1]
    den_ref[...] = den[:, 16:112, :].reshape(F, 12, 8, 128)[:, :, 0:4, 0:LAT]
    lat[...] = jnp.zeros(lat.shape, jnp.float32)
    lat[0:2, :, 0:8, 0:64] = cells_ref[0:2, :, :, 0:64]
    lat[2:6, :, 0:8, 0:64] = latent.astype(jnp.bfloat16).astype(jnp.float32)
    here = lat[:, :, 0:8, :].reshape(192, 128)
    right = pltpu.roll(lat[:, :, 1:9, :].reshape(192, 128), 64, axis=1)
    lane = lax.broadcasted_iota(jnp.int32, (192, 128), 1)
    pair = jnp.where(lane < 64, here, right).reshape(6, 4, 8, 128)
    lower = jnp.concatenate([pair[:, 1:4], pair[:, 3:4]], axis=1)
    window = jnp.concatenate([pair, lower], axis=3).reshape(192, 256).astype(jnp.bfloat16)
    parts = C1 // 128
    for k in range(parts):
        act[k, 0:2, :, 0:16, :] = mid_ref[:, :, :, pl.ds(k * 128, 128)]
    gain = gain_ref[...]
    for p in range(2):
        for q in range(2):
            lanes = pl.ds((2 * p + q) * C1, C1)
            value = b1_ref[...]
            for t in range(3):
                value = value + jnp.dot(
                    window[t * 32 : t * 32 + 128],
                    w1_ref[t, :, lanes],
                    preferred_element_type=jnp.float32,
                )
            power = jnp.mean(value * value, axis=1, keepdims=True)
            normed = value * lax.rsqrt(power + EPSILON) * gain
            active = (normed / (1.0 + jnp.exp(-normed))).reshape(F, 32, C1)
            at = lax.broadcasted_iota(jnp.int32, (32, C1), 0)
            kept = inside(2 * (at // 8) + p, 0, 5, up, down)
            kept = kept & inside(2 * (at % 8) + q, 0, 13, before, after)
            active = jnp.where(kept, active, 0.0)
            value = value.reshape(F, 4, 8, C1)
            active = active.reshape(F, 4, 8, C1)
            for r in range(3):
                cols = pl.ds(q, 8, stride=2)
                for k in range(parts):
                    part = slice(k * 128, k * 128 + 128)
                    for f in range(F):
                        first[k, f, 2 * r + p, cols, :] = value[f, r, :, part]
                        act[k, f + 2, 2 * r + p, cols, :] = active[f, r, :, part]
    for v in range(3):
        for k in range(parts):
            wide[:, :, :, pl.ds(v * C1 + k * 128, 128)] = act[k, :, :, pl.ds(v, 16), :].astype(
                jnp.bfloat16
            )
    middle = [first[k, :, 1:5, pl.ds(1, 16), :].reshape(256, 128) for k in range(parts)]
    total = jnp.concatenate(middle, axis=1) + b2_ref[...]
    for tap in range(9):
        t, u = divmod(tap, 3)
        rows = wide[t : t + 4, u : u + 4].reshape(256, 3 * C1)
        total = total + jnp.dot(rows, w2_ref[tap], preferred_element_type=jnp.float32)
    for k in range(parts):
        for f in range(F):
            for i in range(4):
                at = f * 64 + i * 16
                done[k, f, pl.ds(i, 16, stride=8), :] = total[at : at + 16, k * 128 : k * 128 + 128]
        cells = done[k, :, 0:96, :].reshape(F, 12, 8, 128)[:, :, 0:4]
        out_ref[:, :, :, pl.ds(k * 128, 128)] = cells.astype(jnp.bfloat16)


def tail(*args):
    specs = [pl.BlockSpec(memory_space=pltpu.VMEM)] * len(args)
    specs[5] = pl.BlockSpec(memory_space=pltpu.SMEM)
    return pl.pallas_call(
        tail_kernel,
        in_specs=specs,
        out_specs=[pl.BlockSpec(memory_space=pltpu.VMEM)] * 2,
        out_shape=[
            jax.ShapeDtypeStruct((F, 12, 4, LAT), jnp.float32),
            jax.ShapeDtypeStruct((F, 12, 4, C1), jnp.bfloat16),
        ],
        scratch_shapes=[
            pltpu.VMEM((F, 4, 8, 128), jnp.float32),
            pltpu.VMEM((6, 4, 16, 128), jnp.float32),
            pltpu.VMEM((F, 128, 128), jnp.float32),
            pltpu.VMEM((C1 // 128, F, 6, 24, 128), jnp.float32),
            pltpu.VMEM((C1 // 128, 6, 6, 24, 128), jnp.float32),
            pltpu.VMEM((6, 6, 16, 3 * C1), jnp.bfloat16),
            pltpu.VMEM((C1 // 128, F, 128, 128), jnp.float32),
        ],
        compiler_params=pltpu.CompilerParams(vmem_limit_bytes=32 << 20),
    )(*args)


def window_kernel(w_ref, out_ref):
    out_ref[...] = jnp.zeros(out_ref.shape, out_ref.dtype)
    for t in range(3):
        for u in range(3):
            for v in range(3):
                taps = w_ref[t, u, v]
                for p in range(2):
                    for q in range(2):
                        (dr, a), (dc, b) = divmod(p + u, 2), divmod(q + v, 2)
                        at = dr * 128 + dc * 64 + a * 32 + b * 16
                        out_ref[t, pl.ds(at, LAT), pl.ds((2 * p + q) * C1, C1)] = taps


def window_weights(weight):
    return pl.pallas_call(
        window_kernel,
        out_shape=jax.ShapeDtypeStruct((3, 16 * LAT, 4 * C1), jnp.bfloat16),
        compiler_params=pltpu.CompilerParams(vmem_limit_bytes=16 << 20),
    )(weight)


def put_frames(ref, rows, tokens):
    count = tokens[0].shape[0]
    low = lax.broadcasted_iota(jnp.int32, (count, 128), 1) < 64
    for i in range(2):
        for h in range(2):
            one = tokens[i + 2 * h]
            two = pltpu.roll(tokens[i + 4], 64, axis=1) if h == 0 else jnp.zeros_like(one)
            ref[i, pl.ds(rows + h * count, count), 384:512] = jnp.where(low, one, two)


def get_frames(ref, rows, count):
    out = {}
    for i in range(2):
        for h in range(2):
            both = ref[i, pl.ds(rows + h * count, count), 384:512]
            out[i + 2 * h] = both
            if h == 0:
                out[i + 4] = pltpu.roll(both, 64, axis=1)
    return [out[f] for f in range(6)]


def edge_rows_kernel(noisy_ref, cache_ref, mid_ref, tok_ref, down_ref, up_ref, cells):
    cells[...] = jnp.zeros(cells.shape, jnp.float32)
    cells[0:2, :, 0:12, 0:LAT] = cache_ref[...].astype(jnp.float32)
    cells[2:6, :, 0:12, 0:LAT] = noisy_ref[...]
    lane = lax.broadcasted_iota(jnp.int32, (8, 128), 1)
    tokens = {}
    for r in range(2):
        for f in range(6):
            token = jnp.zeros((8, 128), jnp.float32)
            for k in range(4):
                part = cells[f, 2 * r + k // 2, pl.ds(k % 2, 8, stride=2), :]
                part = pltpu.roll(part, LAT * k, axis=1) if k else part
                token = jnp.where((lane >= LAT * k) & (lane < LAT * k + LAT), part, token)
            tok_ref[f, r] = token
            tokens[f, r] = token
    for ref, row, r in ((down_ref, 3, 1), (up_ref, 0, 0)):
        ref[...] = jnp.zeros(ref.shape, jnp.float32)
        ref[:, 0:12, 0:C1] = mid_ref[:, row].astype(jnp.float32)
        put_frames(ref, 0, [tokens[f, r] for f in range(6)])


def edge_cols_kernel(tok_ref, mid_ref, above_ref, below_ref, toks, mids, right_ref, left_ref):
    above, below = get_frames(above_ref, 0, 8), get_frames(below_ref, 0, 8)
    for f in range(6):
        toks[f, 0] = above[f]
        toks[f, 1] = tok_ref[f, 0]
        toks[f, 2] = tok_ref[f, 1]
        toks[f, 3] = below[f]
    mids[...] = jnp.zeros(mids.shape, jnp.float32)
    mids[:, 0, 0:12, :] = above_ref[:, 0:12, 0:C1]
    mids[:, 1:5, 0:12, :] = mid_ref[...].astype(jnp.float32)
    mids[:, 5, 0:12, :] = below_ref[:, 0:12, 0:C1]
    for ref, token, col in ((right_ref, 5, 11), (left_ref, 0, 0)):
        ref[...] = jnp.zeros(ref.shape, jnp.float32)
        for i in range(2):
            for row in range(6):
                ref[i, pl.ds(row, 1), 0:C1] = mids[i, row, pl.ds(col, 1), :]
        for r in range(4):
            put_rows(ref, r, [toks[f, r, pl.ds(token, 1), :] for f in range(6)])


def put_rows(ref, r, tokens):
    low = lax.broadcasted_iota(jnp.int32, (1, 128), 1) < 64
    for i in range(2):
        for h in range(2):
            one = tokens[i + 2 * h]
            two = pltpu.roll(tokens[i + 4], 64, axis=1) if h == 0 else jnp.zeros_like(one)
            ref[i, pl.ds(4 * h + r, 1), 384:512] = jnp.where(low, one, two)


def place_kernel(toks, mids, left_ref, right_ref, cells_ref, cache_ref):
    cells_ref[...] = jnp.zeros(cells_ref.shape, jnp.float32)
    cache_ref[...] = jnp.zeros(cache_ref.shape, jnp.float32)
    for f in range(6):
        for r in range(4):
            cells_ref[f, r, 1:7, :] = toks[f, r, 0:6, :]
    cache_ref[:, :, 1:13, :] = mids[:, :, 0:12, :]
    for ref, token, col in ((left_ref, 0, 0), (right_ref, 7, 13)):
        frames = get_frames(ref, 0, 4)
        for f in range(6):
            for r in range(4):
                cells_ref[f, r, pl.ds(token, 1), :] = frames[f][r : r + 1]
        for i in range(2):
            for row in range(6):
                cache_ref[i, row, pl.ds(col, 1), :] = ref[i, pl.ds(row, 1), 0:C1]


def small_call(kernel, shapes, scratch=()):
    return pl.pallas_call(
        kernel,
        out_shape=[jax.ShapeDtypeStruct(shape, jnp.float32) for shape in shapes],
        scratch_shapes=[pltpu.VMEM(shape, jnp.float32) for shape in scratch],
        compiler_params=pltpu.CompilerParams(vmem_limit_bytes=8 << 20),
    )


def along(axis, step):
    count = lax.axis_size(axis)
    return [(i, i + step) for i in range(count) if 0 <= i + step < count]


def input_halos(noisy, cache_in, cache_mid):
    edge = (2, 16, 512)
    toks, down, up = small_call(
        edge_rows_kernel, [(6, 2, 8, 128), edge, edge], [(6, 4, 16, 128)]
    )(noisy, cache_in, cache_mid)
    above = lax.ppermute(down, SEQ, along(SEQ, 1))
    below = lax.ppermute(up, SEQ, along(SEQ, -1))
    side = (2, 8, 512)
    toks, mids, right, left = small_call(
        edge_cols_kernel, [(6, 4, 8, 128), (2, 6, 16, C1), side, side]
    )(toks, cache_mid, above, below)
    before = lax.ppermute(right, BLK, along(BLK, 1))
    after = lax.ppermute(left, BLK, along(BLK, -1))
    return small_call(place_kernel, [(6, 4, 8, 128), (2, 6, 16, C1)])(toks, mids, before, after)


def pack_kernel(q_ref, k_ref, v_ref, out_ref):
    for h in range(out_ref.shape[0]):
        lanes = pl.ds(h * HEAD_DIM, HEAD_DIM)
        out_ref[h, :, 0:128] = k_ref[:, lanes]
        out_ref[h, :, 128:256] = v_ref[:, lanes]
        out_ref[h, :, 256:384] = q_ref[:, lanes]


def pack(query_vectors, key_vectors, value_vectors):
    tokens, width = query_vectors.shape
    heads = width // HEAD_DIM
    block = pl.BlockSpec((tokens, width // 2), lambda i: (0, i))
    return pl.pallas_call(
        pack_kernel,
        grid=(2,),
        in_specs=[block] * 3,
        out_specs=pl.BlockSpec((heads // 2, tokens, 3 * HEAD_DIM), lambda i: (i, 0, 0)),
        out_shape=jax.ShapeDtypeStruct((heads, tokens, 3 * HEAD_DIM), jnp.bfloat16),
    )(query_vectors, key_vectors, value_vectors)


def merge_kernel(own_ref, oth_ref, out_ref, vel_ref, piece_ref):
    own, oth = own_ref[...], oth_ref[...]
    gap = pltpu.roll(oth - own, 64, axis=1)
    share = 1.0 / (1.0 + jnp.exp2(gap))
    vel = own * share + oth * (1.0 - share)
    lane = lax.broadcasted_iota(jnp.int32, vel.shape, 1)
    vel_ref[...] = jnp.where(lane < 64, vel, pltpu.roll(vel, 64, axis=1))
    low = lax.broadcasted_iota(jnp.int32, (16, 128), 1) < 64
    zero = jnp.zeros((16, 128), jnp.float32)

    def column(r, at):
        if at < 0 or at >= 48:
            return zero
        return vel_ref[pl.ds(r * 48 + at, 16, stride=96), :]

    for b in range(8):
        for r in range(2):
            for c in range(4):
                at = 6 * b - 1 + c
                both = jnp.where(low, column(r, at), column(r, at + 4))
                for y in range(4):
                    piece_ref[y, b, pl.ds(r * 16 + c, 4, stride=4), :] = both[y * 4 : y * 4 + 4]
    out_ref[...] = piece_ref[...].astype(jnp.bfloat16)


def merge(own, oth):
    rows = own.shape[0]
    whole = pl.BlockSpec((rows, 128), lambda: (0, 0))
    shape = (4, 8, 32, 128)
    return pl.pallas_call(
        merge_kernel,
        in_specs=[whole, whole],
        out_specs=pl.BlockSpec(shape, lambda: (0, 0, 0, 0)),
        out_shape=jax.ShapeDtypeStruct(shape, jnp.bfloat16),
        scratch_shapes=[
            pltpu.VMEM((rows, 128), jnp.float32),
            pltpu.VMEM(shape, jnp.float32),
        ],
        compiler_params=pltpu.CompilerParams(vmem_limit_bytes=24 << 20),
    )(own, oth)


def attention(query_vectors, key_vectors, value_vectors, weight_head, work, inputs):
    packed = pack(query_vectors, key_vectors, value_vectors)
    packed, inputs = lax.optimization_barrier((packed, inputs))
    work = work(*inputs)
    heads, tokens = packed.shape[:2]
    moved = lax.all_to_all(packed, HEAD, split_axis=0, concat_axis=0, tiled=True)
    moved = moved.reshape(heads * tokens, 3 * HEAD_DIM)
    swap = [(0, 1), (1, 0)]
    right = [(i, (i + 1) % 4) for i in range(4)]
    left = [((i + 1) % 4, i) for i in range(4)]
    mid = moved.shape[0] // 2
    a, b, q_own = moved[:mid, :256], moved[mid:, :256], moved[:, 256:]
    (a, b, q_own), work = lax.optimization_barrier(((a, b, q_own), work))
    left_a = lax.ppermute(a, "y", right)
    right_b = lax.ppermute(b, "y", left)
    q_oth = lax.ppermute(q_own, "core", swap)
    state = flash(moved, q_oth, [moved])
    state, a, b = lax.optimization_barrier((state, a, b))
    left_b = lax.ppermute(b, "y", right)
    right_a = lax.ppermute(a, "y", left)
    state = flash(moved, q_oth, [left_a, right_b], state)
    state, left_a, right_b = lax.optimization_barrier((state, left_a, right_b))
    far = [lax.ppermute(left_a, "y", right), lax.ppermute(right_b, "y", left)]
    state = flash(moved, q_oth, [left_b, right_a], state)
    head = lax.axis_index(HEAD)
    weight = lax.dynamic_slice_in_dim(weight_head, head * HEAD_DIM, HEAD_DIM, axis=0)
    weight = jnp.pad(weight, ((0, 0), (0, 64)))
    oth = flash_last(q_oth, 0, far, state, 1, weight)
    oth, state = lax.optimization_barrier((oth, state))
    oth = lax.ppermute(oth, "core", swap)
    own = flash_last(moved, 2, far, state, 0, weight)
    partial = merge(own, oth).reshape(heads, 32, 128)
    parts = lax.all_to_all(partial, HEAD, split_axis=0, concat_axis=0, tiled=True)
    return jnp.sum(parts.astype(jnp.float32), axis=0), work


def shards(
    query_vectors,
    key_vectors,
    value_vectors,
    weight_head,
    noisy_latent,
    noise_level,
    latent_mean,
    latent_scale,
    cache_in,
    weight_in,
    bias_in,
    norm_gain,
    cache_mid,
    weight_mid,
    bias_mid,
):
    def work(noisy, cache_first, cache_second, weight_first):
        row, col = lax.axis_index(SEQ), lax.axis_index(BLK)
        last_row, last_col = lax.axis_size(SEQ) - 1, lax.axis_size(BLK) - 1
        even = lax.axis_index("core") == 0
        beyond = jnp.stack([row > 0, row < last_row, col > 0, col < last_col, even])
        level = jnp.broadcast_to(noise_level, (4 * LAT,))
        affine = jnp.stack([level, jnp.tile(latent_scale, 4), jnp.tile(latent_mean, 4)])
        halos = input_halos(noisy, cache_first, cache_second)
        return (*halos, beyond.astype(jnp.int32), affine, window_weights(weight_first))

    mine, work = attention(
        query_vectors,
        key_vectors,
        value_vectors,
        weight_head,
        work,
        (noisy_latent, cache_in, cache_mid, weight_in),
    )
    cells, cache_second, beyond, affine, weight_first = work

    count = lax.axis_size(SEQ)
    even = lax.axis_index("core") == 0
    low, high = mine[:16], mine[16:]
    near = lax.ppermute(jnp.where(even, high, low), SEQ, [(i, i ^ 1) for i in range(count)])
    pairs = [(i, i + 1) for i in range(1, count - 1, 2)]
    pairs += [(j, i) for i, j in pairs]
    apart = lax.ppermute(jnp.where(even, low, high), SEQ, pairs)
    denoised, features = tail(
        near,
        mine,
        apart,
        cells,
        affine,
        beyond,
        weight_first,
        bias_in.reshape(1, C1),
        norm_gain.reshape(1, C1),
        cache_second,
        weight_mid.reshape(9, 3 * C1, C1),
        bias_mid.reshape(1, C1),
    )
    return denoised.transpose(0, 2, 1, 3), features.transpose(0, 2, 1, 3)


def solution(mesh):
    inner = Mesh(mesh.devices.reshape(4, 4, 2, 2, 4), SHARD)
    tokens, tile = P(SHARD, None), P(None, SEQ, BLK, None)
    in_specs = (
        tokens,
        tokens,
        tokens,
        P(),
        tile,
        P(),
        P(),
        P(),
        tile,
        P(),
        P(),
        P(),
        tile,
        P(),
        P(),
    )
    return jax.shard_map(
        shards, mesh=inner, in_specs=in_specs, out_specs=(tile, tile), check_vma=False
    )
```

```python
import functools
import math

import jax
import jax.numpy as jnp
from jax import lax
from jax.experimental import pallas as pl
from jax.experimental.pallas import tpu as pltpu
from jax.sharding import Mesh
from jax.sharding import PartitionSpec as P

HEAD_DIM = 128
LAT = 16
C1 = 384
F = 4
EPSILON = 1e-06

SEQ = ("y", "zh", "core")
BLK = ("zl", "x")
HEAD = ("zh", "zl", "x")
SHARD = SEQ + BLK

TILE = 512
SUB = 256
CHUNK = 768
NT = (((1,), (1,)), ((), ()))


def mesh_index(axes):
    index = 0
    for axis in axes:
        index = index * lax.axis_size(axis) + lax.axis_index(axis)
    return index


def lane_max(s):
    t = s[:, :128]
    for j in range(1, s.shape[1] // 128):
        t = jnp.maximum(t, s[:, j * 128 : (j + 1) * 128])
    return jnp.max(t, axis=1, keepdims=True)


def flash_kernel(first, last, n_kv, half, *refs):
    q_ref, refs = refs[0], refs[1:]
    if not last:
        qx_ref, refs = refs[0], refs[1:]
    kv_refs, refs = refs[:n_kv], refs[n_kv:]
    if not first:
        st_ref, refs = refs[0], refs[1:]
    if last:
        w_ref, u_ref = refs
        query = q_ref[...]
        own = w_ref[:, pl.ds(pl.multiple_of(mesh_index(HEAD) * HEAD_DIM, HEAD_DIM), HEAD_DIM)]
        weight = jnp.concatenate([own, jnp.zeros_like(own)], axis=0)
    else:
        (so_ref,) = refs
        query = jnp.where(pl.program_id(0) < half, q_ref[...], qx_ref[...])
    scale = math.log2(math.e) / math.sqrt(HEAD_DIM)
    qf = query.astype(jnp.float32) * scale
    q_hi = qf.astype(jnp.bfloat16)
    q_lo = (qf - q_hi.astype(jnp.float32)).astype(jnp.bfloat16)
    q = jnp.concatenate([q_hi, q_lo], axis=1)
    subs = TILE // SUB
    tops, accs = [], []
    for r in range(subs):
        if first:
            tops.append(jnp.full((SUB, 128), -1e30, jnp.float32))
            accs.append(jnp.zeros((SUB, 256), jnp.float32))
        else:
            st = st_ref[pl.ds(r * SUB, SUB), :]
            acc_l = st[:, 128:]
            lane = lax.broadcasted_iota(jnp.int32, (SUB, 128), 1)
            total = jnp.max(jnp.where(lane < 64, acc_l, -1e30), axis=1, keepdims=True)
            top = jnp.max(jnp.where(lane < 64, -1e30, acc_l), axis=1, keepdims=True)
            tops.append(jnp.broadcast_to(top, (SUB, 128)))
            accs.append(
                jnp.concatenate([st[:, :128], jnp.broadcast_to(total, (SUB, 128))], axis=1)
            )
    items = [
        (r, b, c)
        for b in range(n_kv)
        for c in range(kv_refs[b].shape[0] // CHUNK)
        for r in range(subs)
    ]
    ones = jnp.ones((CHUNK, 128), jnp.bfloat16)

    def score(item):
        r, b, c = item
        k = kv_refs[b][pl.ds(c * CHUNK, CHUNK), :128]
        return lax.dot_general(
            q[r * SUB : (r + 1) * SUB],
            jnp.concatenate([k, k], axis=1),
            NT,
            preferred_element_type=jnp.float32,
        )

    s = score(items[0])
    for n, (r, b, c) in enumerate(items):
        following = score(items[n + 1]) if n + 1 < len(items) else None
        top = jnp.maximum(tops[r], lane_max(s))
        p = jnp.exp2(s - top[:, :1]).astype(jnp.bfloat16)
        fade = jnp.exp2(tops[r] - top)
        v = jnp.concatenate([kv_refs[b][pl.ds(c * CHUNK, CHUNK), 128:], ones], axis=1)
        accs[r] = accs[r] * jnp.concatenate([fade, fade], axis=1) + jnp.dot(
            p, v, preferred_element_type=jnp.float32
        )
        tops[r] = top
        s = following
    lane = lax.broadcasted_iota(jnp.int32, (SUB, 128), 1)
    for r in range(subs):
        if last:
            total = accs[r][:, 128:]
            mixed = (accs[r][:, :128] / total).astype(jnp.bfloat16)
            u = lax.dot_general(mixed, weight, NT, preferred_element_type=jnp.float32)
            u_ref[pl.ds(r * SUB, SUB), :] = jnp.where(lane < 64, u, tops[r] + jnp.log2(total))
        else:
            so_ref[pl.ds(r * SUB, SUB), :] = jnp.concatenate(
                [accs[r][:, :128], jnp.where(lane < 64, accs[r][:, 128:], tops[r])], axis=1
            )


def flash(q_own, q_oth, kvs, state=None):
    rows = q_oth.shape[0]
    half = rows // TILE
    keys = sum(kv.shape[0] for kv in kvs)
    in_specs = [
        pl.BlockSpec((TILE, 128), lambda i: (jnp.minimum(i, half - 1), 2)),
        pl.BlockSpec((TILE, 128), lambda i: (jnp.maximum(i - half, 0), 0)),
    ]
    in_specs += [pl.BlockSpec((kv.shape[0], 256), lambda i: (0, 0)) for kv in kvs]
    args = [q_own, q_oth, *kvs]
    if state is not None:
        in_specs.append(pl.BlockSpec((TILE, 256), lambda i: (i, 0)))
        args.append(state)
    return pl.pallas_call(
        functools.partial(flash_kernel, state is None, False, len(kvs), half),
        grid=(2 * half,),
        in_specs=in_specs,
        out_specs=pl.BlockSpec((TILE, 256), lambda i: (i, 0)),
        out_shape=jax.ShapeDtypeStruct((2 * rows, 256), jnp.float32),
        compiler_params=pltpu.CompilerParams(vmem_limit_bytes=20 << 20),
        cost_estimate=flash_cost(2 * rows, keys),
    )(*args)


def flash_last(query, lane_block, kvs, state, half_at, weight):
    rows = query.shape[0]
    half = rows // TILE
    keys = sum(kv.shape[0] for kv in kvs)
    in_specs = [pl.BlockSpec((TILE, 128), lambda i: (i, lane_block))]
    in_specs += [pl.BlockSpec((kv.shape[0], 256), lambda i: (0, 0)) for kv in kvs]
    in_specs += [
        pl.BlockSpec((TILE, 256), lambda i: (i + half_at * half, 0)),
        pl.BlockSpec(weight.shape, lambda i: (0, 0)),
    ]
    return pl.pallas_call(
        functools.partial(flash_kernel, False, True, len(kvs), half),
        grid=(half,),
        in_specs=in_specs,
        out_specs=pl.BlockSpec((TILE, 128), lambda i: (i, 0)),
        out_shape=jax.ShapeDtypeStruct((rows, 128), jnp.float32),
        compiler_params=pltpu.CompilerParams(vmem_limit_bytes=20 << 20),
        cost_estimate=flash_cost(rows, keys),
    )(query, *kvs, state, weight)


def flash_cost(rows, keys):
    return pl.CostEstimate(
        flops=rows * keys * 1024, bytes_accessed=rows * 2048, transcendentals=rows * keys
    )


def inside(at, low, high, before, after):
    return ((at > low) | before) & ((at < high) | after)


def tail_kernel(
    near_ref,
    mine_ref,
    apart_ref,
    cells_ref,
    level_ref,
    scale_ref,
    mean_ref,
    w1_ref,
    b1_ref,
    gain_ref,
    mid_ref,
    w2_ref,
    b2_ref,
    den_ref,
    out_ref,
    vel,
    lat,
    den,
    first,
    act,
    wide,
    done,
    vecs,
):
    even = lax.axis_index("core") == 0
    at_row, at_col = mesh_index(SEQ), mesh_index(BLK)
    up, down = at_row > 0, at_row < lax.axis_size(SEQ) - 1
    before, after = at_col > 0, at_col < lax.axis_size(BLK) - 1
    above = jnp.where(even, apart_ref[...], near_ref[...])
    below = jnp.where(even, near_ref[...], apart_ref[...])
    for at, rows in enumerate((above, mine_ref[0:16, :], mine_ref[16:32, :], below)):
        turned = pltpu.roll(rows, 64, axis=1)
        for f in range(F):
            vel[f, at, 0:4, :] = rows[f * 4 : f * 4 + 4]
            vel[f, at, 4:8, :] = turned[f * 4 : f * 4 + 4]
    vecs[...] = jnp.zeros(vecs.shape, jnp.float32)
    vecs[0:1, 0:LAT] = scale_ref[...].reshape(1, LAT)
    vecs[8:9, 0:LAT] = mean_ref[...].reshape(1, LAT)
    base = vecs[...]
    tiled = base + pltpu.roll(base, LAT, axis=1)
    tiled = tiled + pltpu.roll(tiled, 2 * LAT, axis=1)
    scale, mean = tiled[0:1, 0:64], tiled[8:9, 0:64]
    denoised = cells_ref[2:6, :, :, 0:64] - level_ref[0] * vel[:, :, :, 0:64]
    row = lax.broadcasted_iota(jnp.int32, denoised.shape, 1)
    col = lax.broadcasted_iota(jnp.int32, denoised.shape, 2)
    kept = inside(row, 0, 3, up, down) & inside(col, 0, 7, before, after)
    latent = jnp.where(kept, denoised * scale + mean, 0.0)
    for k in range(4):
        part = jnp.concatenate([denoised, denoised], axis=3).reshape(F * 32, 128)
        part = pltpu.roll(part, 128 - LAT * k, axis=1) if k else part
        part = part.reshape(F, 4, 8, 128)
        for f in range(F):
            for r in range(2):
                rows = pl.ds(8 * (k % 2) + 2 * r + k // 2, 8, stride=16)
                den[f, rows, :] = part[f, r + 1]
    den_ref[...] = den[:, 16:112, :].reshape(F, 12, 8, 128)[:, :, 0:4, 0:LAT]
    lat[...] = jnp.zeros(lat.shape, jnp.float32)
    lat[0:2, :, 0:8, 0:64] = cells_ref[0:2, :, :, 0:64]
    lat[2:6, :, 0:8, 0:64] = latent.astype(jnp.bfloat16).astype(jnp.float32)
    here = lat[:, :, 0:8, :].reshape(192, 128)
    right = pltpu.roll(lat[:, :, 1:9, :].reshape(192, 128), 64, axis=1)
    lane = lax.broadcasted_iota(jnp.int32, (192, 128), 1)
    pair = jnp.where(lane < 64, here, right).reshape(6, 4, 8, 128)
    lower = jnp.concatenate([pair[:, 1:4], pair[:, 3:4]], axis=1)
    window = jnp.concatenate([pair, lower], axis=3).reshape(192, 256).astype(jnp.bfloat16)
    parts = C1 // 128
    for k in range(parts):
        act[k, 0:2, :, 0:16, :] = mid_ref[:, :, :, pl.ds(k * 128, 128)]
    gain = gain_ref[...].reshape(1, C1)
    for p in range(2):
        for q in range(2):
            lanes = pl.ds((2 * p + q) * C1, C1)
            value = b1_ref[...].reshape(1, C1)
            for t in range(3):
                value = value + jnp.dot(
                    window[t * 32 : t * 32 + 128],
                    w1_ref[t, :, lanes],
                    preferred_element_type=jnp.float32,
                )
            power = jnp.mean(value * value, axis=1, keepdims=True)
            normed = value * lax.rsqrt(power + EPSILON) * gain
            active = (normed / (1.0 + jnp.exp(-normed))).reshape(F, 32, C1)
            at = lax.broadcasted_iota(jnp.int32, (32, C1), 0)
            kept = inside(2 * (at // 8) + p, 0, 5, up, down)
            kept = kept & inside(2 * (at % 8) + q, 0, 13, before, after)
            active = jnp.where(kept, active, 0.0)
            value = value.reshape(F, 4, 8, C1)
            active = active.reshape(F, 4, 8, C1)
            for r in range(3):
                cols = pl.ds(q, 8, stride=2)
                for k in range(parts):
                    part = slice(k * 128, k * 128 + 128)
                    for f in range(F):
                        first[k, f, 2 * r + p, cols, :] = value[f, r, :, part]
                        act[k, f + 2, 2 * r + p, cols, :] = active[f, r, :, part]
    for v in range(3):
        for k in range(parts):
            wide[:, :, :, pl.ds(v * C1 + k * 128, 128)] = act[k, :, :, pl.ds(v, 16), :].astype(
                jnp.bfloat16
            )
    middle = [first[k, :, 1:5, pl.ds(1, 16), :].reshape(256, 128) for k in range(parts)]
    total = jnp.concatenate(middle, axis=1) + b2_ref[...].reshape(1, C1)
    for tap in range(9):
        t, u = divmod(tap, 3)
        rows = wide[t : t + 4, u : u + 4].reshape(256, 3 * C1)
        total = total + jnp.dot(rows, w2_ref[tap], preferred_element_type=jnp.float32)
    for k in range(parts):
        for f in range(F):
            for i in range(4):
                at = f * 64 + i * 16
                done[k, f, pl.ds(i, 16, stride=8), :] = total[at : at + 16, k * 128 : k * 128 + 128]
        cells = done[k, :, 0:96, :].reshape(F, 12, 8, 128)[:, :, 0:4]
        out_ref[:, :, :, pl.ds(k * 128, 128)] = cells.astype(jnp.bfloat16)


def tail(*args):
    specs = [pl.BlockSpec(memory_space=pltpu.VMEM)] * len(args)
    specs[4] = pl.BlockSpec(memory_space=pltpu.SMEM)
    return pl.pallas_call(
        tail_kernel,
        in_specs=specs,
        out_specs=[pl.BlockSpec(memory_space=pltpu.VMEM)] * 2,
        out_shape=[
            jax.ShapeDtypeStruct((F, 12, 4, LAT), jnp.float32),
            jax.ShapeDtypeStruct((F, 12, 4, C1), jnp.bfloat16),
        ],
        scratch_shapes=[
            pltpu.VMEM((F, 4, 8, 128), jnp.float32),
            pltpu.VMEM((6, 4, 16, 128), jnp.float32),
            pltpu.VMEM((F, 128, 128), jnp.float32),
            pltpu.VMEM((C1 // 128, F, 6, 24, 128), jnp.float32),
            pltpu.VMEM((C1 // 128, 6, 6, 24, 128), jnp.float32),
            pltpu.VMEM((6, 6, 16, 3 * C1), jnp.bfloat16),
            pltpu.VMEM((C1 // 128, F, 128, 128), jnp.float32),
            pltpu.VMEM((16, 128), jnp.float32),
        ],
        compiler_params=pltpu.CompilerParams(vmem_limit_bytes=32 << 20),
    )(*args)


def window_kernel(w_ref, out_ref):
    out_ref[...] = jnp.zeros(out_ref.shape, out_ref.dtype)
    for t in range(3):
        for u in range(3):
            for v in range(3):
                taps = w_ref[t, u, v]
                for p in range(2):
                    for q in range(2):
                        (dr, a), (dc, b) = divmod(p + u, 2), divmod(q + v, 2)
                        at = dr * 128 + dc * 64 + a * 32 + b * 16
                        out_ref[t, pl.ds(at, LAT), pl.ds((2 * p + q) * C1, C1)] = taps


def window_weights(weight):
    return pl.pallas_call(
        window_kernel,
        out_shape=jax.ShapeDtypeStruct((3, 16 * LAT, 4 * C1), jnp.bfloat16),
        compiler_params=pltpu.CompilerParams(vmem_limit_bytes=16 << 20),
    )(weight)


def put_frames(ref, rows, tokens):
    count = tokens[0].shape[0]
    low = lax.broadcasted_iota(jnp.int32, (count, 128), 1) < 64
    for i in range(2):
        for h in range(2):
            one = tokens[i + 2 * h]
            two = pltpu.roll(tokens[i + 4], 64, axis=1) if h == 0 else jnp.zeros_like(one)
            ref[i, pl.ds(rows + h * count, count), 384:512] = jnp.where(low, one, two)


def get_frames(ref, rows, count):
    out = {}
    for i in range(2):
        for h in range(2):
            both = ref[i, pl.ds(rows + h * count, count), 384:512]
            out[i + 2 * h] = both
            if h == 0:
                out[i + 4] = pltpu.roll(both, 64, axis=1)
    return [out[f] for f in range(6)]


def edge_rows_kernel(noisy_ref, cache_ref, mid_ref, tok_ref, down_ref, up_ref, cells):
    cells[...] = jnp.zeros(cells.shape, jnp.float32)
    cells[0:2, :, 0:12, 0:LAT] = cache_ref[...].astype(jnp.float32)
    cells[2:6, :, 0:12, 0:LAT] = noisy_ref[...]
    lane = lax.broadcasted_iota(jnp.int32, (8, 128), 1)
    tokens = {}
    for r in range(2):
        for f in range(6):
            token = jnp.zeros((8, 128), jnp.float32)
            for k in range(4):
                part = cells[f, 2 * r + k // 2, pl.ds(k % 2, 8, stride=2), :]
                part = pltpu.roll(part, LAT * k, axis=1) if k else part
                token = jnp.where((lane >= LAT * k) & (lane < LAT * k + LAT), part, token)
            tok_ref[f, r] = token
            tokens[f, r] = token
    for ref, row, r in ((down_ref, 3, 1), (up_ref, 0, 0)):
        ref[...] = jnp.zeros(ref.shape, jnp.float32)
        ref[:, 0:12, 0:C1] = mid_ref[:, row].astype(jnp.float32)
        put_frames(ref, 0, [tokens[f, r] for f in range(6)])


def edge_cols_kernel(tok_ref, mid_ref, above_ref, below_ref, toks, mids, right_ref, left_ref):
    above, below = get_frames(above_ref, 0, 8), get_frames(below_ref, 0, 8)
    for f in range(6):
        toks[f, 0] = above[f]
        toks[f, 1] = tok_ref[f, 0]
        toks[f, 2] = tok_ref[f, 1]
        toks[f, 3] = below[f]
    mids[...] = jnp.zeros(mids.shape, jnp.float32)
    mids[:, 0, 0:12, :] = above_ref[:, 0:12, 0:C1]
    mids[:, 1:5, 0:12, :] = mid_ref[...].astype(jnp.float32)
    mids[:, 5, 0:12, :] = below_ref[:, 0:12, 0:C1]
    for ref, token, col in ((right_ref, 5, 11), (left_ref, 0, 0)):
        ref[...] = jnp.zeros(ref.shape, jnp.float32)
        for i in range(2):
            for row in range(6):
                ref[i, pl.ds(row, 1), 0:C1] = mids[i, row, pl.ds(col, 1), :]
        for r in range(4):
            put_rows(ref, r, [toks[f, r, pl.ds(token, 1), :] for f in range(6)])


def put_rows(ref, r, tokens):
    low = lax.broadcasted_iota(jnp.int32, (1, 128), 1) < 64
    for i in range(2):
        for h in range(2):
            one = tokens[i + 2 * h]
            two = pltpu.roll(tokens[i + 4], 64, axis=1) if h == 0 else jnp.zeros_like(one)
            ref[i, pl.ds(4 * h + r, 1), 384:512] = jnp.where(low, one, two)


def place_kernel(toks, mids, left_ref, right_ref, cells_ref, cache_ref):
    cells_ref[...] = jnp.zeros(cells_ref.shape, jnp.float32)
    cache_ref[...] = jnp.zeros(cache_ref.shape, jnp.float32)
    for f in range(6):
        for r in range(4):
            cells_ref[f, r, 1:7, :] = toks[f, r, 0:6, :]
    cache_ref[:, :, 1:13, :] = mids[:, :, 0:12, :]
    for ref, token, col in ((left_ref, 0, 0), (right_ref, 7, 13)):
        frames = get_frames(ref, 0, 4)
        for f in range(6):
            for r in range(4):
                cells_ref[f, r, pl.ds(token, 1), :] = frames[f][r : r + 1]
        for i in range(2):
            for row in range(6):
                cache_ref[i, row, pl.ds(col, 1), :] = ref[i, pl.ds(row, 1), 0:C1]


def small_call(kernel, shapes, scratch=()):
    return pl.pallas_call(
        kernel,
        out_shape=[jax.ShapeDtypeStruct(shape, jnp.float32) for shape in shapes],
        scratch_shapes=[pltpu.VMEM(shape, jnp.float32) for shape in scratch],
        compiler_params=pltpu.CompilerParams(vmem_limit_bytes=8 << 20),
    )


def along(axis, step):
    count = lax.axis_size(axis)
    return [(i, i + step) for i in range(count) if 0 <= i + step < count]


def halo_rows(noisy, cache_in, cache_mid):
    edge = (2, 16, 512)
    toks, down, up = small_call(
        edge_rows_kernel, [(6, 2, 8, 128), edge, edge], [(6, 4, 16, 128)]
    )(noisy, cache_in, cache_mid)
    above = lax.ppermute(down, SEQ, along(SEQ, 1))
    below = lax.ppermute(up, SEQ, along(SEQ, -1))
    side = (2, 8, 512)
    return small_call(edge_cols_kernel, [(6, 4, 8, 128), (2, 6, 16, C1), side, side])(
        toks, cache_mid, above, below
    )


def pack_kernel(q_ref, k_ref, v_ref, out_ref):
    for h in range(out_ref.shape[0]):
        lanes = pl.ds(h * HEAD_DIM, HEAD_DIM)
        out_ref[h, :, 0:128] = k_ref[:, lanes]
        out_ref[h, :, 128:256] = v_ref[:, lanes]
        out_ref[h, :, 256:384] = q_ref[:, lanes]


def pack(query_vectors, key_vectors, value_vectors):
    tokens, width = query_vectors.shape
    heads = width // HEAD_DIM
    block = pl.BlockSpec((tokens, width // 2), lambda i: (0, i))
    return pl.pallas_call(
        pack_kernel,
        grid=(2,),
        in_specs=[block] * 3,
        out_specs=pl.BlockSpec((heads // 2, tokens, 3 * HEAD_DIM), lambda i: (i, 0, 0)),
        out_shape=jax.ShapeDtypeStruct((heads, tokens, 3 * HEAD_DIM), jnp.bfloat16),
    )(query_vectors, key_vectors, value_vectors)


def merge_kernel(own_ref, oth_ref, out_ref, vel_ref, piece_ref):
    own, oth = own_ref[...], oth_ref[...]
    gap = pltpu.roll(oth - own, 64, axis=1)
    share = 1.0 / (1.0 + jnp.exp2(gap))
    vel = own * share + oth * (1.0 - share)
    lane = lax.broadcasted_iota(jnp.int32, vel.shape, 1)
    vel_ref[...] = jnp.where(lane < 64, vel, pltpu.roll(vel, 64, axis=1))
    low = lax.broadcasted_iota(jnp.int32, (16, 128), 1) < 64
    zero = jnp.zeros((16, 128), jnp.float32)

    def column(r, at):
        if at < 0 or at >= 48:
            return zero
        return vel_ref[pl.ds(r * 48 + at, 16, stride=96), :]

    for b in range(8):
        for r in range(2):
            for c in range(4):
                at = 6 * b - 1 + c
                both = jnp.where(low, column(r, at), column(r, at + 4))
                for y in range(4):
                    piece_ref[y, b, pl.ds(r * 16 + c, 4, stride=4), :] = both[y * 4 : y * 4 + 4]
    out_ref[...] = piece_ref[...].astype(jnp.bfloat16)


def merge(own, oth):
    rows = own.shape[0]
    whole = pl.BlockSpec((rows, 128), lambda: (0, 0))
    shape = (4, 8, 32, 128)
    return pl.pallas_call(
        merge_kernel,
        in_specs=[whole, whole],
        out_specs=pl.BlockSpec(shape, lambda: (0, 0, 0, 0)),
        out_shape=jax.ShapeDtypeStruct(shape, jnp.bfloat16),
        scratch_shapes=[
            pltpu.VMEM((rows, 128), jnp.float32),
            pltpu.VMEM(shape, jnp.float32),
        ],
        compiler_params=pltpu.CompilerParams(vmem_limit_bytes=24 << 20),
    )(own, oth)


def head_sum_kernel(parts_ref, mine_ref, near_ref, apart_ref):
    total = parts_ref[0].astype(jnp.float32)
    for h in range(1, parts_ref.shape[0]):
        total = total + parts_ref[h].astype(jnp.float32)
    mine_ref[...] = total
    even = lax.axis_index("core") == 0
    near_ref[...] = jnp.where(even, total[16:32], total[0:16])
    apart_ref[...] = jnp.where(even, total[0:16], total[16:32])


def head_sum(parts):
    return small_call(head_sum_kernel, [(32, 128), (16, 128), (16, 128)])(parts)


def attention(query_vectors, key_vectors, value_vectors, weight_head, inputs):
    packed = pack(query_vectors, key_vectors, value_vectors)
    packed, inputs = lax.optimization_barrier((packed, inputs))
    noisy, cache_in, cache_mid, weight_in = inputs
    rows = halo_rows(noisy, cache_in, cache_mid)
    weight_first = window_weights(weight_in)
    heads, tokens = packed.shape[:2]
    moved = lax.all_to_all(packed, HEAD, split_axis=0, concat_axis=0, tiled=True)
    moved = moved.reshape(heads * tokens, 3 * HEAD_DIM)
    swap = [(0, 1), (1, 0)]
    right = [(i, (i + 1) % 4) for i in range(4)]
    left = [((i + 1) % 4, i) for i in range(4)]
    mid = moved.shape[0] // 2
    a, b, q_own = moved[:mid, :256], moved[mid:, :256], moved[:, 256:]
    a, b, q_own, rows, weight_first = lax.optimization_barrier((a, b, q_own, rows, weight_first))
    left_a = lax.ppermute(a, "y", right)
    right_b = lax.ppermute(b, "y", left)
    q_oth = lax.ppermute(q_own, "core", swap)
    state = flash(moved, q_oth, [moved])
    toks, mids, to_right, to_left = rows
    state, a, b, to_right, to_left = lax.optimization_barrier((state, a, b, to_right, to_left))
    left_b = lax.ppermute(b, "y", right)
    right_a = lax.ppermute(a, "y", left)
    before = lax.ppermute(to_right, BLK, along(BLK, 1))
    after = lax.ppermute(to_left, BLK, along(BLK, -1))
    state = flash(moved, q_oth, [left_a, right_b], state)
    state, left_a, right_b, before, after = lax.optimization_barrier(
        (state, left_a, right_b, before, after)
    )
    borders = small_call(place_kernel, [(6, 4, 8, 128), (2, 6, 16, C1)])(
        toks, mids, before, after
    )
    far = [lax.ppermute(left_a, "y", right), lax.ppermute(right_b, "y", left)]
    state = flash(moved, q_oth, [left_b, right_a], state)
    weight = weight_head.T
    oth = flash_last(q_oth, 0, far, state, 1, weight)
    oth, state = lax.optimization_barrier((oth, state))
    oth = lax.ppermute(oth, "core", swap)
    own = flash_last(moved, 2, far, state, 0, weight)
    partial = merge(own, oth).reshape(heads, 32, 128)
    parts = lax.all_to_all(partial, HEAD, split_axis=0, concat_axis=0, tiled=True)
    return head_sum(parts), (*borders, weight_first)


def shards(
    query_vectors,
    key_vectors,
    value_vectors,
    weight_head,
    noisy_latent,
    noise_level,
    latent_mean,
    latent_scale,
    cache_in,
    weight_in,
    bias_in,
    norm_gain,
    cache_mid,
    weight_mid,
    bias_mid,
):
    (mine, near, apart), (cells, cache_second, weight_first) = attention(
        query_vectors,
        key_vectors,
        value_vectors,
        weight_head,
        (noisy_latent, cache_in, cache_mid, weight_in),
    )

    count = lax.axis_size(SEQ)
    near = lax.ppermute(near, SEQ, [(i, i ^ 1) for i in range(count)])
    pairs = [(i, i + 1) for i in range(1, count - 1, 2)]
    pairs += [(j, i) for i, j in pairs]
    apart = lax.ppermute(apart, SEQ, pairs)
    denoised, features = tail(
        near,
        mine,
        apart,
        cells,
        noise_level,
        latent_scale,
        latent_mean,
        weight_first,
        bias_in,
        norm_gain,
        cache_second,
        weight_mid.reshape(9, 3 * C1, C1),
        bias_mid,
    )
    return denoised.transpose(0, 2, 1, 3), features.transpose(0, 2, 1, 3)


def solution(mesh):
    inner = Mesh(mesh.devices.reshape(4, 4, 2, 2, 4), SHARD)
    tokens, tile = P(SHARD, None), P(None, SEQ, BLK, None)
    in_specs = (
        tokens,
        tokens,
        tokens,
        P(),
        tile,
        P(),
        P(),
        P(),
        tile,
        P(),
        P(),
        P(),
        tile,
        P(),
        P(),
    )
    return jax.shard_map(
        shards, mesh=inner, in_specs=in_specs, out_specs=(tile, tile), check_vma=False
    )
```

```python
import functools
import math

import jax
import jax.numpy as jnp
from jax import lax
from jax.experimental import pallas as pl
from jax.experimental.pallas import tpu as pltpu
from jax.sharding import Mesh
from jax.sharding import PartitionSpec as P

HEAD_DIM = 128
LAT = 16
C1 = 384
F = 4
EPSILON = 1e-06

SEQ = ("y", "zh", "core")
BLK = ("zl", "x")
HEAD = ("zh", "zl", "x")
SHARD = SEQ + BLK

TILE = 1536
SUB = 256
CHUNK = 768
NT = (((1,), (1,)), ((), ()))


def mesh_index(axes):
    index = 0
    for axis in axes:
        index = index * lax.axis_size(axis) + lax.axis_index(axis)
    return index


def lane_max(s):
    t = s[:, :128]
    for j in range(1, s.shape[1] // 128):
        t = jnp.maximum(t, s[:, j * 128 : (j + 1) * 128])
    return jnp.max(t, axis=1, keepdims=True)


def flash_kernel(first, last, n_kv, half, *refs):
    q_ref, refs = refs[0], refs[1:]
    if not last:
        qx_ref, refs = refs[0], refs[1:]
    kv_refs, refs = refs[:n_kv], refs[n_kv:]
    if not first:
        st_ref, refs = refs[0], refs[1:]
    if last:
        w_ref, u_ref = refs
        query = q_ref[...]
        own = w_ref[:, pl.ds(pl.multiple_of(mesh_index(HEAD) * HEAD_DIM, HEAD_DIM), HEAD_DIM)]
        weight = jnp.concatenate([own, jnp.zeros_like(own)], axis=0)
    else:
        (so_ref,) = refs
        query = jnp.where(pl.program_id(0) < half, q_ref[...], qx_ref[...])
    scale = math.log2(math.e) / math.sqrt(HEAD_DIM)
    qf = query.astype(jnp.float32) * scale
    q_hi = qf.astype(jnp.bfloat16)
    q_lo = (qf - q_hi.astype(jnp.float32)).astype(jnp.bfloat16)
    q = jnp.concatenate([q_hi, q_lo], axis=1)
    subs = TILE // SUB
    tops, accs = [], []
    for r in range(subs):
        if first:
            tops.append(jnp.full((SUB, 128), -1e30, jnp.float32))
            accs.append(jnp.zeros((SUB, 256), jnp.float32))
        else:
            st = st_ref[pl.ds(r * SUB, SUB), :]
            acc_l = st[:, 128:]
            lane = lax.broadcasted_iota(jnp.int32, (SUB, 128), 1)
            total = jnp.max(jnp.where(lane < 64, acc_l, -1e30), axis=1, keepdims=True)
            top = jnp.max(jnp.where(lane < 64, -1e30, acc_l), axis=1, keepdims=True)
            tops.append(jnp.broadcast_to(top, (SUB, 128)))
            accs.append(
                jnp.concatenate([st[:, :128], jnp.broadcast_to(total, (SUB, 128))], axis=1)
            )
    items = [
        (r, b, c)
        for r in range(subs)
        for b in range(n_kv)
        for c in range(kv_refs[b].shape[0] // CHUNK)
    ]
    ones = jnp.ones((CHUNK, 128), jnp.bfloat16)

    def score(item):
        r, b, c = item
        k = kv_refs[b][pl.ds(c * CHUNK, CHUNK), :128]
        return lax.dot_general(
            q[r * SUB : (r + 1) * SUB],
            jnp.concatenate([k, k], axis=1),
            NT,
            preferred_element_type=jnp.float32,
        )

    s = score(items[0])
    for n, (r, b, c) in enumerate(items):
        following = score(items[n + 1]) if n + 1 < len(items) else None
        top = jnp.maximum(tops[r], lane_max(s))
        p = jnp.exp2(s - top[:, :1]).astype(jnp.bfloat16)
        fade = jnp.exp2(tops[r] - top)
        v = jnp.concatenate([kv_refs[b][pl.ds(c * CHUNK, CHUNK), 128:], ones], axis=1)
        accs[r] = accs[r] * jnp.concatenate([fade, fade], axis=1) + jnp.dot(
            p, v, preferred_element_type=jnp.float32
        )
        tops[r] = top
        s = following
    lane = lax.broadcasted_iota(jnp.int32, (SUB, 128), 1)
    for r in range(subs):
        if last:
            total = accs[r][:, 128:]
            mixed = (accs[r][:, :128] / total).astype(jnp.bfloat16)
            u = lax.dot_general(mixed, weight, NT, preferred_element_type=jnp.float32)
            u_ref[pl.ds(r * SUB, SUB), :] = jnp.where(lane < 64, u, tops[r] + jnp.log2(total))
        else:
            so_ref[pl.ds(r * SUB, SUB), :] = jnp.concatenate(
                [accs[r][:, :128], jnp.where(lane < 64, accs[r][:, 128:], tops[r])], axis=1
            )


def flash(q_own, q_oth, kvs, state=None):
    rows = q_oth.shape[0]
    half = rows // TILE
    keys = sum(kv.shape[0] for kv in kvs)
    in_specs = [
        pl.BlockSpec((TILE, 128), lambda i: (jnp.minimum(i, half - 1), 2)),
        pl.BlockSpec((TILE, 128), lambda i: (jnp.maximum(i - half, 0), 0)),
    ]
    in_specs += [pl.BlockSpec((kv.shape[0], 256), lambda i: (0, 0)) for kv in kvs]
    args = [q_own, q_oth, *kvs]
    if state is not None:
        in_specs.append(pl.BlockSpec((TILE, 256), lambda i: (i, 0)))
        args.append(state)
    return pl.pallas_call(
        functools.partial(flash_kernel, state is None, False, len(kvs), half),
        grid=(2 * half,),
        in_specs=in_specs,
        out_specs=pl.BlockSpec((TILE, 256), lambda i: (i, 0)),
        out_shape=jax.ShapeDtypeStruct((2 * rows, 256), jnp.float32),
        compiler_params=pltpu.CompilerParams(vmem_limit_bytes=20 << 20),
        cost_estimate=flash_cost(2 * rows, keys),
    )(*args)


def flash_last(query, lane_block, kvs, state, half_at, weight):
    rows = query.shape[0]
    half = rows // TILE
    keys = sum(kv.shape[0] for kv in kvs)
    in_specs = [pl.BlockSpec((TILE, 128), lambda i: (i, lane_block))]
    in_specs += [pl.BlockSpec((kv.shape[0], 256), lambda i: (0, 0)) for kv in kvs]
    in_specs += [
        pl.BlockSpec((TILE, 256), lambda i: (i + half_at * half, 0)),
        pl.BlockSpec(weight.shape, lambda i: (0, 0)),
    ]
    return pl.pallas_call(
        functools.partial(flash_kernel, False, True, len(kvs), half),
        grid=(half,),
        in_specs=in_specs,
        out_specs=pl.BlockSpec((TILE, 128), lambda i: (i, 0)),
        out_shape=jax.ShapeDtypeStruct((rows, 128), jnp.float32),
        compiler_params=pltpu.CompilerParams(vmem_limit_bytes=20 << 20),
        cost_estimate=flash_cost(rows, keys),
    )(query, *kvs, state, weight)


def flash_cost(rows, keys):
    return pl.CostEstimate(
        flops=rows * keys * 1024, bytes_accessed=rows * 2048, transcendentals=rows * keys
    )


def inside(at, low, high, before, after):
    return ((at > low) | before) & ((at < high) | after)


def tail_kernel(
    near_ref,
    mine_ref,
    apart_ref,
    cells_ref,
    level_ref,
    scale_ref,
    mean_ref,
    w1_ref,
    b1_ref,
    gain_ref,
    mid_ref,
    w2_ref,
    b2_ref,
    den_ref,
    out_ref,
    vel,
    lat,
    den,
    first,
    act,
    wide,
    done,
    vecs,
):
    even = lax.axis_index("core") == 0
    at_row, at_col = mesh_index(SEQ), mesh_index(BLK)
    up, down = at_row > 0, at_row < lax.axis_size(SEQ) - 1
    before, after = at_col > 0, at_col < lax.axis_size(BLK) - 1
    above = jnp.where(even, apart_ref[...], near_ref[...])
    below = jnp.where(even, near_ref[...], apart_ref[...])
    for at, rows in enumerate((above, mine_ref[0:16, :], mine_ref[16:32, :], below)):
        turned = pltpu.roll(rows, 64, axis=1)
        for f in range(F):
            vel[f, at, 0:4, :] = rows[f * 4 : f * 4 + 4]
            vel[f, at, 4:8, :] = turned[f * 4 : f * 4 + 4]
    vecs[...] = jnp.zeros(vecs.shape, jnp.float32)
    vecs[0:1, 0:LAT] = scale_ref[...].reshape(1, LAT)
    vecs[8:9, 0:LAT] = mean_ref[...].reshape(1, LAT)
    base = vecs[...]
    tiled = base + pltpu.roll(base, LAT, axis=1)
    tiled = tiled + pltpu.roll(tiled, 2 * LAT, axis=1)
    scale, mean = tiled[0:1, 0:64], tiled[8:9, 0:64]
    denoised = cells_ref[2:6, :, :, 0:64] - level_ref[0] * vel[:, :, :, 0:64]
    row = lax.broadcasted_iota(jnp.int32, denoised.shape, 1)
    col = lax.broadcasted_iota(jnp.int32, denoised.shape, 2)
    kept = inside(row, 0, 3, up, down) & inside(col, 0, 7, before, after)
    latent = jnp.where(kept, denoised * scale + mean, 0.0)
    for k in range(4):
        part = jnp.concatenate([denoised, denoised], axis=3).reshape(F * 32, 128)
        part = pltpu.roll(part, 128 - LAT * k, axis=1) if k else part
        part = part.reshape(F, 4, 8, 128)
        for f in range(F):
            for r in range(2):
                rows = pl.ds(8 * (k % 2) + 2 * r + k // 2, 8, stride=16)
                den[f, rows, :] = part[f, r + 1]
    den_ref[...] = den[:, 16:112, :].reshape(F, 12, 8, 128)[:, :, 0:4, 0:LAT]
    lat[...] = jnp.zeros(lat.shape, jnp.float32)
    lat[0:2, :, 0:8, 0:64] = cells_ref[0:2, :, :, 0:64]
    lat[2:6, :, 0:8, 0:64] = latent.astype(jnp.bfloat16).astype(jnp.float32)
    here = lat[:, :, 0:8, :].reshape(192, 128)
    right = pltpu.roll(lat[:, :, 1:9, :].reshape(192, 128), 64, axis=1)
    lane = lax.broadcasted_iota(jnp.int32, (192, 128), 1)
    pair = jnp.where(lane < 64, here, right).reshape(6, 4, 8, 128)
    lower = jnp.concatenate([pair[:, 1:4], pair[:, 3:4]], axis=1)
    window = jnp.concatenate([pair, lower], axis=3).reshape(192, 256).astype(jnp.bfloat16)
    parts = C1 // 128
    for k in range(parts):
        act[k, 0:2, :, 0:16, :] = mid_ref[:, :, :, pl.ds(k * 128, 128)]
    gain = gain_ref[...].reshape(1, C1)
    for p in range(2):
        for q in range(2):
            lanes = pl.ds((2 * p + q) * C1, C1)
            value = b1_ref[...].reshape(1, C1)
            for t in range(3):
                value = value + jnp.dot(
                    window[t * 32 : t * 32 + 128],
                    w1_ref[t, :, lanes],
                    preferred_element_type=jnp.float32,
                )
            power = jnp.mean(value * value, axis=1, keepdims=True)
            normed = value * lax.rsqrt(power + EPSILON) * gain
            active = (normed / (1.0 + jnp.exp(-normed))).reshape(F, 32, C1)
            at = lax.broadcasted_iota(jnp.int32, (32, C1), 0)
            kept = inside(2 * (at // 8) + p, 0, 5, up, down)
            kept = kept & inside(2 * (at % 8) + q, 0, 13, before, after)
            active = jnp.where(kept, active, 0.0)
            value = value.reshape(F, 4, 8, C1)
            active = active.reshape(F, 4, 8, C1)
            for r in range(3):
                cols = pl.ds(q, 8, stride=2)
                for k in range(parts):
                    part = slice(k * 128, k * 128 + 128)
                    for f in range(F):
                        first[k, f, 2 * r + p, cols, :] = value[f, r, :, part]
                        act[k, f + 2, 2 * r + p, cols, :] = active[f, r, :, part]
    for v in range(3):
        for k in range(parts):
            wide[:, :, :, pl.ds(v * C1 + k * 128, 128)] = act[k, :, :, pl.ds(v, 16), :].astype(
                jnp.bfloat16
            )
    middle = [first[k, :, 1:5, pl.ds(1, 16), :].reshape(256, 128) for k in range(parts)]
    total = jnp.concatenate(middle, axis=1) + b2_ref[...].reshape(1, C1)
    for tap in range(9):
        t, u = divmod(tap, 3)
        rows = wide[t : t + 4, u : u + 4].reshape(256, 3 * C1)
        total = total + jnp.dot(rows, w2_ref[tap], preferred_element_type=jnp.float32)
    for k in range(parts):
        for f in range(F):
            for i in range(4):
                at = f * 64 + i * 16
                done[k, f, pl.ds(i, 16, stride=8), :] = total[at : at + 16, k * 128 : k * 128 + 128]
        cells = done[k, :, 0:96, :].reshape(F, 12, 8, 128)[:, :, 0:4]
        out_ref[:, :, :, pl.ds(k * 128, 128)] = cells.astype(jnp.bfloat16)


def tail(*args):
    specs = [pl.BlockSpec(memory_space=pltpu.VMEM)] * len(args)
    specs[4] = pl.BlockSpec(memory_space=pltpu.SMEM)
    return pl.pallas_call(
        tail_kernel,
        in_specs=specs,
        out_specs=[pl.BlockSpec(memory_space=pltpu.VMEM)] * 2,
        out_shape=[
            jax.ShapeDtypeStruct((F, 12, 4, LAT), jnp.float32),
            jax.ShapeDtypeStruct((F, 12, 4, C1), jnp.bfloat16),
        ],
        scratch_shapes=[
            pltpu.VMEM((F, 4, 8, 128), jnp.float32),
            pltpu.VMEM((6, 4, 16, 128), jnp.float32),
            pltpu.VMEM((F, 128, 128), jnp.float32),
            pltpu.VMEM((C1 // 128, F, 6, 24, 128), jnp.float32),
            pltpu.VMEM((C1 // 128, 6, 6, 24, 128), jnp.float32),
            pltpu.VMEM((6, 6, 16, 3 * C1), jnp.bfloat16),
            pltpu.VMEM((C1 // 128, F, 128, 128), jnp.float32),
            pltpu.VMEM((16, 128), jnp.float32),
        ],
        compiler_params=pltpu.CompilerParams(vmem_limit_bytes=32 << 20),
    )(*args)


def window_kernel(w_ref, out_ref):
    out_ref[...] = jnp.zeros(out_ref.shape, out_ref.dtype)
    for t in range(3):
        for u in range(3):
            for v in range(3):
                taps = w_ref[t, u, v]
                for p in range(2):
                    for q in range(2):
                        (dr, a), (dc, b) = divmod(p + u, 2), divmod(q + v, 2)
                        at = dr * 128 + dc * 64 + a * 32 + b * 16
                        out_ref[t, pl.ds(at, LAT), pl.ds((2 * p + q) * C1, C1)] = taps


def window_weights(weight):
    return pl.pallas_call(
        window_kernel,
        out_shape=jax.ShapeDtypeStruct((3, 16 * LAT, 4 * C1), jnp.bfloat16),
        compiler_params=pltpu.CompilerParams(vmem_limit_bytes=16 << 20),
    )(weight)


def put_frames(ref, rows, tokens):
    count = tokens[0].shape[0]
    low = lax.broadcasted_iota(jnp.int32, (count, 128), 1) < 64
    for i in range(2):
        for h in range(2):
            one = tokens[i + 2 * h]
            two = pltpu.roll(tokens[i + 4], 64, axis=1) if h == 0 else jnp.zeros_like(one)
            ref[i, pl.ds(rows + h * count, count), 384:512] = jnp.where(low, one, two)


def get_frames(ref, rows, count):
    out = {}
    for i in range(2):
        for h in range(2):
            both = ref[i, pl.ds(rows + h * count, count), 384:512]
            out[i + 2 * h] = both
            if h == 0:
                out[i + 4] = pltpu.roll(both, 64, axis=1)
    return [out[f] for f in range(6)]


def edges_kernel(noisy_ref, cache_ref, mid_ref, tok_ref, *refs):
    down_ref, up_ref, right_ref, left_ref = refs[:4]
    corner_refs, cells, mids = refs[4:8], refs[8], refs[9]
    cells[...] = jnp.zeros(cells.shape, jnp.float32)
    cells[0:2, :, 0:12, 0:LAT] = cache_ref[...].astype(jnp.float32)
    cells[2:6, :, 0:12, 0:LAT] = noisy_ref[...]
    mids[:, :, 0:12, :] = mid_ref[...].astype(jnp.float32)
    lane = lax.broadcasted_iota(jnp.int32, (8, 128), 1)
    tokens = {}
    for r in range(2):
        for f in range(6):
            token = jnp.zeros((8, 128), jnp.float32)
            for k in range(4):
                part = cells[f, 2 * r + k // 2, pl.ds(k % 2, 8, stride=2), :]
                part = pltpu.roll(part, LAT * k, axis=1) if k else part
                token = jnp.where((lane >= LAT * k) & (lane < LAT * k + LAT), part, token)
            tok_ref[f, r] = token
            tokens[f, r] = token
    for ref, row, r in ((down_ref, 3, 1), (up_ref, 0, 0)):
        ref[...] = jnp.zeros(ref.shape, jnp.float32)
        ref[:, 0:12, 0:C1] = mids[:, row, 0:12, :]
        put_frames(ref, 0, [tokens[f, r] for f in range(6)])
    for ref, token, col in ((right_ref, 5, 11), (left_ref, 0, 0)):
        ref[...] = jnp.zeros(ref.shape, jnp.float32)
        for i in range(2):
            for row in range(4):
                ref[i, pl.ds(row, 1), 0:C1] = mids[i, row, pl.ds(col, 1), :]
        for r in range(2):
            put_rows(ref, r, [tok_ref[f, r, pl.ds(token, 1), :] for f in range(6)])
    low = lax.broadcasted_iota(jnp.int32, (1, 128), 1) < 64
    for ref, (row, r), (token, col) in zip(
        corner_refs, ((3, 1), (3, 1), (0, 0), (0, 0)), ((5, 11), (0, 0), (5, 11), (0, 0))
    ):
        ref[...] = jnp.zeros(ref.shape, jnp.float32)
        for i in range(2):
            ref[pl.ds(i, 1), 0:C1] = mids[i, row, pl.ds(col, 1), :]
        for f in range(4):
            one = tok_ref[f, r, pl.ds(token, 1), :]
            two = pltpu.roll(tok_ref[f % 2 + 4, r, pl.ds(token, 1), :], 64, axis=1)
            ref[pl.ds(f, 1), 384:512] = jnp.where(low, one, two)


def put_rows(ref, r, tokens):
    low = lax.broadcasted_iota(jnp.int32, (1, 128), 1) < 64
    for i in range(2):
        for h in range(2):
            one = tokens[i + 2 * h]
            two = pltpu.roll(tokens[i + 4], 64, axis=1) if h == 0 else jnp.zeros_like(one)
            ref[i, pl.ds(4 * h + r, 1), 384:512] = jnp.where(low, one, two)


def place_kernel(tok_ref, mid_ref, *refs):
    above_ref, below_ref, before_ref, after_ref = refs[:4]
    corner_refs, cells_ref, cache_ref = refs[4:8], refs[8], refs[9]
    cells_ref[...] = jnp.zeros(cells_ref.shape, jnp.float32)
    cache_ref[...] = jnp.zeros(cache_ref.shape, jnp.float32)
    for f in range(6):
        for r in range(2):
            cells_ref[f, r + 1, 1:7, :] = tok_ref[f, r, 0:6, :]
    cache_ref[:, 1:5, 1:13, :] = mid_ref[...].astype(jnp.float32)
    for ref, r, row in ((above_ref, 0, 0), (below_ref, 3, 5)):
        frames = get_frames(ref, 0, 8)
        for f in range(6):
            cells_ref[f, r, 1:7, :] = frames[f][0:6]
        cache_ref[:, row, 1:13, :] = ref[:, 0:12, 0:C1]
    for ref, token, col in ((before_ref, 0, 0), (after_ref, 7, 13)):
        frames = get_frames(ref, 0, 4)
        for f in range(6):
            for r in range(2):
                cells_ref[f, r + 1, pl.ds(token, 1), :] = frames[f][r : r + 1]
        for i in range(2):
            for row in range(4):
                cache_ref[i, row + 1, pl.ds(col, 1), :] = ref[i, pl.ds(row, 1), 0:C1]
    for ref, (r, row), (token, col) in zip(
        corner_refs, ((0, 0), (0, 0), (3, 5), (3, 5)), ((0, 0), (7, 13), (0, 0), (7, 13))
    ):
        for i in range(2):
            cache_ref[i, row, pl.ds(col, 1), :] = ref[pl.ds(i, 1), 0:C1]
        for f in range(6):
            both = ref[pl.ds(f % 4, 1), 384:512]
            cells_ref[f, r, pl.ds(token, 1), :] = pltpu.roll(both, 64, axis=1) if f > 3 else both


def small_call(kernel, shapes, scratch=()):
    return pl.pallas_call(
        kernel,
        out_shape=[jax.ShapeDtypeStruct(shape, jnp.float32) for shape in shapes],
        scratch_shapes=[pltpu.VMEM(shape, jnp.float32) for shape in scratch],
        compiler_params=pltpu.CompilerParams(vmem_limit_bytes=8 << 20),
    )


def along(axis, step):
    count = lax.axis_size(axis)
    return [(i, i + step) for i in range(count) if 0 <= i + step < count]


def input_borders(noisy, cache_in, cache_mid):
    edge, side, corner = (2, 16, 512), (2, 8, 512), (8, 512)
    toks, down, up, right, left, *corners = small_call(
        edges_kernel,
        [(6, 2, 8, 128), edge, edge, side, side] + [corner] * 4,
        [(6, 4, 16, 128), (2, 4, 16, C1)],
    )(noisy, cache_in, cache_mid)
    around = [
        lax.ppermute(down, SEQ, along(SEQ, 1)),
        lax.ppermute(up, SEQ, along(SEQ, -1)),
        lax.ppermute(right, BLK, along(BLK, 1)),
        lax.ppermute(left, BLK, along(BLK, -1)),
    ]
    cols = lax.axis_size(BLK)
    for part, (row, col) in zip(corners, ((1, 1), (1, -1), (-1, 1), (-1, -1))):
        diagonal = [
            (i * cols + j, m * cols + n)
            for i, m in along(SEQ, row)
            for j, n in along(BLK, col)
        ]
        around.append(lax.ppermute(part, SHARD, diagonal))
    return small_call(place_kernel, [(6, 4, 8, 128), (2, 6, 16, C1)])(toks, cache_mid, *around)


def pack_kernel(q_ref, k_ref, v_ref, out_ref):
    for h in range(out_ref.shape[0]):
        lanes = pl.ds(h * HEAD_DIM, HEAD_DIM)
        out_ref[h, :, 0:128] = k_ref[:, lanes]
        out_ref[h, :, 128:256] = v_ref[:, lanes]
        out_ref[h, :, 256:384] = q_ref[:, lanes]


def pack(query_vectors, key_vectors, value_vectors):
    tokens, width = query_vectors.shape
    heads = width // HEAD_DIM
    block = pl.BlockSpec((tokens, width), lambda i: (0, i))
    return pl.pallas_call(
        pack_kernel,
        grid=(1,),
        in_specs=[block] * 3,
        out_specs=pl.BlockSpec((heads, tokens, 3 * HEAD_DIM), lambda i: (i, 0, 0)),
        out_shape=jax.ShapeDtypeStruct((heads, tokens, 3 * HEAD_DIM), jnp.bfloat16),
    )(query_vectors, key_vectors, value_vectors)


def merge_kernel(own_ref, oth_ref, out_ref, vel_ref, piece_ref):
    own, oth = own_ref[...], oth_ref[...]
    gap = pltpu.roll(oth - own, 64, axis=1)
    share = 1.0 / (1.0 + jnp.exp2(gap))
    vel = own * share + oth * (1.0 - share)
    lane = lax.broadcasted_iota(jnp.int32, vel.shape, 1)
    vel_ref[...] = jnp.where(lane < 64, vel, pltpu.roll(vel, 64, axis=1))
    low = lax.broadcasted_iota(jnp.int32, (16, 128), 1) < 64
    zero = jnp.zeros((16, 128), jnp.float32)

    def column(r, at):
        if at < 0 or at >= 48:
            return zero
        return vel_ref[pl.ds(r * 48 + at, 16, stride=96), :]

    for b in range(8):
        for r in range(2):
            for c in range(4):
                at = 6 * b - 1 + c
                both = jnp.where(low, column(r, at), column(r, at + 4))
                for y in range(4):
                    piece_ref[y, b, pl.ds(r * 16 + c, 4, stride=4), :] = both[y * 4 : y * 4 + 4]
    out_ref[...] = piece_ref[...].astype(jnp.bfloat16)


def merge(own, oth):
    rows = own.shape[0]
    whole = pl.BlockSpec((rows, 128), lambda: (0, 0))
    shape = (4, 8, 32, 128)
    return pl.pallas_call(
        merge_kernel,
        in_specs=[whole, whole],
        out_specs=pl.BlockSpec(shape, lambda: (0, 0, 0, 0)),
        out_shape=jax.ShapeDtypeStruct(shape, jnp.bfloat16),
        scratch_shapes=[
            pltpu.VMEM((rows, 128), jnp.float32),
            pltpu.VMEM(shape, jnp.float32),
        ],
        compiler_params=pltpu.CompilerParams(vmem_limit_bytes=24 << 20),
    )(own, oth)


def head_sum_kernel(parts_ref, mine_ref, near_ref, apart_ref):
    total = parts_ref[0].astype(jnp.float32)
    for h in range(1, parts_ref.shape[0]):
        total = total + parts_ref[h].astype(jnp.float32)
    mine_ref[...] = total
    even = lax.axis_index("core") == 0
    near_ref[...] = jnp.where(even, total[16:32], total[0:16])
    apart_ref[...] = jnp.where(even, total[0:16], total[16:32])


def head_sum(parts):
    return small_call(head_sum_kernel, [(32, 128), (16, 128), (16, 128)])(parts)


def attention(query_vectors, key_vectors, value_vectors, weight_head, inputs):
    packed = pack(query_vectors, key_vectors, value_vectors)
    packed, inputs = lax.optimization_barrier((packed, inputs))
    noisy, cache_in, cache_mid, weight_in = inputs
    borders = input_borders(noisy, cache_in, cache_mid)
    weight_first = window_weights(weight_in)
    heads, tokens = packed.shape[:2]
    moved = lax.all_to_all(packed, HEAD, split_axis=0, concat_axis=0, tiled=True)
    moved = moved.reshape(heads * tokens, 3 * HEAD_DIM)
    swap = [(0, 1), (1, 0)]
    right = [(i, (i + 1) % 4) for i in range(4)]
    left = [((i + 1) % 4, i) for i in range(4)]
    mid = moved.shape[0] // 2
    a, b, q_own = moved[:mid, :256], moved[mid:, :256], moved[:, 256:]
    a, b, q_own, borders, weight_first = lax.optimization_barrier(
        (a, b, q_own, borders, weight_first)
    )
    left_a = lax.ppermute(a, "y", right)
    right_b = lax.ppermute(b, "y", left)
    q_oth = lax.ppermute(q_own, "core", swap)
    state = flash(moved, q_oth, [moved])
    state, a, b = lax.optimization_barrier((state, a, b))
    left_b = lax.ppermute(b, "y", right)
    right_a = lax.ppermute(a, "y", left)
    state = flash(moved, q_oth, [left_a, right_b], state)
    state, left_a, right_b = lax.optimization_barrier((state, left_a, right_b))
    far = [lax.ppermute(left_a, "y", right), lax.ppermute(right_b, "y", left)]
    state = flash(moved, q_oth, [left_b, right_a], state)
    weight = weight_head.T
    oth = flash_last(q_oth, 0, far, state, 1, weight)
    oth, state = lax.optimization_barrier((oth, state))
    oth = lax.ppermute(oth, "core", swap)
    own = flash_last(moved, 2, far, state, 0, weight)
    partial = merge(own, oth).reshape(heads, 32, 128)
    parts = lax.all_to_all(partial, HEAD, split_axis=0, concat_axis=0, tiled=True)
    return head_sum(parts), (*borders, weight_first)


def shards(
    query_vectors,
    key_vectors,
    value_vectors,
    weight_head,
    noisy_latent,
    noise_level,
    latent_mean,
    latent_scale,
    cache_in,
    weight_in,
    bias_in,
    norm_gain,
    cache_mid,
    weight_mid,
    bias_mid,
):
    (mine, near, apart), (cells, cache_second, weight_first) = attention(
        query_vectors,
        key_vectors,
        value_vectors,
        weight_head,
        (noisy_latent, cache_in, cache_mid, weight_in),
    )

    count = lax.axis_size(SEQ)
    near = lax.ppermute(near, SEQ, [(i, i ^ 1) for i in range(count)])
    pairs = [(i, i + 1) for i in range(1, count - 1, 2)]
    pairs += [(j, i) for i, j in pairs]
    apart = lax.ppermute(apart, SEQ, pairs)
    denoised, features = tail(
        near,
        mine,
        apart,
        cells,
        noise_level,
        latent_scale,
        latent_mean,
        weight_first,
        bias_in,
        norm_gain,
        cache_second,
        weight_mid.reshape(9, 3 * C1, C1),
        bias_mid,
    )
    return denoised.transpose(0, 2, 1, 3), features.transpose(0, 2, 1, 3)


def solution(mesh):
    inner = Mesh(mesh.devices.reshape(4, 4, 2, 2, 4), SHARD)
    tokens, tile = P(SHARD, None), P(None, SEQ, BLK, None)
    in_specs = (
        tokens,
        tokens,
        tokens,
        P(),
        tile,
        P(),
        P(),
        P(),
        tile,
        P(),
        P(),
        P(),
        tile,
        P(),
        P(),
    )
    return jax.shard_map(
        shards, mesh=inner, in_specs=in_specs, out_specs=(tile, tile), check_vma=False
    )
```

```python
import functools
import math

import jax
import jax.numpy as jnp
from jax import lax
from jax.experimental import pallas as pl
from jax.experimental.pallas import tpu as pltpu
from jax.sharding import Mesh
from jax.sharding import PartitionSpec as P

HEAD_DIM = 128
LAT = 16
C1 = 384
F = 4
EPSILON = 1e-06

SEQ = ("y", "zh", "core")
BLK = ("zl", "x")
HEAD = ("zh", "zl", "x")
SHARD = SEQ + BLK

TILE = 1536
SUB = 256
CHUNK = 768
NT = (((1,), (1,)), ((), ()))


def mesh_index(axes):
    index = 0
    for axis in axes:
        index = index * lax.axis_size(axis) + lax.axis_index(axis)
    return index


def lane_max(s):
    t = s[:, :128]
    for j in range(1, s.shape[1] // 128):
        t = jnp.maximum(t, s[:, j * 128 : (j + 1) * 128])
    return jnp.max(t, axis=1, keepdims=True)


def flash_kernel(first, last, n_kv, half, *refs):
    q_ref, refs = refs[0], refs[1:]
    if not last:
        qx_ref, refs = refs[0], refs[1:]
    kv_refs, refs = refs[:n_kv], refs[n_kv:]
    if not first:
        st_ref, refs = refs[0], refs[1:]
    if last:
        w_ref, u_ref = refs
        query = q_ref[...]
        own = w_ref[:, pl.ds(pl.multiple_of(mesh_index(HEAD) * HEAD_DIM, HEAD_DIM), HEAD_DIM)]
        weight = jnp.concatenate([own, jnp.zeros_like(own)], axis=0)
    else:
        (so_ref,) = refs
        query = jnp.where(pl.program_id(0) < half, q_ref[...], qx_ref[...])
    scale = math.log2(math.e) / math.sqrt(HEAD_DIM)
    qf = query.astype(jnp.float32) * scale
    q_hi = qf.astype(jnp.bfloat16)
    q_lo = (qf - q_hi.astype(jnp.float32)).astype(jnp.bfloat16)
    q = jnp.concatenate([q_hi, q_lo], axis=1)
    subs = TILE // SUB
    tops, accs = [], []
    for r in range(subs):
        if first:
            tops.append(jnp.full((SUB, 128), -1e30, jnp.float32))
            accs.append(jnp.zeros((SUB, 256), jnp.float32))
        else:
            st = st_ref[pl.ds(r * SUB, SUB), :]
            acc_l = st[:, 128:]
            lane = lax.broadcasted_iota(jnp.int32, (SUB, 128), 1)
            total = jnp.max(jnp.where(lane < 64, acc_l, -1e30), axis=1, keepdims=True)
            top = jnp.max(jnp.where(lane < 64, -1e30, acc_l), axis=1, keepdims=True)
            tops.append(jnp.broadcast_to(top, (SUB, 128)))
            accs.append(
                jnp.concatenate([st[:, :128], jnp.broadcast_to(total, (SUB, 128))], axis=1)
            )
    items = [
        (r, b, c)
        for r in range(subs)
        for b in range(n_kv)
        for c in range(kv_refs[b].shape[0] // CHUNK)
    ]
    ones = jnp.ones((CHUNK, 128), jnp.bfloat16)

    def score(item):
        r, b, c = item
        k = kv_refs[b][pl.ds(c * CHUNK, CHUNK), :128]
        return lax.dot_general(
            q[r * SUB : (r + 1) * SUB],
            jnp.concatenate([k, k], axis=1),
            NT,
            preferred_element_type=jnp.float32,
        )

    s = score(items[0])
    for n, (r, b, c) in enumerate(items):
        following = score(items[n + 1]) if n + 1 < len(items) else None
        top = jnp.maximum(tops[r], lane_max(s))
        p = jnp.exp2(s - top[:, :1]).astype(jnp.bfloat16)
        fade = jnp.exp2(tops[r] - top)
        v = jnp.concatenate([kv_refs[b][pl.ds(c * CHUNK, CHUNK), 128:], ones], axis=1)
        accs[r] = accs[r] * jnp.concatenate([fade, fade], axis=1) + jnp.dot(
            p, v, preferred_element_type=jnp.float32
        )
        tops[r] = top
        s = following
    lane = lax.broadcasted_iota(jnp.int32, (SUB, 128), 1)
    for r in range(subs):
        if last:
            total = accs[r][:, 128:]
            mixed = (accs[r][:, :128] / total).astype(jnp.bfloat16)
            u = lax.dot_general(mixed, weight, NT, preferred_element_type=jnp.float32)
            u_ref[pl.ds(r * SUB, SUB), :] = jnp.where(lane < 64, u, tops[r] + jnp.log2(total))
        else:
            so_ref[pl.ds(r * SUB, SUB), :] = jnp.concatenate(
                [accs[r][:, :128], jnp.where(lane < 64, accs[r][:, 128:], tops[r])], axis=1
            )


def flash(q_own, q_oth, kvs, state=None):
    rows = q_oth.shape[0]
    half = rows // TILE
    keys = sum(kv.shape[0] for kv in kvs)
    in_specs = [
        pl.BlockSpec((TILE, 128), lambda i: (jnp.minimum(i, half - 1), 2)),
        pl.BlockSpec((TILE, 128), lambda i: (jnp.maximum(i - half, 0), 0)),
    ]
    in_specs += [pl.BlockSpec((kv.shape[0], 256), lambda i: (0, 0)) for kv in kvs]
    args = [q_own, q_oth, *kvs]
    if state is not None:
        in_specs.append(pl.BlockSpec((TILE, 256), lambda i: (i, 0)))
        args.append(state)
    return pl.pallas_call(
        functools.partial(flash_kernel, state is None, False, len(kvs), half),
        grid=(2 * half,),
        in_specs=in_specs,
        out_specs=pl.BlockSpec((TILE, 256), lambda i: (i, 0)),
        out_shape=jax.ShapeDtypeStruct((2 * rows, 256), jnp.float32),
        compiler_params=pltpu.CompilerParams(vmem_limit_bytes=20 << 20),
        cost_estimate=flash_cost(2 * rows, keys),
    )(*args)


def flash_last(query, lane_block, kvs, state, half_at, weight):
    rows = query.shape[0]
    half = rows // TILE
    keys = sum(kv.shape[0] for kv in kvs)
    in_specs = [pl.BlockSpec((TILE, 128), lambda i: (i, lane_block))]
    in_specs += [pl.BlockSpec((kv.shape[0], 256), lambda i: (0, 0)) for kv in kvs]
    in_specs += [
        pl.BlockSpec((TILE, 256), lambda i: (i + half_at * half, 0)),
        pl.BlockSpec(weight.shape, lambda i: (0, 0)),
    ]
    return pl.pallas_call(
        functools.partial(flash_kernel, False, True, len(kvs), half),
        grid=(half,),
        in_specs=in_specs,
        out_specs=pl.BlockSpec((TILE, 128), lambda i: (i, 0)),
        out_shape=jax.ShapeDtypeStruct((rows, 128), jnp.float32),
        compiler_params=pltpu.CompilerParams(vmem_limit_bytes=20 << 20),
        cost_estimate=flash_cost(rows, keys),
    )(query, *kvs, state, weight)


def flash_cost(rows, keys):
    return pl.CostEstimate(
        flops=rows * keys * 1024, bytes_accessed=rows * 2048, transcendentals=rows * keys
    )


def inside(at, low, high, before, after):
    return ((at > low) | before) & ((at < high) | after)


def tail_kernel(
    near_ref,
    mine_ref,
    apart_ref,
    cells_ref,
    level_ref,
    scale_ref,
    mean_ref,
    w1_ref,
    b1_ref,
    gain_ref,
    mid_ref,
    w2_ref,
    b2_ref,
    den_ref,
    out_ref,
    vel,
    lat,
    den,
    first,
    act,
    wide,
    done,
    vecs,
):
    even = lax.axis_index("core") == 0
    at_row, at_col = mesh_index(SEQ), mesh_index(BLK)
    up, down = at_row > 0, at_row < lax.axis_size(SEQ) - 1
    before, after = at_col > 0, at_col < lax.axis_size(BLK) - 1
    above = jnp.where(even, apart_ref[...], near_ref[...])
    below = jnp.where(even, near_ref[...], apart_ref[...])
    for at, rows in enumerate((above, mine_ref[0:16, :], mine_ref[16:32, :], below)):
        turned = pltpu.roll(rows, 64, axis=1)
        for f in range(F):
            vel[f, at, 0:4, :] = rows[f * 4 : f * 4 + 4]
            vel[f, at, 4:8, :] = turned[f * 4 : f * 4 + 4]
    vecs[...] = jnp.zeros(vecs.shape, jnp.float32)
    vecs[0:1, 0:LAT] = scale_ref[...].reshape(1, LAT)
    vecs[8:9, 0:LAT] = mean_ref[...].reshape(1, LAT)
    base = vecs[...]
    tiled = base + pltpu.roll(base, LAT, axis=1)
    tiled = tiled + pltpu.roll(tiled, 2 * LAT, axis=1)
    scale, mean = tiled[0:1, 0:64], tiled[8:9, 0:64]
    denoised = cells_ref[2:6, :, :, 0:64] - level_ref[0] * vel[:, :, :, 0:64]
    row = lax.broadcasted_iota(jnp.int32, denoised.shape, 1)
    col = lax.broadcasted_iota(jnp.int32, denoised.shape, 2)
    kept = inside(row, 0, 3, up, down) & inside(col, 0, 7, before, after)
    latent = jnp.where(kept, denoised * scale + mean, 0.0)
    for k in range(4):
        part = jnp.concatenate([denoised, denoised], axis=3).reshape(F * 32, 128)
        part = pltpu.roll(part, 128 - LAT * k, axis=1) if k else part
        part = part.reshape(F, 4, 8, 128)
        for f in range(F):
            for r in range(2):
                rows = pl.ds(8 * (k % 2) + 2 * r + k // 2, 8, stride=16)
                den[f, rows, :] = part[f, r + 1]
    den_ref[...] = den[:, 16:112, :].reshape(F, 12, 8, 128)[:, :, 0:4, 0:LAT]
    lat[...] = jnp.zeros(lat.shape, jnp.float32)
    lat[0:2, :, 0:8, 0:64] = cells_ref[0:2, :, :, 0:64]
    lat[2:6, :, 0:8, 0:64] = latent.astype(jnp.bfloat16).astype(jnp.float32)
    here = lat[:, :, 0:8, :].reshape(192, 128)
    right = pltpu.roll(lat[:, :, 1:9, :].reshape(192, 128), 64, axis=1)
    lane = lax.broadcasted_iota(jnp.int32, (192, 128), 1)
    pair = jnp.where(lane < 64, here, right).reshape(6, 4, 8, 128)
    lower = jnp.concatenate([pair[:, 1:4], pair[:, 3:4]], axis=1)
    window = jnp.concatenate([pair, lower], axis=3).reshape(192, 256).astype(jnp.bfloat16)
    parts = C1 // 128
    for k in range(parts):
        act[k, 0:2, :, 0:16, :] = mid_ref[:, :, :, pl.ds(k * 128, 128)]
    gain = gain_ref[...].reshape(1, C1)
    for p in range(2):
        for q in range(2):
            lanes = pl.ds((2 * p + q) * C1, C1)
            value = b1_ref[...].reshape(1, C1)
            for t in range(3):
                value = value + jnp.dot(
                    window[t * 32 : t * 32 + 128],
                    w1_ref[t, :, lanes],
                    preferred_element_type=jnp.float32,
                )
            power = jnp.mean(value * value, axis=1, keepdims=True)
            normed = value * lax.rsqrt(power + EPSILON) * gain
            active = (normed / (1.0 + jnp.exp(-normed))).reshape(F, 32, C1)
            at = lax.broadcasted_iota(jnp.int32, (32, C1), 0)
            kept = inside(2 * (at // 8) + p, 0, 5, up, down)
            kept = kept & inside(2 * (at % 8) + q, 0, 13, before, after)
            active = jnp.where(kept, active, 0.0)
            value = value.reshape(F, 4, 8, C1)
            active = active.reshape(F, 4, 8, C1)
            for r in range(3):
                cols = pl.ds(q, 8, stride=2)
                for k in range(parts):
                    part = slice(k * 128, k * 128 + 128)
                    for f in range(F):
                        first[k, f, 2 * r + p, cols, :] = value[f, r, :, part]
                        act[k, f + 2, 2 * r + p, cols, :] = active[f, r, :, part]
    for v in range(3):
        for k in range(parts):
            wide[:, :, :, pl.ds(v * C1 + k * 128, 128)] = act[k, :, :, pl.ds(v, 16), :].astype(
                jnp.bfloat16
            )
    middle = [first[k, :, 1:5, pl.ds(1, 16), :].reshape(256, 128) for k in range(parts)]
    total = jnp.concatenate(middle, axis=1) + b2_ref[...].reshape(1, C1)
    for tap in range(9):
        t, u = divmod(tap, 3)
        rows = wide[t : t + 4, u : u + 4].reshape(256, 3 * C1)
        total = total + jnp.dot(rows, w2_ref[tap], preferred_element_type=jnp.float32)
    for k in range(parts):
        for f in range(F):
            for i in range(4):
                at = f * 64 + i * 16
                done[k, f, pl.ds(i, 16, stride=8), :] = total[at : at + 16, k * 128 : k * 128 + 128]
        cells = done[k, :, 0:96, :].reshape(F, 12, 8, 128)[:, :, 0:4]
        out_ref[:, :, :, pl.ds(k * 128, 128)] = cells.astype(jnp.bfloat16)


def tail(*args):
    specs = [pl.BlockSpec(memory_space=pltpu.VMEM)] * len(args)
    specs[4] = pl.BlockSpec(memory_space=pltpu.SMEM)
    return pl.pallas_call(
        tail_kernel,
        in_specs=specs,
        out_specs=[pl.BlockSpec(memory_space=pltpu.VMEM)] * 2,
        out_shape=[
            jax.ShapeDtypeStruct((F, 12, 4, LAT), jnp.float32),
            jax.ShapeDtypeStruct((F, 12, 4, C1), jnp.bfloat16),
        ],
        scratch_shapes=[
            pltpu.VMEM((F, 4, 8, 128), jnp.float32),
            pltpu.VMEM((6, 4, 16, 128), jnp.float32),
            pltpu.VMEM((F, 128, 128), jnp.float32),
            pltpu.VMEM((C1 // 128, F, 6, 24, 128), jnp.float32),
            pltpu.VMEM((C1 // 128, 6, 6, 24, 128), jnp.float32),
            pltpu.VMEM((6, 6, 16, 3 * C1), jnp.bfloat16),
            pltpu.VMEM((C1 // 128, F, 128, 128), jnp.float32),
            pltpu.VMEM((16, 128), jnp.float32),
        ],
        compiler_params=pltpu.CompilerParams(vmem_limit_bytes=32 << 20),
    )(*args)


def window_kernel(w_ref, out_ref):
    out_ref[...] = jnp.zeros(out_ref.shape, out_ref.dtype)
    for t in range(3):
        for u in range(3):
            for v in range(3):
                taps = w_ref[t, u, v]
                for p in range(2):
                    for q in range(2):
                        (dr, a), (dc, b) = divmod(p + u, 2), divmod(q + v, 2)
                        at = dr * 128 + dc * 64 + a * 32 + b * 16
                        out_ref[t, pl.ds(at, LAT), pl.ds((2 * p + q) * C1, C1)] = taps


def window_weights(weight):
    return pl.pallas_call(
        window_kernel,
        out_shape=jax.ShapeDtypeStruct((3, 16 * LAT, 4 * C1), jnp.bfloat16),
        compiler_params=pltpu.CompilerParams(vmem_limit_bytes=16 << 20),
    )(weight)


def put_frames(ref, rows, tokens):
    count = tokens[0].shape[0]
    low = lax.broadcasted_iota(jnp.int32, (count, 128), 1) < 64
    for i in range(2):
        for h in range(2):
            one = tokens[i + 2 * h]
            two = pltpu.roll(tokens[i + 4], 64, axis=1) if h == 0 else jnp.zeros_like(one)
            ref[i, pl.ds(rows + h * count, count), 384:512] = jnp.where(low, one, two)


def get_frames(ref, rows, count):
    out = {}
    for i in range(2):
        for h in range(2):
            both = ref[i, pl.ds(rows + h * count, count), 384:512]
            out[i + 2 * h] = both
            if h == 0:
                out[i + 4] = pltpu.roll(both, 64, axis=1)
    return [out[f] for f in range(6)]


def edge_rows_kernel(noisy_ref, cache_ref, mid_ref, tok_ref, down_ref, up_ref, cells):
    cells[...] = jnp.zeros(cells.shape, jnp.float32)
    cells[0:2, :, 0:12, 0:LAT] = cache_ref[...].astype(jnp.float32)
    cells[2:6, :, 0:12, 0:LAT] = noisy_ref[...]
    lane = lax.broadcasted_iota(jnp.int32, (8, 128), 1)
    tokens = {}
    for r in range(2):
        for f in range(6):
            token = jnp.zeros((8, 128), jnp.float32)
            for k in range(4):
                part = cells[f, 2 * r + k // 2, pl.ds(k % 2, 8, stride=2), :]
                part = pltpu.roll(part, LAT * k, axis=1) if k else part
                token = jnp.where((lane >= LAT * k) & (lane < LAT * k + LAT), part, token)
            tok_ref[f, r] = token
            tokens[f, r] = token
    for ref, row, r in ((down_ref, 3, 1), (up_ref, 0, 0)):
        ref[...] = jnp.zeros(ref.shape, jnp.float32)
        ref[:, 0:12, 0:C1] = mid_ref[:, row].astype(jnp.float32)
        put_frames(ref, 0, [tokens[f, r] for f in range(6)])


def edge_cols_kernel(tok_ref, mid_ref, above_ref, below_ref, toks, mids, right_ref, left_ref):
    above, below = get_frames(above_ref, 0, 8), get_frames(below_ref, 0, 8)
    for f in range(6):
        toks[f, 0] = above[f]
        toks[f, 1] = tok_ref[f, 0]
        toks[f, 2] = tok_ref[f, 1]
        toks[f, 3] = below[f]
    mids[...] = jnp.zeros(mids.shape, jnp.float32)
    mids[:, 0, 0:12, :] = above_ref[:, 0:12, 0:C1]
    mids[:, 1:5, 0:12, :] = mid_ref[...].astype(jnp.float32)
    mids[:, 5, 0:12, :] = below_ref[:, 0:12, 0:C1]
    for ref, token, col in ((right_ref, 5, 11), (left_ref, 0, 0)):
        ref[...] = jnp.zeros(ref.shape, jnp.float32)
        for i in range(2):
            for row in range(6):
                ref[i, pl.ds(row, 1), 0:C1] = mids[i, row, pl.ds(col, 1), :]
        for r in range(4):
            put_rows(ref, r, [toks[f, r, pl.ds(token, 1), :] for f in range(6)])


def put_rows(ref, r, tokens):
    low = lax.broadcasted_iota(jnp.int32, (1, 128), 1) < 64
    for i in range(2):
        for h in range(2):
            one = tokens[i + 2 * h]
            two = pltpu.roll(tokens[i + 4], 64, axis=1) if h == 0 else jnp.zeros_like(one)
            ref[i, pl.ds(4 * h + r, 1), 384:512] = jnp.where(low, one, two)


def place_kernel(toks, mids, left_ref, right_ref, cells_ref, cache_ref):
    cells_ref[...] = jnp.zeros(cells_ref.shape, jnp.float32)
    cache_ref[...] = jnp.zeros(cache_ref.shape, jnp.float32)
    for f in range(6):
        for r in range(4):
            cells_ref[f, r, 1:7, :] = toks[f, r, 0:6, :]
    cache_ref[:, :, 1:13, :] = mids[:, :, 0:12, :]
    for ref, token, col in ((left_ref, 0, 0), (right_ref, 7, 13)):
        frames = get_frames(ref, 0, 4)
        for f in range(6):
            for r in range(4):
                cells_ref[f, r, pl.ds(token, 1), :] = frames[f][r : r + 1]
        for i in range(2):
            for row in range(6):
                cache_ref[i, row, pl.ds(col, 1), :] = ref[i, pl.ds(row, 1), 0:C1]


def small_call(kernel, shapes, scratch=()):
    return pl.pallas_call(
        kernel,
        out_shape=[jax.ShapeDtypeStruct(shape, jnp.float32) for shape in shapes],
        scratch_shapes=[pltpu.VMEM(shape, jnp.float32) for shape in scratch],
        compiler_params=pltpu.CompilerParams(vmem_limit_bytes=8 << 20),
    )


def along(axis, step):
    count = lax.axis_size(axis)
    return [(i, i + step) for i in range(count) if 0 <= i + step < count]


def halo_rows(noisy, cache_in, cache_mid):
    edge = (2, 16, 512)
    toks, down, up = small_call(
        edge_rows_kernel, [(6, 2, 8, 128), edge, edge], [(6, 4, 16, 128)]
    )(noisy, cache_in, cache_mid)
    above = lax.ppermute(down, SEQ, along(SEQ, 1))
    below = lax.ppermute(up, SEQ, along(SEQ, -1))
    side = (2, 8, 512)
    return small_call(edge_cols_kernel, [(6, 4, 8, 128), (2, 6, 16, C1), side, side])(
        toks, cache_mid, above, below
    )


def pack_kernel(q_ref, k_ref, v_ref, out_ref):
    for h in range(out_ref.shape[0]):
        lanes = pl.ds(h * HEAD_DIM, HEAD_DIM)
        out_ref[h, :, 0:128] = k_ref[:, lanes]
        out_ref[h, :, 128:256] = v_ref[:, lanes]
        out_ref[h, :, 256:384] = q_ref[:, lanes]


def pack(query_vectors, key_vectors, value_vectors):
    tokens, width = query_vectors.shape
    heads = width // HEAD_DIM
    block = pl.BlockSpec((tokens, width // 2), lambda i: (0, i))
    return pl.pallas_call(
        pack_kernel,
        grid=(2,),
        in_specs=[block] * 3,
        out_specs=pl.BlockSpec((heads // 2, tokens, 3 * HEAD_DIM), lambda i: (i, 0, 0)),
        out_shape=jax.ShapeDtypeStruct((heads, tokens, 3 * HEAD_DIM), jnp.bfloat16),
    )(query_vectors, key_vectors, value_vectors)


def merge_kernel(own_ref, oth_ref, out_ref, vel_ref, piece_ref):
    own, oth = own_ref[...], oth_ref[...]
    gap = pltpu.roll(oth - own, 64, axis=1)
    share = 1.0 / (1.0 + jnp.exp2(gap))
    vel = own * share + oth * (1.0 - share)
    lane = lax.broadcasted_iota(jnp.int32, vel.shape, 1)
    vel_ref[...] = jnp.where(lane < 64, vel, pltpu.roll(vel, 64, axis=1))
    low = lax.broadcasted_iota(jnp.int32, (16, 128), 1) < 64
    zero = jnp.zeros((16, 128), jnp.float32)

    def column(r, at):
        if at < 0 or at >= 48:
            return zero
        return vel_ref[pl.ds(r * 48 + at, 16, stride=96), :]

    for b in range(8):
        for r in range(2):
            for c in range(4):
                at = 6 * b - 1 + c
                both = jnp.where(low, column(r, at), column(r, at + 4))
                for y in range(4):
                    piece_ref[y, b, pl.ds(r * 16 + c, 4, stride=4), :] = both[y * 4 : y * 4 + 4]
    out_ref[...] = piece_ref[...].astype(jnp.bfloat16)


def merge(own, oth):
    rows = own.shape[0]
    whole = pl.BlockSpec((rows, 128), lambda: (0, 0))
    shape = (4, 8, 32, 128)
    return pl.pallas_call(
        merge_kernel,
        in_specs=[whole, whole],
        out_specs=pl.BlockSpec(shape, lambda: (0, 0, 0, 0)),
        out_shape=jax.ShapeDtypeStruct(shape, jnp.bfloat16),
        scratch_shapes=[
            pltpu.VMEM((rows, 128), jnp.float32),
            pltpu.VMEM(shape, jnp.float32),
        ],
        compiler_params=pltpu.CompilerParams(vmem_limit_bytes=24 << 20),
    )(own, oth)


def head_sum_kernel(parts_ref, mine_ref, near_ref, apart_ref):
    total = parts_ref[0].astype(jnp.float32)
    for h in range(1, parts_ref.shape[0]):
        total = total + parts_ref[h].astype(jnp.float32)
    mine_ref[...] = total
    even = lax.axis_index("core") == 0
    near_ref[...] = jnp.where(even, total[16:32], total[0:16])
    apart_ref[...] = jnp.where(even, total[0:16], total[16:32])


def head_sum(parts):
    return small_call(head_sum_kernel, [(32, 128), (16, 128), (16, 128)])(parts)


def attention(query_vectors, key_vectors, value_vectors, weight_head, inputs):
    packed = pack(query_vectors, key_vectors, value_vectors)
    packed, inputs = lax.optimization_barrier((packed, inputs))
    noisy, cache_in, cache_mid, weight_in = inputs
    rows = halo_rows(noisy, cache_in, cache_mid)
    weight_first = window_weights(weight_in)
    heads, tokens = packed.shape[:2]
    moved = lax.all_to_all(packed, HEAD, split_axis=0, concat_axis=0, tiled=True)
    moved = moved.reshape(heads * tokens, 3 * HEAD_DIM)
    swap = [(0, 1), (1, 0)]
    right = [(i, (i + 1) % 4) for i in range(4)]
    left = [((i + 1) % 4, i) for i in range(4)]
    mid = moved.shape[0] // 2
    a, b, q_own = moved[:mid, :256], moved[mid:, :256], moved[:, 256:]
    a, b, q_own, rows, weight_first = lax.optimization_barrier((a, b, q_own, rows, weight_first))
    left_a = lax.ppermute(a, "y", right)
    right_b = lax.ppermute(b, "y", left)
    q_oth = lax.ppermute(q_own, "core", swap)
    state = flash(moved, q_oth, [moved])
    toks, mids, to_right, to_left = rows
    state, a, b, to_right = lax.optimization_barrier((state, a, b, to_right))
    left_b = lax.ppermute(b, "y", right)
    right_a = lax.ppermute(a, "y", left)
    before = lax.ppermute(to_right, BLK, along(BLK, 1))
    state = flash(moved, q_oth, [left_a, right_b], state)
    state, left_a, right_b, to_left = lax.optimization_barrier((state, left_a, right_b, to_left))
    after = lax.ppermute(to_left, BLK, along(BLK, -1))
    borders = small_call(place_kernel, [(6, 4, 8, 128), (2, 6, 16, C1)])(
        toks, mids, before, after
    )
    far = [lax.ppermute(left_a, "y", right), lax.ppermute(right_b, "y", left)]
    state = flash(moved, q_oth, [left_b, right_a], state)
    weight = weight_head.T
    oth = flash_last(q_oth, 0, far, state, 1, weight)
    oth, state = lax.optimization_barrier((oth, state))
    oth = lax.ppermute(oth, "core", swap)
    own = flash_last(moved, 2, far, state, 0, weight)
    partial = merge(own, oth).reshape(heads, 32, 128)
    parts = lax.all_to_all(partial, HEAD, split_axis=0, concat_axis=0, tiled=True)
    return head_sum(parts), (*borders, weight_first)


def shards(
    query_vectors,
    key_vectors,
    value_vectors,
    weight_head,
    noisy_latent,
    noise_level,
    latent_mean,
    latent_scale,
    cache_in,
    weight_in,
    bias_in,
    norm_gain,
    cache_mid,
    weight_mid,
    bias_mid,
):
    (mine, near, apart), (cells, cache_second, weight_first) = attention(
        query_vectors,
        key_vectors,
        value_vectors,
        weight_head,
        (noisy_latent, cache_in, cache_mid, weight_in),
    )

    count = lax.axis_size(SEQ)
    near = lax.ppermute(near, SEQ, [(i, i ^ 1) for i in range(count)])
    pairs = [(i, i + 1) for i in range(1, count - 1, 2)]
    pairs += [(j, i) for i, j in pairs]
    apart = lax.ppermute(apart, SEQ, pairs)
    denoised, features = tail(
        near,
        mine,
        apart,
        cells,
        noise_level,
        latent_scale,
        latent_mean,
        weight_first,
        bias_in,
        norm_gain,
        cache_second,
        weight_mid.reshape(9, 3 * C1, C1),
        bias_mid,
    )
    return denoised.transpose(0, 2, 1, 3), features.transpose(0, 2, 1, 3)


def solution(mesh):
    inner = Mesh(mesh.devices.reshape(4, 4, 2, 2, 4), SHARD)
    tokens, tile = P(SHARD, None), P(None, SEQ, BLK, None)
    in_specs = (
        tokens,
        tokens,
        tokens,
        P(),
        tile,
        P(),
        P(),
        P(),
        tile,
        P(),
        P(),
        P(),
        tile,
        P(),
        P(),
    )
    return jax.shard_map(
        shards, mesh=inner, in_specs=in_specs, out_specs=(tile, tile), check_vma=False
    )
```

```python
import functools
import math

import jax
import jax.numpy as jnp
from jax import lax
from jax.experimental import pallas as pl
from jax.experimental.pallas import tpu as pltpu
from jax.sharding import Mesh
from jax.sharding import PartitionSpec as P

HEAD_DIM = 128
LAT = 16
C1 = 384
F = 4
EPSILON = 1e-06

SEQ = ("y", "zh", "core")
BLK = ("zl", "x")
HEAD = ("zh", "zl", "x")
SHARD = SEQ + BLK

TILE = 1536
SUB = 256
CHUNK = 768
NT = (((1,), (1,)), ((), ()))


def mesh_index(axes):
    index = 0
    for axis in axes:
        index = index * lax.axis_size(axis) + lax.axis_index(axis)
    return index


def lane_max(s):
    t = s[:, :128]
    for j in range(1, s.shape[1] // 128):
        t = jnp.maximum(t, s[:, j * 128 : (j + 1) * 128])
    return jnp.max(t, axis=1, keepdims=True)


def flash_kernel(first, last, n_kv, half, *refs):
    q_ref, refs = refs[0], refs[1:]
    if not last:
        qx_ref, refs = refs[0], refs[1:]
    kv_refs, refs = refs[:n_kv], refs[n_kv:]
    if not first:
        st_ref, refs = refs[0], refs[1:]
    if last:
        w_ref, u_ref = refs
        query = q_ref[...]
        own = w_ref[:, pl.ds(pl.multiple_of(mesh_index(HEAD) * HEAD_DIM, HEAD_DIM), HEAD_DIM)]
        weight = jnp.concatenate([own, jnp.zeros_like(own)], axis=0)
    else:
        (so_ref,) = refs
        query = jnp.where(pl.program_id(0) < half, q_ref[...], qx_ref[...])
    scale = math.log2(math.e) / math.sqrt(HEAD_DIM)
    qf = query.astype(jnp.float32) * scale
    q_hi = qf.astype(jnp.bfloat16)
    q_lo = (qf - q_hi.astype(jnp.float32)).astype(jnp.bfloat16)
    q = jnp.concatenate([q_hi, q_lo], axis=1)
    subs = TILE // SUB
    tops, accs = [], []
    for r in range(subs):
        if first:
            tops.append(jnp.full((SUB, 128), -1e30, jnp.float32))
            accs.append(jnp.zeros((SUB, 256), jnp.float32))
        else:
            st = st_ref[pl.ds(r * SUB, SUB), :]
            acc_l = st[:, 128:]
            lane = lax.broadcasted_iota(jnp.int32, (SUB, 128), 1)
            total = jnp.max(jnp.where(lane < 64, acc_l, -1e30), axis=1, keepdims=True)
            top = jnp.max(jnp.where(lane < 64, -1e30, acc_l), axis=1, keepdims=True)
            tops.append(jnp.broadcast_to(top, (SUB, 128)))
            accs.append(
                jnp.concatenate([st[:, :128], jnp.broadcast_to(total, (SUB, 128))], axis=1)
            )
    items = [
        (r, b, c)
        for r in range(subs)
        for b in range(n_kv)
        for c in range(kv_refs[b].shape[0] // CHUNK)
    ]
    ones = jnp.ones((CHUNK, 128), jnp.bfloat16)

    def score(item):
        r, b, c = item
        k = kv_refs[b][pl.ds(c * CHUNK, CHUNK), :128]
        return lax.dot_general(
            q[r * SUB : (r + 1) * SUB],
            jnp.concatenate([k, k], axis=1),
            NT,
            preferred_element_type=jnp.float32,
        )

    s = score(items[0])
    for n, (r, b, c) in enumerate(items):
        following = score(items[n + 1]) if n + 1 < len(items) else None
        top = jnp.maximum(tops[r], lane_max(s))
        p = jnp.exp2(s - top[:, :1]).astype(jnp.bfloat16)
        fade = jnp.exp2(tops[r] - top)
        v = jnp.concatenate([kv_refs[b][pl.ds(c * CHUNK, CHUNK), 128:], ones], axis=1)
        accs[r] = accs[r] * jnp.concatenate([fade, fade], axis=1) + jnp.dot(
            p, v, preferred_element_type=jnp.float32
        )
        tops[r] = top
        s = following
    lane = lax.broadcasted_iota(jnp.int32, (SUB, 128), 1)
    for r in range(subs):
        if last:
            total = accs[r][:, 128:]
            mixed = (accs[r][:, :128] / total).astype(jnp.bfloat16)
            u = lax.dot_general(mixed, weight, NT, preferred_element_type=jnp.float32)
            u_ref[pl.ds(r * SUB, SUB), :] = jnp.where(lane < 64, u, tops[r] + jnp.log2(total))
        else:
            so_ref[pl.ds(r * SUB, SUB), :] = jnp.concatenate(
                [accs[r][:, :128], jnp.where(lane < 64, accs[r][:, 128:], tops[r])], axis=1
            )


def flash(q_own, q_oth, kvs, state=None):
    rows = q_oth.shape[0]
    half = rows // TILE
    keys = sum(kv.shape[0] for kv in kvs)
    in_specs = [
        pl.BlockSpec((TILE, 128), lambda i: (jnp.minimum(i, half - 1), 2)),
        pl.BlockSpec((TILE, 128), lambda i: (jnp.maximum(i - half, 0), 0)),
    ]
    in_specs += [pl.BlockSpec((kv.shape[0], 256), lambda i: (0, 0)) for kv in kvs]
    args = [q_own, q_oth, *kvs]
    if state is not None:
        in_specs.append(pl.BlockSpec((TILE, 256), lambda i: (i, 0)))
        args.append(state)
    return pl.pallas_call(
        functools.partial(flash_kernel, state is None, False, len(kvs), half),
        grid=(2 * half,),
        in_specs=in_specs,
        out_specs=pl.BlockSpec((TILE, 256), lambda i: (i, 0)),
        out_shape=jax.ShapeDtypeStruct((2 * rows, 256), jnp.float32),
        compiler_params=pltpu.CompilerParams(vmem_limit_bytes=20 << 20),
        cost_estimate=flash_cost(2 * rows, keys),
    )(*args)


def flash_last(query, lane_block, kvs, state, half_at, weight):
    rows = query.shape[0]
    half = rows // TILE
    keys = sum(kv.shape[0] for kv in kvs)
    in_specs = [pl.BlockSpec((TILE, 128), lambda i: (i, lane_block))]
    in_specs += [pl.BlockSpec((kv.shape[0], 256), lambda i: (0, 0)) for kv in kvs]
    in_specs += [
        pl.BlockSpec((TILE, 256), lambda i: (i + half_at * half, 0)),
        pl.BlockSpec(weight.shape, lambda i: (0, 0)),
    ]
    return pl.pallas_call(
        functools.partial(flash_kernel, False, True, len(kvs), half),
        grid=(half,),
        in_specs=in_specs,
        out_specs=pl.BlockSpec((TILE, 128), lambda i: (i, 0)),
        out_shape=jax.ShapeDtypeStruct((rows, 128), jnp.float32),
        compiler_params=pltpu.CompilerParams(vmem_limit_bytes=20 << 20),
        cost_estimate=flash_cost(rows, keys),
    )(query, *kvs, state, weight)


def flash_cost(rows, keys):
    return pl.CostEstimate(
        flops=rows * keys * 1024, bytes_accessed=rows * 2048, transcendentals=rows * keys
    )


def inside(at, low, high, before, after):
    return ((at > low) | before) & ((at < high) | after)


def tail_kernel(
    near_ref,
    mine_ref,
    apart_ref,
    toks,
    mids,
    before_ref,
    after_ref,
    level_ref,
    scale_ref,
    mean_ref,
    w1_ref,
    b1_ref,
    gain_ref,
    w2_ref,
    b2_ref,
    den_ref,
    out_ref,
    vel,
    lat,
    den,
    first,
    act,
    wide,
    done,
    vecs,
    cells_ref,
    mid_ref,
):
    place(toks, mids, before_ref, after_ref, cells_ref, mid_ref)
    even = lax.axis_index("core") == 0
    at_row, at_col = mesh_index(SEQ), mesh_index(BLK)
    up, down = at_row > 0, at_row < lax.axis_size(SEQ) - 1
    before, after = at_col > 0, at_col < lax.axis_size(BLK) - 1
    above = jnp.where(even, apart_ref[...], near_ref[...])
    below = jnp.where(even, near_ref[...], apart_ref[...])
    for at, rows in enumerate((above, mine_ref[0:16, :], mine_ref[16:32, :], below)):
        turned = pltpu.roll(rows, 64, axis=1)
        for f in range(F):
            vel[f, at, 0:4, :] = rows[f * 4 : f * 4 + 4]
            vel[f, at, 4:8, :] = turned[f * 4 : f * 4 + 4]
    vecs[...] = jnp.zeros(vecs.shape, jnp.float32)
    vecs[0:1, 0:LAT] = scale_ref[...].reshape(1, LAT)
    vecs[8:9, 0:LAT] = mean_ref[...].reshape(1, LAT)
    base = vecs[...]
    tiled = base + pltpu.roll(base, LAT, axis=1)
    tiled = tiled + pltpu.roll(tiled, 2 * LAT, axis=1)
    scale, mean = tiled[0:1, 0:64], tiled[8:9, 0:64]
    denoised = cells_ref[2:6, :, :, 0:64] - level_ref[0] * vel[:, :, :, 0:64]
    row = lax.broadcasted_iota(jnp.int32, denoised.shape, 1)
    col = lax.broadcasted_iota(jnp.int32, denoised.shape, 2)
    kept = inside(row, 0, 3, up, down) & inside(col, 0, 7, before, after)
    latent = jnp.where(kept, denoised * scale + mean, 0.0)
    for k in range(4):
        part = jnp.concatenate([denoised, denoised], axis=3).reshape(F * 32, 128)
        part = pltpu.roll(part, 128 - LAT * k, axis=1) if k else part
        part = part.reshape(F, 4, 8, 128)
        for f in range(F):
            for r in range(2):
                rows = pl.ds(8 * (k % 2) + 2 * r + k // 2, 8, stride=16)
                den[f, rows, :] = part[f, r + 1]
    den_ref[...] = den[:, 16:112, :].reshape(F, 12, 8, 128)[:, :, 0:4, 0:LAT]
    lat[...] = jnp.zeros(lat.shape, jnp.float32)
    lat[0:2, :, 0:8, 0:64] = cells_ref[0:2, :, :, 0:64]
    lat[2:6, :, 0:8, 0:64] = latent.astype(jnp.bfloat16).astype(jnp.float32)
    here = lat[:, :, 0:8, :].reshape(192, 128)
    right = pltpu.roll(lat[:, :, 1:9, :].reshape(192, 128), 64, axis=1)
    lane = lax.broadcasted_iota(jnp.int32, (192, 128), 1)
    pair = jnp.where(lane < 64, here, right).reshape(6, 4, 8, 128)
    lower = jnp.concatenate([pair[:, 1:4], pair[:, 3:4]], axis=1)
    window = jnp.concatenate([pair, lower], axis=3).reshape(192, 256).astype(jnp.bfloat16)
    parts = C1 // 128
    for k in range(parts):
        act[k, 0:2, :, 0:16, :] = mid_ref[:, :, :, pl.ds(k * 128, 128)]
    gain = gain_ref[...].reshape(1, C1)
    for p in range(2):
        for q in range(2):
            lanes = pl.ds((2 * p + q) * C1, C1)
            value = b1_ref[...].reshape(1, C1)
            for t in range(3):
                value = value + jnp.dot(
                    window[t * 32 : t * 32 + 128],
                    w1_ref[t, :, lanes],
                    preferred_element_type=jnp.float32,
                )
            power = jnp.mean(value * value, axis=1, keepdims=True)
            normed = value * lax.rsqrt(power + EPSILON) * gain
            active = (normed / (1.0 + jnp.exp(-normed))).reshape(F, 32, C1)
            at = lax.broadcasted_iota(jnp.int32, (32, C1), 0)
            kept = inside(2 * (at // 8) + p, 0, 5, up, down)
            kept = kept & inside(2 * (at % 8) + q, 0, 13, before, after)
            active = jnp.where(kept, active, 0.0)
            value = value.reshape(F, 4, 8, C1)
            active = active.reshape(F, 4, 8, C1)
            for r in range(3):
                cols = pl.ds(q, 8, stride=2)
                for k in range(parts):
                    part = slice(k * 128, k * 128 + 128)
                    for f in range(F):
                        first[k, f, 2 * r + p, cols, :] = value[f, r, :, part]
                        act[k, f + 2, 2 * r + p, cols, :] = active[f, r, :, part]
    for v in range(3):
        for k in range(parts):
            wide[:, :, :, pl.ds(v * C1 + k * 128, 128)] = act[k, :, :, pl.ds(v, 16), :].astype(
                jnp.bfloat16
            )
    middle = [first[k, :, 1:5, pl.ds(1, 16), :].reshape(256, 128) for k in range(parts)]
    total = jnp.concatenate(middle, axis=1) + b2_ref[...].reshape(1, C1)
    for tap in range(9):
        t, u = divmod(tap, 3)
        rows = wide[t : t + 4, u : u + 4].reshape(256, 3 * C1)
        total = total + jnp.dot(rows, w2_ref[tap], preferred_element_type=jnp.float32)
    for k in range(parts):
        for f in range(F):
            for i in range(4):
                at = f * 64 + i * 16
                done[k, f, pl.ds(i, 16, stride=8), :] = total[at : at + 16, k * 128 : k * 128 + 128]
        cells = done[k, :, 0:96, :].reshape(F, 12, 8, 128)[:, :, 0:4]
        out_ref[:, :, :, pl.ds(k * 128, 128)] = cells.astype(jnp.bfloat16)


def tail(*args):
    specs = [pl.BlockSpec(memory_space=pltpu.VMEM)] * len(args)
    specs[7] = pl.BlockSpec(memory_space=pltpu.SMEM)
    return pl.pallas_call(
        tail_kernel,
        in_specs=specs,
        out_specs=[pl.BlockSpec(memory_space=pltpu.VMEM)] * 2,
        out_shape=[
            jax.ShapeDtypeStruct((F, 12, 4, LAT), jnp.float32),
            jax.ShapeDtypeStruct((F, 12, 4, C1), jnp.bfloat16),
        ],
        scratch_shapes=[
            pltpu.VMEM((F, 4, 8, 128), jnp.float32),
            pltpu.VMEM((6, 4, 16, 128), jnp.float32),
            pltpu.VMEM((F, 128, 128), jnp.float32),
            pltpu.VMEM((C1 // 128, F, 6, 24, 128), jnp.float32),
            pltpu.VMEM((C1 // 128, 6, 6, 24, 128), jnp.float32),
            pltpu.VMEM((6, 6, 16, 3 * C1), jnp.bfloat16),
            pltpu.VMEM((C1 // 128, F, 128, 128), jnp.float32),
            pltpu.VMEM((16, 128), jnp.float32),
            pltpu.VMEM((6, 4, 8, 128), jnp.float32),
            pltpu.VMEM((2, 6, 16, C1), jnp.float32),
        ],
        compiler_params=pltpu.CompilerParams(vmem_limit_bytes=32 << 20),
    )(*args)


def window_kernel(w_ref, out_ref):
    out_ref[...] = jnp.zeros(out_ref.shape, out_ref.dtype)
    for t in range(3):
        for u in range(3):
            for v in range(3):
                taps = w_ref[t, u, v]
                for p in range(2):
                    for q in range(2):
                        (dr, a), (dc, b) = divmod(p + u, 2), divmod(q + v, 2)
                        at = dr * 128 + dc * 64 + a * 32 + b * 16
                        out_ref[t, pl.ds(at, LAT), pl.ds((2 * p + q) * C1, C1)] = taps


def window_weights(weight):
    return pl.pallas_call(
        window_kernel,
        out_shape=jax.ShapeDtypeStruct((3, 16 * LAT, 4 * C1), jnp.bfloat16),
        compiler_params=pltpu.CompilerParams(vmem_limit_bytes=16 << 20),
    )(weight)


def put_frames(ref, rows, tokens):
    count = tokens[0].shape[0]
    low = lax.broadcasted_iota(jnp.int32, (count, 128), 1) < 64
    for i in range(2):
        for h in range(2):
            one = tokens[i + 2 * h]
            two = pltpu.roll(tokens[i + 4], 64, axis=1) if h == 0 else jnp.zeros_like(one)
            ref[i, pl.ds(rows + h * count, count), 384:512] = jnp.where(low, one, two)


def get_frames(ref, rows, count):
    out = {}
    for i in range(2):
        for h in range(2):
            both = ref[i, pl.ds(rows + h * count, count), 384:512]
            out[i + 2 * h] = both
            if h == 0:
                out[i + 4] = pltpu.roll(both, 64, axis=1)
    return [out[f] for f in range(6)]


def edge_rows_kernel(noisy_ref, cache_ref, mid_ref, tok_ref, down_ref, up_ref, cells):
    cells[...] = jnp.zeros(cells.shape, jnp.float32)
    cells[0:2, :, 0:12, 0:LAT] = cache_ref[...].astype(jnp.float32)
    cells[2:6, :, 0:12, 0:LAT] = noisy_ref[...]
    lane = lax.broadcasted_iota(jnp.int32, (8, 128), 1)
    tokens = {}
    for r in range(2):
        for f in range(6):
            token = jnp.zeros((8, 128), jnp.float32)
            for k in range(4):
                part = cells[f, 2 * r + k // 2, pl.ds(k % 2, 8, stride=2), :]
                part = pltpu.roll(part, LAT * k, axis=1) if k else part
                token = jnp.where((lane >= LAT * k) & (lane < LAT * k + LAT), part, token)
            tok_ref[f, r] = token
            tokens[f, r] = token
    for ref, row, r in ((down_ref, 3, 1), (up_ref, 0, 0)):
        ref[...] = jnp.zeros(ref.shape, jnp.float32)
        ref[:, 0:12, 0:C1] = mid_ref[:, row].astype(jnp.float32)
        put_frames(ref, 0, [tokens[f, r] for f in range(6)])


def edge_cols_kernel(tok_ref, mid_ref, above_ref, below_ref, toks, mids, right_ref, left_ref):
    above, below = get_frames(above_ref, 0, 8), get_frames(below_ref, 0, 8)
    for f in range(6):
        toks[f, 0] = above[f]
        toks[f, 1] = tok_ref[f, 0]
        toks[f, 2] = tok_ref[f, 1]
        toks[f, 3] = below[f]
    mids[...] = jnp.zeros(mids.shape, jnp.float32)
    mids[:, 0, 0:12, :] = above_ref[:, 0:12, 0:C1]
    mids[:, 1:5, 0:12, :] = mid_ref[...].astype(jnp.float32)
    mids[:, 5, 0:12, :] = below_ref[:, 0:12, 0:C1]
    for ref, token, col in ((right_ref, 5, 11), (left_ref, 0, 0)):
        ref[...] = jnp.zeros(ref.shape, jnp.float32)
        for i in range(2):
            for row in range(6):
                ref[i, pl.ds(row, 1), 0:C1] = mids[i, row, pl.ds(col, 1), :]
        for r in range(4):
            put_rows(ref, r, [toks[f, r, pl.ds(token, 1), :] for f in range(6)])


def put_rows(ref, r, tokens):
    low = lax.broadcasted_iota(jnp.int32, (1, 128), 1) < 64
    for i in range(2):
        for h in range(2):
            one = tokens[i + 2 * h]
            two = pltpu.roll(tokens[i + 4], 64, axis=1) if h == 0 else jnp.zeros_like(one)
            ref[i, pl.ds(4 * h + r, 1), 384:512] = jnp.where(low, one, two)


def place(toks, mids, left_ref, right_ref, cells_ref, cache_ref):
    cells_ref[...] = jnp.zeros(cells_ref.shape, jnp.float32)
    cache_ref[...] = jnp.zeros(cache_ref.shape, jnp.float32)
    for f in range(6):
        for r in range(4):
            cells_ref[f, r, 1:7, :] = toks[f, r, 0:6, :]
    cache_ref[:, :, 1:13, :] = mids[:, :, 0:12, :]
    for ref, token, col in ((left_ref, 0, 0), (right_ref, 7, 13)):
        frames = get_frames(ref, 0, 4)
        for f in range(6):
            for r in range(4):
                cells_ref[f, r, pl.ds(token, 1), :] = frames[f][r : r + 1]
        for i in range(2):
            for row in range(6):
                cache_ref[i, row, pl.ds(col, 1), :] = ref[i, pl.ds(row, 1), 0:C1]


def small_call(kernel, shapes, scratch=()):
    return pl.pallas_call(
        kernel,
        out_shape=[jax.ShapeDtypeStruct(shape, jnp.float32) for shape in shapes],
        scratch_shapes=[pltpu.VMEM(shape, jnp.float32) for shape in scratch],
        compiler_params=pltpu.CompilerParams(vmem_limit_bytes=8 << 20),
    )


def along(axis, step):
    count = lax.axis_size(axis)
    return [(i, i + step) for i in range(count) if 0 <= i + step < count]


def halo_rows(noisy, cache_in, cache_mid):
    edge = (2, 16, 512)
    toks, down, up = small_call(
        edge_rows_kernel, [(6, 2, 8, 128), edge, edge], [(6, 4, 16, 128)]
    )(noisy, cache_in, cache_mid)
    above = lax.ppermute(down, SEQ, along(SEQ, 1))
    below = lax.ppermute(up, SEQ, along(SEQ, -1))
    side = (2, 8, 512)
    return small_call(edge_cols_kernel, [(6, 4, 8, 128), (2, 6, 16, C1), side, side])(
        toks, cache_mid, above, below
    )


def pack_kernel(q_ref, k_ref, v_ref, out_ref):
    for h in range(out_ref.shape[0]):
        lanes = pl.ds(h * HEAD_DIM, HEAD_DIM)
        out_ref[h, :, 0:128] = k_ref[:, lanes]
        out_ref[h, :, 128:256] = v_ref[:, lanes]
        out_ref[h, :, 256:384] = q_ref[:, lanes]


def pack(query_vectors, key_vectors, value_vectors):
    tokens, width = query_vectors.shape
    heads = width // HEAD_DIM
    block = pl.BlockSpec((tokens, width // 2), lambda i: (0, i))
    return pl.pallas_call(
        pack_kernel,
        grid=(2,),
        in_specs=[block] * 3,
        out_specs=pl.BlockSpec((heads // 2, tokens, 3 * HEAD_DIM), lambda i: (i, 0, 0)),
        out_shape=jax.ShapeDtypeStruct((heads, tokens, 3 * HEAD_DIM), jnp.bfloat16),
    )(query_vectors, key_vectors, value_vectors)


def merge_kernel(own_ref, oth_ref, out_ref, vel_ref, piece_ref):
    own, oth = own_ref[...], oth_ref[...]
    gap = pltpu.roll(oth - own, 64, axis=1)
    share = 1.0 / (1.0 + jnp.exp2(gap))
    vel = own * share + oth * (1.0 - share)
    lane = lax.broadcasted_iota(jnp.int32, vel.shape, 1)
    vel_ref[...] = jnp.where(lane < 64, vel, pltpu.roll(vel, 64, axis=1))
    low = lax.broadcasted_iota(jnp.int32, (16, 128), 1) < 64
    zero = jnp.zeros((16, 128), jnp.float32)

    def column(r, at):
        if at < 0 or at >= 48:
            return zero
        return vel_ref[pl.ds(r * 48 + at, 16, stride=96), :]

    for b in range(8):
        for r in range(2):
            for c in range(4):
                at = 6 * b - 1 + c
                both = jnp.where(low, column(r, at), column(r, at + 4))
                for y in range(4):
                    piece_ref[y, b, pl.ds(r * 16 + c, 4, stride=4), :] = both[y * 4 : y * 4 + 4]
    out_ref[...] = piece_ref[...].astype(jnp.bfloat16)


def merge(own, oth):
    rows = own.shape[0]
    whole = pl.BlockSpec((rows, 128), lambda: (0, 0))
    shape = (4, 8, 32, 128)
    return pl.pallas_call(
        merge_kernel,
        in_specs=[whole, whole],
        out_specs=pl.BlockSpec(shape, lambda: (0, 0, 0, 0)),
        out_shape=jax.ShapeDtypeStruct(shape, jnp.bfloat16),
        scratch_shapes=[
            pltpu.VMEM((rows, 128), jnp.float32),
            pltpu.VMEM(shape, jnp.float32),
        ],
        compiler_params=pltpu.CompilerParams(vmem_limit_bytes=24 << 20),
    )(own, oth)


def head_sum_kernel(parts_ref, mine_ref, near_ref, apart_ref):
    total = parts_ref[0].astype(jnp.float32)
    for h in range(1, parts_ref.shape[0]):
        total = total + parts_ref[h].astype(jnp.float32)
    mine_ref[...] = total
    even = lax.axis_index("core") == 0
    near_ref[...] = jnp.where(even, total[16:32], total[0:16])
    apart_ref[...] = jnp.where(even, total[0:16], total[16:32])


def head_sum(parts):
    return small_call(head_sum_kernel, [(32, 128), (16, 128), (16, 128)])(parts)


def attention(query_vectors, key_vectors, value_vectors, weight_head, inputs):
    packed = pack(query_vectors, key_vectors, value_vectors)
    packed, inputs = lax.optimization_barrier((packed, inputs))
    noisy, cache_in, cache_mid, weight_in = inputs
    rows = halo_rows(noisy, cache_in, cache_mid)
    weight_first = window_weights(weight_in)
    heads, tokens = packed.shape[:2]
    moved = lax.all_to_all(packed, HEAD, split_axis=0, concat_axis=0, tiled=True)
    moved = moved.reshape(heads * tokens, 3 * HEAD_DIM)
    swap = [(0, 1), (1, 0)]
    right = [(i, (i + 1) % 4) for i in range(4)]
    left = [((i + 1) % 4, i) for i in range(4)]
    mid = moved.shape[0] // 2
    a, b, q_own = moved[:mid, :256], moved[mid:, :256], moved[:, 256:]
    a, b, q_own, rows, weight_first = lax.optimization_barrier((a, b, q_own, rows, weight_first))
    left_a = lax.ppermute(a, "y", right)
    right_b = lax.ppermute(b, "y", left)
    q_oth = lax.ppermute(q_own, "core", swap)
    state = flash(moved, q_oth, [moved])
    toks, mids, to_right, to_left = rows
    state, a, b = lax.optimization_barrier((state, a, b))
    left_b = lax.ppermute(b, "y", right)
    right_a = lax.ppermute(a, "y", left)
    state = flash(moved, q_oth, [left_a, right_b], state)
    state, left_a, right_b = lax.optimization_barrier((state, left_a, right_b))
    far = [lax.ppermute(left_a, "y", right), lax.ppermute(right_b, "y", left)]
    state = flash(moved, q_oth, [left_b, right_a], state)
    state, to_right, to_left = lax.optimization_barrier((state, to_right, to_left))
    before = lax.ppermute(to_right, BLK, along(BLK, 1))
    after = lax.ppermute(to_left, BLK, along(BLK, -1))
    state, before, after = lax.optimization_barrier((state, before, after))
    weight = weight_head.T
    oth = flash_last(q_oth, 0, far, state, 1, weight)
    oth, state = lax.optimization_barrier((oth, state))
    oth = lax.ppermute(oth, "core", swap)
    own = flash_last(moved, 2, far, state, 0, weight)
    partial = merge(own, oth).reshape(heads, 32, 128)
    parts = lax.all_to_all(partial, HEAD, split_axis=0, concat_axis=0, tiled=True)
    return head_sum(parts), (toks, mids, before, after, weight_first)


def shards(
    query_vectors,
    key_vectors,
    value_vectors,
    weight_head,
    noisy_latent,
    noise_level,
    latent_mean,
    latent_scale,
    cache_in,
    weight_in,
    bias_in,
    norm_gain,
    cache_mid,
    weight_mid,
    bias_mid,
):
    (mine, near, apart), (toks, mids, before, after, weight_first) = attention(
        query_vectors,
        key_vectors,
        value_vectors,
        weight_head,
        (noisy_latent, cache_in, cache_mid, weight_in),
    )

    count = lax.axis_size(SEQ)
    near = lax.ppermute(near, SEQ, [(i, i ^ 1) for i in range(count)])
    pairs = [(i, i + 1) for i in range(1, count - 1, 2)]
    pairs += [(j, i) for i, j in pairs]
    apart = lax.ppermute(apart, SEQ, pairs)
    denoised, features = tail(
        near,
        mine,
        apart,
        toks,
        mids,
        before,
        after,
        noise_level,
        latent_scale,
        latent_mean,
        weight_first,
        bias_in,
        norm_gain,
        weight_mid.reshape(9, 3 * C1, C1),
        bias_mid,
    )
    return denoised.transpose(0, 2, 1, 3), features.transpose(0, 2, 1, 3)


def solution(mesh):
    inner = Mesh(mesh.devices.reshape(4, 4, 2, 2, 4), SHARD)
    tokens, tile = P(SHARD, None), P(None, SEQ, BLK, None)
    in_specs = (
        tokens,
        tokens,
        tokens,
        P(),
        tile,
        P(),
        P(),
        P(),
        tile,
        P(),
        P(),
        P(),
        tile,
        P(),
        P(),
    )
    return jax.shard_map(
        shards, mesh=inner, in_specs=in_specs, out_specs=(tile, tile), check_vma=False
    )
```

```python
import functools
import math

import jax
import jax.numpy as jnp
from jax import lax
from jax.experimental import pallas as pl
from jax.experimental.pallas import tpu as pltpu
from jax.sharding import Mesh
from jax.sharding import PartitionSpec as P

HEAD_DIM = 128
LAT = 16
C1 = 384
F = 4
EPSILON = 1e-06

SEQ = ("y", "zh", "core")
BLK = ("zl", "x")
HEAD = ("zh", "zl", "x")
SHARD = SEQ + BLK

TILE = 1536
SUB = 256
CHUNK = 768
NT = (((1,), (1,)), ((), ()))


def mesh_index(axes):
    index = 0
    for axis in axes:
        index = index * lax.axis_size(axis) + lax.axis_index(axis)
    return index


def lane_max(s):
    t = s[:, :128]
    for j in range(1, s.shape[1] // 128):
        t = jnp.maximum(t, s[:, j * 128 : (j + 1) * 128])
    return jnp.max(t, axis=1, keepdims=True)


def flash_kernel(first, last, n_kv, half, *refs):
    q_ref, refs = refs[0], refs[1:]
    if not last:
        qx_ref, refs = refs[0], refs[1:]
    kv_refs, refs = refs[:n_kv], refs[n_kv:]
    if not first:
        st_ref, refs = refs[0], refs[1:]
    if last:
        w_ref, u_ref = refs
        query = q_ref[...]
        own = w_ref[:, pl.ds(pl.multiple_of(mesh_index(HEAD) * HEAD_DIM, HEAD_DIM), HEAD_DIM)]
        weight = jnp.concatenate([own, jnp.zeros_like(own)], axis=0)
    else:
        (so_ref,) = refs
        query = jnp.where(pl.program_id(0) < half, q_ref[...], qx_ref[...])
    scale = math.log2(math.e) / math.sqrt(HEAD_DIM)
    qf = query.astype(jnp.float32) * scale
    q_hi = qf.astype(jnp.bfloat16)
    q_lo = (qf - q_hi.astype(jnp.float32)).astype(jnp.bfloat16)
    q = jnp.concatenate([q_hi, q_lo], axis=1)
    subs = TILE // SUB
    tops, accs = [], []
    for r in range(subs):
        if first:
            tops.append(jnp.full((SUB, 128), -1e30, jnp.float32))
            accs.append(jnp.zeros((SUB, 256), jnp.float32))
        else:
            st = st_ref[pl.ds(r * SUB, SUB), :]
            acc_l = st[:, 128:]
            lane = lax.broadcasted_iota(jnp.int32, (SUB, 128), 1)
            total = jnp.max(jnp.where(lane < 64, acc_l, -1e30), axis=1, keepdims=True)
            top = jnp.max(jnp.where(lane < 64, -1e30, acc_l), axis=1, keepdims=True)
            tops.append(jnp.broadcast_to(top, (SUB, 128)))
            accs.append(
                jnp.concatenate([st[:, :128], jnp.broadcast_to(total, (SUB, 128))], axis=1)
            )
    items = [
        (r, b, c)
        for r in range(subs)
        for b in range(n_kv)
        for c in range(kv_refs[b].shape[0] // CHUNK)
    ]
    ones = jnp.ones((CHUNK, 128), jnp.bfloat16)

    def score(item):
        r, b, c = item
        k = kv_refs[b][pl.ds(c * CHUNK, CHUNK), :128]
        return lax.dot_general(
            q[r * SUB : (r + 1) * SUB],
            jnp.concatenate([k, k], axis=1),
            NT,
            preferred_element_type=jnp.float32,
        )

    s = score(items[0])
    for n, (r, b, c) in enumerate(items):
        following = score(items[n + 1]) if n + 1 < len(items) else None
        top = jnp.maximum(tops[r], lane_max(s))
        p = jnp.exp2(s - top[:, :1]).astype(jnp.bfloat16)
        fade = jnp.exp2(tops[r] - top)
        v = jnp.concatenate([kv_refs[b][pl.ds(c * CHUNK, CHUNK), 128:], ones], axis=1)
        accs[r] = accs[r] * jnp.concatenate([fade, fade], axis=1) + jnp.dot(
            p, v, preferred_element_type=jnp.float32
        )
        tops[r] = top
        s = following
    lane = lax.broadcasted_iota(jnp.int32, (SUB, 128), 1)
    for r in range(subs):
        if last:
            total = accs[r][:, 128:]
            mixed = (accs[r][:, :128] / total).astype(jnp.bfloat16)
            u = lax.dot_general(mixed, weight, NT, preferred_element_type=jnp.float32)
            u_ref[pl.ds(r * SUB, SUB), :] = jnp.where(lane < 64, u, tops[r] + jnp.log2(total))
        else:
            so_ref[pl.ds(r * SUB, SUB), :] = jnp.concatenate(
                [accs[r][:, :128], jnp.where(lane < 64, accs[r][:, 128:], tops[r])], axis=1
            )


def flash(q_own, q_oth, kvs, state=None):
    rows = q_oth.shape[0]
    half = rows // TILE
    keys = sum(kv.shape[0] for kv in kvs)
    in_specs = [
        pl.BlockSpec((TILE, 128), lambda i: (jnp.minimum(i, half - 1), 2)),
        pl.BlockSpec((TILE, 128), lambda i: (jnp.maximum(i - half, 0), 0)),
    ]
    in_specs += [pl.BlockSpec((kv.shape[0], 256), lambda i: (0, 0)) for kv in kvs]
    args = [q_own, q_oth, *kvs]
    if state is not None:
        in_specs.append(pl.BlockSpec((TILE, 256), lambda i: (i, 0)))
        args.append(state)
    return pl.pallas_call(
        functools.partial(flash_kernel, state is None, False, len(kvs), half),
        grid=(2 * half,),
        in_specs=in_specs,
        out_specs=pl.BlockSpec((TILE, 256), lambda i: (i, 0)),
        out_shape=jax.ShapeDtypeStruct((2 * rows, 256), jnp.float32),
        compiler_params=pltpu.CompilerParams(vmem_limit_bytes=20 << 20),
        cost_estimate=flash_cost(2 * rows, keys),
    )(*args)


def flash_last(query, lane_block, kvs, state, half_at, weight):
    rows = query.shape[0]
    half = rows // TILE
    keys = sum(kv.shape[0] for kv in kvs)
    in_specs = [pl.BlockSpec((TILE, 128), lambda i: (i, lane_block))]
    in_specs += [pl.BlockSpec((kv.shape[0], 256), lambda i: (0, 0)) for kv in kvs]
    in_specs += [
        pl.BlockSpec((TILE, 256), lambda i: (i + half_at * half, 0)),
        pl.BlockSpec(weight.shape, lambda i: (0, 0)),
    ]
    return pl.pallas_call(
        functools.partial(flash_kernel, False, True, len(kvs), half),
        grid=(half,),
        in_specs=in_specs,
        out_specs=pl.BlockSpec((TILE, 128), lambda i: (i, 0)),
        out_shape=jax.ShapeDtypeStruct((rows, 128), jnp.float32),
        compiler_params=pltpu.CompilerParams(vmem_limit_bytes=20 << 20),
        cost_estimate=flash_cost(rows, keys),
    )(query, *kvs, state, weight)


def flash_cost(rows, keys):
    return pl.CostEstimate(
        flops=rows * keys * 1024, bytes_accessed=rows * 2048, transcendentals=rows * keys
    )


def inside(at, low, high, before, after):
    return ((at > low) | before) & ((at < high) | after)


def tail_kernel(
    near_ref,
    mine_ref,
    apart_ref,
    toks,
    mids,
    before_ref,
    after_ref,
    level_ref,
    scale_ref,
    mean_ref,
    w1_ref,
    b1_ref,
    gain_ref,
    w2_ref,
    b2_ref,
    den_ref,
    out_ref,
    vel,
    lat,
    den,
    first,
    act,
    wide,
    done,
    vecs,
    cells_ref,
    mid_ref,
    w1_buf,
    w2_buf,
    sems,
):
    fetch_first = pltpu.make_async_copy(w1_ref, w1_buf, sems.at[9])
    fetch_first.start()
    for tap in range(9):
        pltpu.make_async_copy(w2_ref.at[tap], w2_buf.at[tap], sems.at[tap]).start()
    place(toks, mids, before_ref, after_ref, cells_ref, mid_ref)
    even = lax.axis_index("core") == 0
    at_row, at_col = mesh_index(SEQ), mesh_index(BLK)
    up, down = at_row > 0, at_row < lax.axis_size(SEQ) - 1
    before, after = at_col > 0, at_col < lax.axis_size(BLK) - 1
    above = jnp.where(even, apart_ref[...], near_ref[...])
    below = jnp.where(even, near_ref[...], apart_ref[...])
    for at, rows in enumerate((above, mine_ref[0:16, :], mine_ref[16:32, :], below)):
        turned = pltpu.roll(rows, 64, axis=1)
        for f in range(F):
            vel[f, at, 0:4, :] = rows[f * 4 : f * 4 + 4]
            vel[f, at, 4:8, :] = turned[f * 4 : f * 4 + 4]
    vecs[...] = jnp.zeros(vecs.shape, jnp.float32)
    vecs[0:1, 0:LAT] = scale_ref[...].reshape(1, LAT)
    vecs[8:9, 0:LAT] = mean_ref[...].reshape(1, LAT)
    base = vecs[...]
    tiled = base + pltpu.roll(base, LAT, axis=1)
    tiled = tiled + pltpu.roll(tiled, 2 * LAT, axis=1)
    scale, mean = tiled[0:1, 0:64], tiled[8:9, 0:64]
    denoised = cells_ref[2:6, :, :, 0:64] - level_ref[0] * vel[:, :, :, 0:64]
    row = lax.broadcasted_iota(jnp.int32, denoised.shape, 1)
    col = lax.broadcasted_iota(jnp.int32, denoised.shape, 2)
    kept = inside(row, 0, 3, up, down) & inside(col, 0, 7, before, after)
    latent = jnp.where(kept, denoised * scale + mean, 0.0)
    for k in range(4):
        part = jnp.concatenate([denoised, denoised], axis=3).reshape(F * 32, 128)
        part = pltpu.roll(part, 128 - LAT * k, axis=1) if k else part
        part = part.reshape(F, 4, 8, 128)
        for f in range(F):
            for r in range(2):
                rows = pl.ds(8 * (k % 2) + 2 * r + k // 2, 8, stride=16)
                den[f, rows, :] = part[f, r + 1]
    den_ref[...] = den[:, 16:112, :].reshape(F, 12, 8, 128)[:, :, 0:4, 0:LAT]
    lat[...] = jnp.zeros(lat.shape, jnp.float32)
    lat[0:2, :, 0:8, 0:64] = cells_ref[0:2, :, :, 0:64]
    lat[2:6, :, 0:8, 0:64] = latent.astype(jnp.bfloat16).astype(jnp.float32)
    here = lat[:, :, 0:8, :].reshape(192, 128)
    right = pltpu.roll(lat[:, :, 1:9, :].reshape(192, 128), 64, axis=1)
    lane = lax.broadcasted_iota(jnp.int32, (192, 128), 1)
    pair = jnp.where(lane < 64, here, right).reshape(6, 4, 8, 128)
    lower = jnp.concatenate([pair[:, 1:4], pair[:, 3:4]], axis=1)
    window = jnp.concatenate([pair, lower], axis=3).reshape(192, 256).astype(jnp.bfloat16)
    parts = C1 // 128
    for k in range(parts):
        act[k, 0:2, :, 0:16, :] = mid_ref[:, :, :, pl.ds(k * 128, 128)]
    gain = gain_ref[...].reshape(1, C1)
    fetch_first.wait()
    for p in range(2):
        for q in range(2):
            lanes = pl.ds((2 * p + q) * C1, C1)
            value = b1_ref[...].reshape(1, C1)
            for t in range(3):
                value = value + jnp.dot(
                    window[t * 32 : t * 32 + 128],
                    w1_buf[t, :, lanes],
                    preferred_element_type=jnp.float32,
                )
            power = jnp.mean(value * value, axis=1, keepdims=True)
            normed = value * lax.rsqrt(power + EPSILON) * gain
            active = (normed / (1.0 + jnp.exp(-normed))).reshape(F, 32, C1)
            at = lax.broadcasted_iota(jnp.int32, (32, C1), 0)
            kept = inside(2 * (at // 8) + p, 0, 5, up, down)
            kept = kept & inside(2 * (at % 8) + q, 0, 13, before, after)
            active = jnp.where(kept, active, 0.0)
            value = value.reshape(F, 4, 8, C1)
            active = active.reshape(F, 4, 8, C1)
            for r in range(3):
                cols = pl.ds(q, 8, stride=2)
                for k in range(parts):
                    part = slice(k * 128, k * 128 + 128)
                    for f in range(F):
                        first[k, f, 2 * r + p, cols, :] = value[f, r, :, part]
                        act[k, f + 2, 2 * r + p, cols, :] = active[f, r, :, part]
    for v in range(3):
        for k in range(parts):
            wide[:, :, :, pl.ds(v * C1 + k * 128, 128)] = act[k, :, :, pl.ds(v, 16), :].astype(
                jnp.bfloat16
            )
    middle = [first[k, :, 1:5, pl.ds(1, 16), :].reshape(256, 128) for k in range(parts)]
    total = jnp.concatenate(middle, axis=1) + b2_ref[...].reshape(1, C1)
    for tap in range(9):
        t, u = divmod(tap, 3)
        rows = wide[t : t + 4, u : u + 4].reshape(256, 3 * C1)
        pltpu.make_async_copy(w2_ref.at[tap], w2_buf.at[tap], sems.at[tap]).wait()
        total = total + jnp.dot(rows, w2_buf[tap], preferred_element_type=jnp.float32)
    for k in range(parts):
        for f in range(F):
            for i in range(4):
                at = f * 64 + i * 16
                done[k, f, pl.ds(i, 16, stride=8), :] = total[at : at + 16, k * 128 : k * 128 + 128]
        cells = done[k, :, 0:96, :].reshape(F, 12, 8, 128)[:, :, 0:4]
        out_ref[:, :, :, pl.ds(k * 128, 128)] = cells.astype(jnp.bfloat16)


def tail(*args):
    specs = [pl.BlockSpec(memory_space=pltpu.VMEM)] * len(args)
    specs[7] = pl.BlockSpec(memory_space=pltpu.SMEM)
    specs[10] = specs[13] = pl.BlockSpec(memory_space=pl.ANY)
    return pl.pallas_call(
        tail_kernel,
        in_specs=specs,
        out_specs=[pl.BlockSpec(memory_space=pltpu.VMEM)] * 2,
        out_shape=[
            jax.ShapeDtypeStruct((F, 12, 4, LAT), jnp.float32),
            jax.ShapeDtypeStruct((F, 12, 4, C1), jnp.bfloat16),
        ],
        scratch_shapes=[
            pltpu.VMEM((F, 4, 8, 128), jnp.float32),
            pltpu.VMEM((6, 4, 16, 128), jnp.float32),
            pltpu.VMEM((F, 128, 128), jnp.float32),
            pltpu.VMEM((C1 // 128, F, 6, 24, 128), jnp.float32),
            pltpu.VMEM((C1 // 128, 6, 6, 24, 128), jnp.float32),
            pltpu.VMEM((6, 6, 16, 3 * C1), jnp.bfloat16),
            pltpu.VMEM((C1 // 128, F, 128, 128), jnp.float32),
            pltpu.VMEM((16, 128), jnp.float32),
            pltpu.VMEM((6, 4, 8, 128), jnp.float32),
            pltpu.VMEM((2, 6, 16, C1), jnp.float32),
            pltpu.VMEM((3, 16 * LAT, 4 * C1), jnp.bfloat16),
            pltpu.VMEM((9, 3 * C1, C1), jnp.bfloat16),
            pltpu.SemaphoreType.DMA((10,)),
        ],
        compiler_params=pltpu.CompilerParams(vmem_limit_bytes=60 << 20),
    )(*args)


def window_kernel(w_ref, out_ref):
    out_ref[...] = jnp.zeros(out_ref.shape, out_ref.dtype)
    for t in range(3):
        for u in range(3):
            for v in range(3):
                taps = w_ref[t, u, v]
                for p in range(2):
                    for q in range(2):
                        (dr, a), (dc, b) = divmod(p + u, 2), divmod(q + v, 2)
                        at = dr * 128 + dc * 64 + a * 32 + b * 16
                        out_ref[t, pl.ds(at, LAT), pl.ds((2 * p + q) * C1, C1)] = taps


def window_weights(weight):
    return pl.pallas_call(
        window_kernel,
        out_shape=jax.ShapeDtypeStruct((3, 16 * LAT, 4 * C1), jnp.bfloat16),
        compiler_params=pltpu.CompilerParams(vmem_limit_bytes=16 << 20),
    )(weight)


def put_frames(ref, rows, tokens):
    count = tokens[0].shape[0]
    low = lax.broadcasted_iota(jnp.int32, (count, 128), 1) < 64
    for i in range(2):
        for h in range(2):
            one = tokens[i + 2 * h]
            two = pltpu.roll(tokens[i + 4], 64, axis=1) if h == 0 else jnp.zeros_like(one)
            ref[i, pl.ds(rows + h * count, count), 384:512] = jnp.where(low, one, two)


def get_frames(ref, rows, count):
    out = {}
    for i in range(2):
        for h in range(2):
            both = ref[i, pl.ds(rows + h * count, count), 384:512]
            out[i + 2 * h] = both
            if h == 0:
                out[i + 4] = pltpu.roll(both, 64, axis=1)
    return [out[f] for f in range(6)]


def edge_rows_kernel(noisy_ref, cache_ref, mid_ref, tok_ref, down_ref, up_ref, cells):
    cells[...] = jnp.zeros(cells.shape, jnp.float32)
    cells[0:2, :, 0:12, 0:LAT] = cache_ref[...].astype(jnp.float32)
    cells[2:6, :, 0:12, 0:LAT] = noisy_ref[...]
    lane = lax.broadcasted_iota(jnp.int32, (8, 128), 1)
    tokens = {}
    for r in range(2):
        for f in range(6):
            token = jnp.zeros((8, 128), jnp.float32)
            for k in range(4):
                part = cells[f, 2 * r + k // 2, pl.ds(k % 2, 8, stride=2), :]
                part = pltpu.roll(part, LAT * k, axis=1) if k else part
                token = jnp.where((lane >= LAT * k) & (lane < LAT * k + LAT), part, token)
            tok_ref[f, r] = token
            tokens[f, r] = token
    for ref, row, r in ((down_ref, 3, 1), (up_ref, 0, 0)):
        ref[...] = jnp.zeros(ref.shape, jnp.float32)
        ref[:, 0:12, 0:C1] = mid_ref[:, row].astype(jnp.float32)
        put_frames(ref, 0, [tokens[f, r] for f in range(6)])


def edge_cols_kernel(tok_ref, mid_ref, above_ref, below_ref, toks, mids, right_ref, left_ref):
    above, below = get_frames(above_ref, 0, 8), get_frames(below_ref, 0, 8)
    for f in range(6):
        toks[f, 0] = above[f]
        toks[f, 1] = tok_ref[f, 0]
        toks[f, 2] = tok_ref[f, 1]
        toks[f, 3] = below[f]
    mids[...] = jnp.zeros(mids.shape, jnp.float32)
    mids[:, 0, 0:12, :] = above_ref[:, 0:12, 0:C1]
    mids[:, 1:5, 0:12, :] = mid_ref[...].astype(jnp.float32)
    mids[:, 5, 0:12, :] = below_ref[:, 0:12, 0:C1]
    for ref, token, col in ((right_ref, 5, 11), (left_ref, 0, 0)):
        ref[...] = jnp.zeros(ref.shape, jnp.float32)
        for i in range(2):
            for row in range(6):
                ref[i, pl.ds(row, 1), 0:C1] = mids[i, row, pl.ds(col, 1), :]
        for r in range(4):
            put_rows(ref, r, [toks[f, r, pl.ds(token, 1), :] for f in range(6)])


def put_rows(ref, r, tokens):
    low = lax.broadcasted_iota(jnp.int32, (1, 128), 1) < 64
    for i in range(2):
        for h in range(2):
            one = tokens[i + 2 * h]
            two = pltpu.roll(tokens[i + 4], 64, axis=1) if h == 0 else jnp.zeros_like(one)
            ref[i, pl.ds(4 * h + r, 1), 384:512] = jnp.where(low, one, two)


def place(toks, mids, left_ref, right_ref, cells_ref, cache_ref):
    cells_ref[...] = jnp.zeros(cells_ref.shape, jnp.float32)
    cache_ref[...] = jnp.zeros(cache_ref.shape, jnp.float32)
    for f in range(6):
        for r in range(4):
            cells_ref[f, r, 1:7, :] = toks[f, r, 0:6, :]
    cache_ref[:, :, 1:13, :] = mids[:, :, 0:12, :]
    for ref, token, col in ((left_ref, 0, 0), (right_ref, 7, 13)):
        frames = get_frames(ref, 0, 4)
        for f in range(6):
            for r in range(4):
                cells_ref[f, r, pl.ds(token, 1), :] = frames[f][r : r + 1]
        for i in range(2):
            for row in range(6):
                cache_ref[i, row, pl.ds(col, 1), :] = ref[i, pl.ds(row, 1), 0:C1]


def small_call(kernel, shapes, scratch=()):
    return pl.pallas_call(
        kernel,
        out_shape=[jax.ShapeDtypeStruct(shape, jnp.float32) for shape in shapes],
        scratch_shapes=[pltpu.VMEM(shape, jnp.float32) for shape in scratch],
        compiler_params=pltpu.CompilerParams(vmem_limit_bytes=8 << 20),
    )


def along(axis, step):
    count = lax.axis_size(axis)
    return [(i, i + step) for i in range(count) if 0 <= i + step < count]


def halo_rows(noisy, cache_in, cache_mid):
    edge = (2, 16, 512)
    toks, down, up = small_call(
        edge_rows_kernel, [(6, 2, 8, 128), edge, edge], [(6, 4, 16, 128)]
    )(noisy, cache_in, cache_mid)
    above = lax.ppermute(down, SEQ, along(SEQ, 1))
    below = lax.ppermute(up, SEQ, along(SEQ, -1))
    side = (2, 8, 512)
    return small_call(edge_cols_kernel, [(6, 4, 8, 128), (2, 6, 16, C1), side, side])(
        toks, cache_mid, above, below
    )


def pack_kernel(q_ref, k_ref, v_ref, out_ref):
    for h in range(out_ref.shape[0]):
        lanes = pl.ds(h * HEAD_DIM, HEAD_DIM)
        out_ref[h, :, 0:128] = k_ref[:, lanes]
        out_ref[h, :, 128:256] = v_ref[:, lanes]
        out_ref[h, :, 256:384] = q_ref[:, lanes]


def pack(query_vectors, key_vectors, value_vectors):
    tokens, width = query_vectors.shape
    heads = width // HEAD_DIM
    block = pl.BlockSpec((tokens, width // 2), lambda i: (0, i))
    return pl.pallas_call(
        pack_kernel,
        grid=(2,),
        in_specs=[block] * 3,
        out_specs=pl.BlockSpec((heads // 2, tokens, 3 * HEAD_DIM), lambda i: (i, 0, 0)),
        out_shape=jax.ShapeDtypeStruct((heads, tokens, 3 * HEAD_DIM), jnp.bfloat16),
    )(query_vectors, key_vectors, value_vectors)


def merge_kernel(own_ref, oth_ref, out_ref, vel_ref, piece_ref):
    own, oth = own_ref[...], oth_ref[...]
    gap = pltpu.roll(oth - own, 64, axis=1)
    share = 1.0 / (1.0 + jnp.exp2(gap))
    vel = own * share + oth * (1.0 - share)
    lane = lax.broadcasted_iota(jnp.int32, vel.shape, 1)
    vel_ref[...] = jnp.where(lane < 64, vel, pltpu.roll(vel, 64, axis=1))
    low = lax.broadcasted_iota(jnp.int32, (16, 128), 1) < 64
    zero = jnp.zeros((16, 128), jnp.float32)

    def column(r, at):
        if at < 0 or at >= 48:
            return zero
        return vel_ref[pl.ds(r * 48 + at, 16, stride=96), :]

    for b in range(8):
        for r in range(2):
            for c in range(4):
                at = 6 * b - 1 + c
                both = jnp.where(low, column(r, at), column(r, at + 4))
                for y in range(4):
                    piece_ref[y, b, pl.ds(r * 16 + c, 4, stride=4), :] = both[y * 4 : y * 4 + 4]
    out_ref[...] = piece_ref[...].astype(jnp.bfloat16)


def merge(own, oth):
    rows = own.shape[0]
    whole = pl.BlockSpec((rows, 128), lambda: (0, 0))
    shape = (4, 8, 32, 128)
    return pl.pallas_call(
        merge_kernel,
        in_specs=[whole, whole],
        out_specs=pl.BlockSpec(shape, lambda: (0, 0, 0, 0)),
        out_shape=jax.ShapeDtypeStruct(shape, jnp.bfloat16),
        scratch_shapes=[
            pltpu.VMEM((rows, 128), jnp.float32),
            pltpu.VMEM(shape, jnp.float32),
        ],
        compiler_params=pltpu.CompilerParams(vmem_limit_bytes=24 << 20),
    )(own, oth)


def head_sum_kernel(parts_ref, mine_ref, near_ref, apart_ref):
    total = parts_ref[0].astype(jnp.float32)
    for h in range(1, parts_ref.shape[0]):
        total = total + parts_ref[h].astype(jnp.float32)
    mine_ref[...] = total
    even = lax.axis_index("core") == 0
    near_ref[...] = jnp.where(even, total[16:32], total[0:16])
    apart_ref[...] = jnp.where(even, total[0:16], total[16:32])


def head_sum(parts):
    return small_call(head_sum_kernel, [(32, 128), (16, 128), (16, 128)])(parts)


def attention(query_vectors, key_vectors, value_vectors, weight_head, inputs):
    packed = pack(query_vectors, key_vectors, value_vectors)
    packed, inputs = lax.optimization_barrier((packed, inputs))
    noisy, cache_in, cache_mid, weight_in = inputs
    rows = halo_rows(noisy, cache_in, cache_mid)
    weight_first = window_weights(weight_in)
    heads, tokens = packed.shape[:2]
    moved = lax.all_to_all(packed, HEAD, split_axis=0, concat_axis=0, tiled=True)
    moved = moved.reshape(heads * tokens, 3 * HEAD_DIM)
    swap = [(0, 1), (1, 0)]
    right = [(i, (i + 1) % 4) for i in range(4)]
    left = [((i + 1) % 4, i) for i in range(4)]
    mid = moved.shape[0] // 2
    a, b, q_own = moved[:mid, :256], moved[mid:, :256], moved[:, 256:]
    a, b, q_own, rows, weight_first = lax.optimization_barrier((a, b, q_own, rows, weight_first))
    left_a = lax.ppermute(a, "y", right)
    right_b = lax.ppermute(b, "y", left)
    q_oth = lax.ppermute(q_own, "core", swap)
    state = flash(moved, q_oth, [moved])
    toks, mids, to_right, to_left = rows
    state, a, b = lax.optimization_barrier((state, a, b))
    left_b = lax.ppermute(b, "y", right)
    right_a = lax.ppermute(a, "y", left)
    state = flash(moved, q_oth, [left_a, right_b], state)
    state, left_a, right_b = lax.optimization_barrier((state, left_a, right_b))
    far = [lax.ppermute(left_a, "y", right), lax.ppermute(right_b, "y", left)]
    state = flash(moved, q_oth, [left_b, right_a], state)
    weight = weight_head.T
    oth = flash_last(q_oth, 0, far, state, 1, weight)
    oth, state = lax.optimization_barrier((oth, state))
    oth = lax.ppermute(oth, "core", swap)
    own = flash_last(moved, 2, far, state, 0, weight)
    partial = merge(own, oth).reshape(heads, 32, 128)
    partial, to_right, to_left = lax.optimization_barrier((partial, to_right, to_left))
    before = lax.ppermute(to_right, BLK, along(BLK, 1))
    after = lax.ppermute(to_left, BLK, along(BLK, -1))
    parts = lax.all_to_all(partial, HEAD, split_axis=0, concat_axis=0, tiled=True)
    return head_sum(parts), (toks, mids, before, after, weight_first)


def shards(
    query_vectors,
    key_vectors,
    value_vectors,
    weight_head,
    noisy_latent,
    noise_level,
    latent_mean,
    latent_scale,
    cache_in,
    weight_in,
    bias_in,
    norm_gain,
    cache_mid,
    weight_mid,
    bias_mid,
):
    (mine, near, apart), (toks, mids, before, after, weight_first) = attention(
        query_vectors,
        key_vectors,
        value_vectors,
        weight_head,
        (noisy_latent, cache_in, cache_mid, weight_in),
    )

    count = lax.axis_size(SEQ)
    near = lax.ppermute(near, SEQ, [(i, i ^ 1) for i in range(count)])
    pairs = [(i, i + 1) for i in range(1, count - 1, 2)]
    pairs += [(j, i) for i, j in pairs]
    apart = lax.ppermute(apart, SEQ, pairs)
    denoised, features = tail(
        near,
        mine,
        apart,
        toks,
        mids,
        before,
        after,
        noise_level,
        latent_scale,
        latent_mean,
        weight_first,
        bias_in,
        norm_gain,
        weight_mid.reshape(9, 3 * C1, C1),
        bias_mid,
    )
    return denoised.transpose(0, 2, 1, 3), features.transpose(0, 2, 1, 3)


def solution(mesh):
    inner = Mesh(mesh.devices.reshape(4, 4, 2, 2, 4), SHARD)
    tokens, tile = P(SHARD, None), P(None, SEQ, BLK, None)
    in_specs = (
        tokens,
        tokens,
        tokens,
        P(),
        tile,
        P(),
        P(),
        P(),
        tile,
        P(),
        P(),
        P(),
        tile,
        P(),
        P(),
    )
    return jax.shard_map(
        shards, mesh=inner, in_specs=in_specs, out_specs=(tile, tile), check_vma=False
    )
```

```python
import functools
import math

import jax
import jax.numpy as jnp
from jax import lax
from jax.experimental import pallas as pl
from jax.experimental.pallas import tpu as pltpu
from jax.sharding import Mesh
from jax.sharding import PartitionSpec as P

HEAD_DIM = 128
LAT = 16
C1 = 384
F = 4
EPSILON = 1e-06

SEQ = ("y", "zh", "core")
BLK = ("zl", "x")
HEAD = ("zh", "zl", "x")
SHARD = SEQ + BLK

TILE = 1536
SUB = 256
CHUNK = 768
NT = (((1,), (1,)), ((), ()))


def mesh_index(axes):
    index = 0
    for axis in axes:
        index = index * lax.axis_size(axis) + lax.axis_index(axis)
    return index


def lane_max(s):
    t = s[:, :128]
    for j in range(1, s.shape[1] // 128):
        t = jnp.maximum(t, s[:, j * 128 : (j + 1) * 128])
    return jnp.max(t, axis=1, keepdims=True)


def flash_kernel(first, last, n_kv, half, *refs):
    q_ref, refs = refs[0], refs[1:]
    if not last:
        qx_ref, refs = refs[0], refs[1:]
    kv_refs, refs = refs[:n_kv], refs[n_kv:]
    if not first:
        st_ref, refs = refs[0], refs[1:]
    if last:
        w_ref, u_ref = refs
        query = q_ref[...]
        own = w_ref[:, pl.ds(pl.multiple_of(mesh_index(HEAD) * HEAD_DIM, HEAD_DIM), HEAD_DIM)]
        weight = jnp.concatenate([own, jnp.zeros_like(own)], axis=0)
    else:
        (so_ref,) = refs
        query = jnp.where(pl.program_id(0) < half, q_ref[...], qx_ref[...])
    scale = math.log2(math.e) / math.sqrt(HEAD_DIM)
    qf = query.astype(jnp.float32) * scale
    q_hi = qf.astype(jnp.bfloat16)
    q_lo = (qf - q_hi.astype(jnp.float32)).astype(jnp.bfloat16)
    q = jnp.concatenate([q_hi, q_lo], axis=1)
    subs = TILE // SUB
    tops, accs = [], []
    for r in range(subs):
        if first:
            tops.append(jnp.full((SUB, 128), -1e30, jnp.float32))
            accs.append(jnp.zeros((SUB, 256), jnp.float32))
        else:
            st = st_ref[pl.ds(r * SUB, SUB), :]
            acc_l = st[:, 128:]
            lane = lax.broadcasted_iota(jnp.int32, (SUB, 128), 1)
            total = jnp.max(jnp.where(lane < 64, acc_l, -1e30), axis=1, keepdims=True)
            top = jnp.max(jnp.where(lane < 64, -1e30, acc_l), axis=1, keepdims=True)
            tops.append(jnp.broadcast_to(top, (SUB, 128)))
            accs.append(
                jnp.concatenate([st[:, :128], jnp.broadcast_to(total, (SUB, 128))], axis=1)
            )
    items = [
        (r, b, c)
        for r in range(subs)
        for b in range(n_kv)
        for c in range(kv_refs[b].shape[0] // CHUNK)
    ]
    ones = jnp.ones((CHUNK, 128), jnp.bfloat16)

    def score(item):
        r, b, c = item
        k = kv_refs[b][pl.ds(c * CHUNK, CHUNK), :128]
        return lax.dot_general(
            q[r * SUB : (r + 1) * SUB],
            jnp.concatenate([k, k], axis=1),
            NT,
            preferred_element_type=jnp.float32,
        )

    s = score(items[0])
    for n, (r, b, c) in enumerate(items):
        following = score(items[n + 1]) if n + 1 < len(items) else None
        top = jnp.maximum(tops[r], lane_max(s))
        p = jnp.exp2(s - top[:, :1]).astype(jnp.bfloat16)
        fade = jnp.exp2(tops[r] - top)
        v = jnp.concatenate([kv_refs[b][pl.ds(c * CHUNK, CHUNK), 128:], ones], axis=1)
        accs[r] = accs[r] * jnp.concatenate([fade, fade], axis=1) + jnp.dot(
            p, v, preferred_element_type=jnp.float32
        )
        tops[r] = top
        s = following
    lane = lax.broadcasted_iota(jnp.int32, (SUB, 128), 1)
    for r in range(subs):
        if last:
            total = accs[r][:, 128:]
            mixed = (accs[r][:, :128] / total).astype(jnp.bfloat16)
            u = lax.dot_general(mixed, weight, NT, preferred_element_type=jnp.float32)
            u_ref[pl.ds(r * SUB, SUB), :] = jnp.where(lane < 64, u, tops[r] + jnp.log2(total))
        else:
            so_ref[pl.ds(r * SUB, SUB), :] = jnp.concatenate(
                [accs[r][:, :128], jnp.where(lane < 64, accs[r][:, 128:], tops[r])], axis=1
            )


def flash(q_own, q_oth, kvs, state=None):
    rows = q_oth.shape[0]
    half = rows // TILE
    keys = sum(kv.shape[0] for kv in kvs)
    in_specs = [
        pl.BlockSpec((TILE, 128), lambda i: (jnp.minimum(i, half - 1), 2)),
        pl.BlockSpec((TILE, 128), lambda i: (jnp.maximum(i - half, 0), 0)),
    ]
    in_specs += [pl.BlockSpec((kv.shape[0], 256), lambda i: (0, 0)) for kv in kvs]
    args = [q_own, q_oth, *kvs]
    if state is not None:
        in_specs.append(pl.BlockSpec((TILE, 256), lambda i: (i, 0)))
        args.append(state)
    return pl.pallas_call(
        functools.partial(flash_kernel, state is None, False, len(kvs), half),
        grid=(2 * half,),
        in_specs=in_specs,
        out_specs=pl.BlockSpec((TILE, 256), lambda i: (i, 0)),
        out_shape=jax.ShapeDtypeStruct((2 * rows, 256), jnp.float32),
        compiler_params=pltpu.CompilerParams(vmem_limit_bytes=20 << 20),
        cost_estimate=flash_cost(2 * rows, keys),
    )(*args)


def flash_last(query, lane_block, kvs, state, half_at, weight):
    rows = query.shape[0]
    half = rows // TILE
    keys = sum(kv.shape[0] for kv in kvs)
    in_specs = [pl.BlockSpec((TILE, 128), lambda i: (i, lane_block))]
    in_specs += [pl.BlockSpec((kv.shape[0], 256), lambda i: (0, 0)) for kv in kvs]
    in_specs += [
        pl.BlockSpec((TILE, 256), lambda i: (i + half_at * half, 0)),
        pl.BlockSpec(weight.shape, lambda i: (0, 0)),
    ]
    return pl.pallas_call(
        functools.partial(flash_kernel, False, True, len(kvs), half),
        grid=(half,),
        in_specs=in_specs,
        out_specs=pl.BlockSpec((TILE, 128), lambda i: (i, 0)),
        out_shape=jax.ShapeDtypeStruct((rows, 128), jnp.float32),
        compiler_params=pltpu.CompilerParams(vmem_limit_bytes=20 << 20),
        cost_estimate=flash_cost(rows, keys),
    )(query, *kvs, state, weight)


def flash_cost(rows, keys):
    return pl.CostEstimate(
        flops=rows * keys * 1024, bytes_accessed=rows * 2048, transcendentals=rows * keys
    )


def inside(at, low, high, before, after):
    return ((at > low) | before) & ((at < high) | after)


def tail_kernel(
    near_ref,
    mine_ref,
    apart_ref,
    toks,
    mids,
    before_ref,
    after_ref,
    level_ref,
    scale_ref,
    mean_ref,
    w1_ref,
    b1_ref,
    gain_ref,
    w2_ref,
    b2_ref,
    den_ref,
    out_ref,
    vel,
    lat,
    den,
    first,
    act,
    wide,
    done,
    vecs,
    cells_ref,
    mid_ref,
    w1_buf,
    w2_buf,
    sems,
):
    for tap in range(9):
        pltpu.make_async_copy(w2_ref.at[tap], w2_buf.at[tap], sems.at[tap]).start()
    window_weights(w1_ref, w1_buf)
    place(toks, mids, before_ref, after_ref, cells_ref, mid_ref)
    even = lax.axis_index("core") == 0
    at_row, at_col = mesh_index(SEQ), mesh_index(BLK)
    up, down = at_row > 0, at_row < lax.axis_size(SEQ) - 1
    before, after = at_col > 0, at_col < lax.axis_size(BLK) - 1
    above = jnp.where(even, apart_ref[...], near_ref[...])
    below = jnp.where(even, near_ref[...], apart_ref[...])
    for at, rows in enumerate((above, mine_ref[0:16, :], mine_ref[16:32, :], below)):
        turned = pltpu.roll(rows, 64, axis=1)
        for f in range(F):
            vel[f, at, 0:4, :] = rows[f * 4 : f * 4 + 4]
            vel[f, at, 4:8, :] = turned[f * 4 : f * 4 + 4]
    vecs[...] = jnp.zeros(vecs.shape, jnp.float32)
    vecs[0:1, 0:LAT] = scale_ref[...].reshape(1, LAT)
    vecs[8:9, 0:LAT] = mean_ref[...].reshape(1, LAT)
    base = vecs[...]
    tiled = base + pltpu.roll(base, LAT, axis=1)
    tiled = tiled + pltpu.roll(tiled, 2 * LAT, axis=1)
    scale, mean = tiled[0:1, 0:64], tiled[8:9, 0:64]
    denoised = cells_ref[2:6, :, :, 0:64] - level_ref[0] * vel[:, :, :, 0:64]
    row = lax.broadcasted_iota(jnp.int32, denoised.shape, 1)
    col = lax.broadcasted_iota(jnp.int32, denoised.shape, 2)
    kept = inside(row, 0, 3, up, down) & inside(col, 0, 7, before, after)
    latent = jnp.where(kept, denoised * scale + mean, 0.0)
    for k in range(4):
        part = jnp.concatenate([denoised, denoised], axis=3).reshape(F * 32, 128)
        part = pltpu.roll(part, 128 - LAT * k, axis=1) if k else part
        part = part.reshape(F, 4, 8, 128)
        for f in range(F):
            for r in range(2):
                rows = pl.ds(8 * (k % 2) + 2 * r + k // 2, 8, stride=16)
                den[f, rows, :] = part[f, r + 1]
    den_ref[...] = den[:, 16:112, :].reshape(F, 12, 8, 128)[:, :, 0:4, 0:LAT]
    lat[...] = jnp.zeros(lat.shape, jnp.float32)
    lat[0:2, :, 0:8, 0:64] = cells_ref[0:2, :, :, 0:64]
    lat[2:6, :, 0:8, 0:64] = latent.astype(jnp.bfloat16).astype(jnp.float32)
    here = lat[:, :, 0:8, :].reshape(192, 128)
    right = pltpu.roll(lat[:, :, 1:9, :].reshape(192, 128), 64, axis=1)
    lane = lax.broadcasted_iota(jnp.int32, (192, 128), 1)
    pair = jnp.where(lane < 64, here, right).reshape(6, 4, 8, 128)
    lower = jnp.concatenate([pair[:, 1:4], pair[:, 3:4]], axis=1)
    window = jnp.concatenate([pair, lower], axis=3).reshape(192, 256).astype(jnp.bfloat16)
    parts = C1 // 128
    for k in range(parts):
        act[k, 0:2, :, 0:16, :] = mid_ref[:, :, :, pl.ds(k * 128, 128)]
    gain = gain_ref[...].reshape(1, C1)
    for p in range(2):
        for q in range(2):
            lanes = pl.ds((2 * p + q) * C1, C1)
            value = b1_ref[...].reshape(1, C1)
            for t in range(3):
                value = value + jnp.dot(
                    window[t * 32 : t * 32 + 128],
                    w1_buf[t, :, lanes],
                    preferred_element_type=jnp.float32,
                )
            power = jnp.mean(value * value, axis=1, keepdims=True)
            normed = value * lax.rsqrt(power + EPSILON) * gain
            active = (normed / (1.0 + jnp.exp(-normed))).reshape(F, 32, C1)
            at = lax.broadcasted_iota(jnp.int32, (32, C1), 0)
            kept = inside(2 * (at // 8) + p, 0, 5, up, down)
            kept = kept & inside(2 * (at % 8) + q, 0, 13, before, after)
            active = jnp.where(kept, active, 0.0)
            value = value.reshape(F, 4, 8, C1)
            active = active.reshape(F, 4, 8, C1)
            for r in range(3):
                cols = pl.ds(q, 8, stride=2)
                for k in range(parts):
                    part = slice(k * 128, k * 128 + 128)
                    for f in range(F):
                        first[k, f, 2 * r + p, cols, :] = value[f, r, :, part]
                        act[k, f + 2, 2 * r + p, cols, :] = active[f, r, :, part]
    for v in range(3):
        for k in range(parts):
            wide[:, :, :, pl.ds(v * C1 + k * 128, 128)] = act[k, :, :, pl.ds(v, 16), :].astype(
                jnp.bfloat16
            )
    middle = [first[k, :, 1:5, pl.ds(1, 16), :].reshape(256, 128) for k in range(parts)]
    total = jnp.concatenate(middle, axis=1) + b2_ref[...].reshape(1, C1)
    for tap in range(9):
        t, u = divmod(tap, 3)
        rows = wide[t : t + 4, u : u + 4].reshape(256, 3 * C1)
        pltpu.make_async_copy(w2_ref.at[tap], w2_buf.at[tap], sems.at[tap]).wait()
        total = total + jnp.dot(rows, w2_buf[tap], preferred_element_type=jnp.float32)
    for k in range(parts):
        for f in range(F):
            for i in range(4):
                at = f * 64 + i * 16
                done[k, f, pl.ds(i, 16, stride=8), :] = total[at : at + 16, k * 128 : k * 128 + 128]
        cells = done[k, :, 0:96, :].reshape(F, 12, 8, 128)[:, :, 0:4]
        out_ref[:, :, :, pl.ds(k * 128, 128)] = cells.astype(jnp.bfloat16)


def tail(*args):
    specs = [pl.BlockSpec(memory_space=pltpu.VMEM)] * len(args)
    specs[7] = pl.BlockSpec(memory_space=pltpu.SMEM)
    specs[13] = pl.BlockSpec(memory_space=pl.ANY)
    return pl.pallas_call(
        tail_kernel,
        in_specs=specs,
        out_specs=[pl.BlockSpec(memory_space=pltpu.VMEM)] * 2,
        out_shape=[
            jax.ShapeDtypeStruct((F, 12, 4, LAT), jnp.float32),
            jax.ShapeDtypeStruct((F, 12, 4, C1), jnp.bfloat16),
        ],
        scratch_shapes=[
            pltpu.VMEM((F, 4, 8, 128), jnp.float32),
            pltpu.VMEM((6, 4, 16, 128), jnp.float32),
            pltpu.VMEM((F, 128, 128), jnp.float32),
            pltpu.VMEM((C1 // 128, F, 6, 24, 128), jnp.float32),
            pltpu.VMEM((C1 // 128, 6, 6, 24, 128), jnp.float32),
            pltpu.VMEM((6, 6, 16, 3 * C1), jnp.bfloat16),
            pltpu.VMEM((C1 // 128, F, 128, 128), jnp.float32),
            pltpu.VMEM((16, 128), jnp.float32),
            pltpu.VMEM((6, 4, 8, 128), jnp.float32),
            pltpu.VMEM((2, 6, 16, C1), jnp.float32),
            pltpu.VMEM((3, 16 * LAT, 4 * C1), jnp.bfloat16),
            pltpu.VMEM((9, 3 * C1, C1), jnp.bfloat16),
            pltpu.SemaphoreType.DMA((9,)),
        ],
        compiler_params=pltpu.CompilerParams(vmem_limit_bytes=53 << 20),
    )(*args)


def window_weights(w_ref, out_ref):
    out_ref[...] = jnp.zeros(out_ref.shape, out_ref.dtype)
    for t in range(3):
        for u in range(3):
            for v in range(3):
                taps = w_ref[t, u, v]
                for p in range(2):
                    for q in range(2):
                        (dr, a), (dc, b) = divmod(p + u, 2), divmod(q + v, 2)
                        at = dr * 128 + dc * 64 + a * 32 + b * 16
                        out_ref[t, pl.ds(at, LAT), pl.ds((2 * p + q) * C1, C1)] = taps


def put_frames(ref, rows, tokens):
    count = tokens[0].shape[0]
    low = lax.broadcasted_iota(jnp.int32, (count, 128), 1) < 64
    for i in range(2):
        for h in range(2):
            one = tokens[i + 2 * h]
            two = pltpu.roll(tokens[i + 4], 64, axis=1) if h == 0 else jnp.zeros_like(one)
            ref[i, pl.ds(rows + h * count, count), 384:512] = jnp.where(low, one, two)


def get_frames(ref, rows, count):
    out = {}
    for i in range(2):
        for h in range(2):
            both = ref[i, pl.ds(rows + h * count, count), 384:512]
            out[i + 2 * h] = both
            if h == 0:
                out[i + 4] = pltpu.roll(both, 64, axis=1)
    return [out[f] for f in range(6)]


def edge_rows_kernel(noisy_ref, cache_ref, mid_ref, tok_ref, down_ref, up_ref, cells):
    cells[...] = jnp.zeros(cells.shape, jnp.float32)
    cells[0:2, :, 0:12, 0:LAT] = cache_ref[...].astype(jnp.float32)
    cells[2:6, :, 0:12, 0:LAT] = noisy_ref[...]
    lane = lax.broadcasted_iota(jnp.int32, (8, 128), 1)
    tokens = {}
    for r in range(2):
        for f in range(6):
            token = jnp.zeros((8, 128), jnp.float32)
            for k in range(4):
                part = cells[f, 2 * r + k // 2, pl.ds(k % 2, 8, stride=2), :]
                part = pltpu.roll(part, LAT * k, axis=1) if k else part
                token = jnp.where((lane >= LAT * k) & (lane < LAT * k + LAT), part, token)
            tok_ref[f, r] = token
            tokens[f, r] = token
    for ref, row, r in ((down_ref, 3, 1), (up_ref, 0, 0)):
        ref[...] = jnp.zeros(ref.shape, jnp.float32)
        ref[:, 0:12, 0:C1] = mid_ref[:, row].astype(jnp.float32)
        put_frames(ref, 0, [tokens[f, r] for f in range(6)])


def edge_cols_kernel(tok_ref, mid_ref, above_ref, below_ref, toks, mids, right_ref, left_ref):
    above, below = get_frames(above_ref, 0, 8), get_frames(below_ref, 0, 8)
    for f in range(6):
        toks[f, 0] = above[f]
        toks[f, 1] = tok_ref[f, 0]
        toks[f, 2] = tok_ref[f, 1]
        toks[f, 3] = below[f]
    mids[...] = jnp.zeros(mids.shape, jnp.float32)
    mids[:, 0, 0:12, :] = above_ref[:, 0:12, 0:C1]
    mids[:, 1:5, 0:12, :] = mid_ref[...].astype(jnp.float32)
    mids[:, 5, 0:12, :] = below_ref[:, 0:12, 0:C1]
    for ref, token, col in ((right_ref, 5, 11), (left_ref, 0, 0)):
        ref[...] = jnp.zeros(ref.shape, jnp.float32)
        for i in range(2):
            for row in range(6):
                ref[i, pl.ds(row, 1), 0:C1] = mids[i, row, pl.ds(col, 1), :]
        for r in range(4):
            put_rows(ref, r, [toks[f, r, pl.ds(token, 1), :] for f in range(6)])


def put_rows(ref, r, tokens):
    low = lax.broadcasted_iota(jnp.int32, (1, 128), 1) < 64
    for i in range(2):
        for h in range(2):
            one = tokens[i + 2 * h]
            two = pltpu.roll(tokens[i + 4], 64, axis=1) if h == 0 else jnp.zeros_like(one)
            ref[i, pl.ds(4 * h + r, 1), 384:512] = jnp.where(low, one, two)


def place(toks, mids, left_ref, right_ref, cells_ref, cache_ref):
    cells_ref[...] = jnp.zeros(cells_ref.shape, jnp.float32)
    cache_ref[...] = jnp.zeros(cache_ref.shape, jnp.float32)
    for f in range(6):
        for r in range(4):
            cells_ref[f, r, 1:7, :] = toks[f, r, 0:6, :]
    cache_ref[:, :, 1:13, :] = mids[:, :, 0:12, :]
    for ref, token, col in ((left_ref, 0, 0), (right_ref, 7, 13)):
        frames = get_frames(ref, 0, 4)
        for f in range(6):
            for r in range(4):
                cells_ref[f, r, pl.ds(token, 1), :] = frames[f][r : r + 1]
        for i in range(2):
            for row in range(6):
                cache_ref[i, row, pl.ds(col, 1), :] = ref[i, pl.ds(row, 1), 0:C1]


def small_call(kernel, shapes, scratch=()):
    return pl.pallas_call(
        kernel,
        out_shape=[jax.ShapeDtypeStruct(shape, jnp.float32) for shape in shapes],
        scratch_shapes=[pltpu.VMEM(shape, jnp.float32) for shape in scratch],
        compiler_params=pltpu.CompilerParams(vmem_limit_bytes=8 << 20),
    )


def along(axis, step):
    count = lax.axis_size(axis)
    return [(i, i + step) for i in range(count) if 0 <= i + step < count]


def halo_rows(noisy, cache_in, cache_mid):
    edge = (2, 16, 512)
    toks, down, up = small_call(
        edge_rows_kernel, [(6, 2, 8, 128), edge, edge], [(6, 4, 16, 128)]
    )(noisy, cache_in, cache_mid)
    above = lax.ppermute(down, SEQ, along(SEQ, 1))
    below = lax.ppermute(up, SEQ, along(SEQ, -1))
    side = (2, 8, 512)
    return small_call(edge_cols_kernel, [(6, 4, 8, 128), (2, 6, 16, C1), side, side])(
        toks, cache_mid, above, below
    )


def pack_kernel(q_ref, k_ref, v_ref, out_ref):
    for h in range(out_ref.shape[0]):
        lanes = pl.ds(h * HEAD_DIM, HEAD_DIM)
        out_ref[h, :, 0:128] = k_ref[:, lanes]
        out_ref[h, :, 128:256] = v_ref[:, lanes]
        out_ref[h, :, 256:384] = q_ref[:, lanes]


def pack(query_vectors, key_vectors, value_vectors):
    tokens, width = query_vectors.shape
    heads = width // HEAD_DIM
    block = pl.BlockSpec((tokens, width // 2), lambda i: (0, i))
    return pl.pallas_call(
        pack_kernel,
        grid=(2,),
        in_specs=[block] * 3,
        out_specs=pl.BlockSpec((heads // 2, tokens, 3 * HEAD_DIM), lambda i: (i, 0, 0)),
        out_shape=jax.ShapeDtypeStruct((heads, tokens, 3 * HEAD_DIM), jnp.bfloat16),
    )(query_vectors, key_vectors, value_vectors)


def merge_kernel(own_ref, oth_ref, out_ref, vel_ref, piece_ref):
    own, oth = own_ref[...], oth_ref[...]
    gap = pltpu.roll(oth - own, 64, axis=1)
    share = 1.0 / (1.0 + jnp.exp2(gap))
    vel = own * share + oth * (1.0 - share)
    lane = lax.broadcasted_iota(jnp.int32, vel.shape, 1)
    vel_ref[...] = jnp.where(lane < 64, vel, pltpu.roll(vel, 64, axis=1))
    low = lax.broadcasted_iota(jnp.int32, (16, 128), 1) < 64
    zero = jnp.zeros((16, 128), jnp.float32)

    def column(r, at):
        if at < 0 or at >= 48:
            return zero
        return vel_ref[pl.ds(r * 48 + at, 16, stride=96), :]

    for b in range(8):
        for r in range(2):
            for c in range(4):
                at = 6 * b - 1 + c
                both = jnp.where(low, column(r, at), column(r, at + 4))
                for y in range(4):
                    piece_ref[y, b, pl.ds(r * 16 + c, 4, stride=4), :] = both[y * 4 : y * 4 + 4]
    out_ref[...] = piece_ref[...].astype(jnp.bfloat16)


def merge(own, oth):
    rows = own.shape[0]
    whole = pl.BlockSpec((rows, 128), lambda: (0, 0))
    shape = (4, 8, 32, 128)
    return pl.pallas_call(
        merge_kernel,
        in_specs=[whole, whole],
        out_specs=pl.BlockSpec(shape, lambda: (0, 0, 0, 0)),
        out_shape=jax.ShapeDtypeStruct(shape, jnp.bfloat16),
        scratch_shapes=[
            pltpu.VMEM((rows, 128), jnp.float32),
            pltpu.VMEM(shape, jnp.float32),
        ],
        compiler_params=pltpu.CompilerParams(vmem_limit_bytes=24 << 20),
    )(own, oth)


def head_sum_kernel(parts_ref, mine_ref, near_ref, apart_ref):
    total = parts_ref[0].astype(jnp.float32)
    for h in range(1, parts_ref.shape[0]):
        total = total + parts_ref[h].astype(jnp.float32)
    mine_ref[...] = total
    even = lax.axis_index("core") == 0
    near_ref[...] = jnp.where(even, total[16:32], total[0:16])
    apart_ref[...] = jnp.where(even, total[0:16], total[16:32])


def head_sum(parts):
    return small_call(head_sum_kernel, [(32, 128), (16, 128), (16, 128)])(parts)


def attention(query_vectors, key_vectors, value_vectors, weight_head, inputs):
    packed = pack(query_vectors, key_vectors, value_vectors)
    packed, inputs = lax.optimization_barrier((packed, inputs))
    noisy, cache_in, cache_mid = inputs
    rows = halo_rows(noisy, cache_in, cache_mid)
    heads, tokens = packed.shape[:2]
    moved = lax.all_to_all(packed, HEAD, split_axis=0, concat_axis=0, tiled=True)
    moved = moved.reshape(heads * tokens, 3 * HEAD_DIM)
    swap = [(0, 1), (1, 0)]
    right = [(i, (i + 1) % 4) for i in range(4)]
    left = [((i + 1) % 4, i) for i in range(4)]
    mid = moved.shape[0] // 2
    a, b, q_own = moved[:mid, :256], moved[mid:, :256], moved[:, 256:]
    a, b, q_own, rows = lax.optimization_barrier((a, b, q_own, rows))
    left_a = lax.ppermute(a, "y", right)
    right_b = lax.ppermute(b, "y", left)
    q_oth = lax.ppermute(q_own, "core", swap)
    state = flash(moved, q_oth, [moved])
    toks, mids, to_right, to_left = rows
    state, a, b = lax.optimization_barrier((state, a, b))
    left_b = lax.ppermute(b, "y", right)
    right_a = lax.ppermute(a, "y", left)
    state = flash(moved, q_oth, [left_a, right_b], state)
    state, left_a, right_b = lax.optimization_barrier((state, left_a, right_b))
    far = [lax.ppermute(left_a, "y", right), lax.ppermute(right_b, "y", left)]
    state = flash(moved, q_oth, [left_b, right_a], state)
    weight = weight_head.T
    oth = flash_last(q_oth, 0, far, state, 1, weight)
    oth, state = lax.optimization_barrier((oth, state))
    oth = lax.ppermute(oth, "core", swap)
    own = flash_last(moved, 2, far, state, 0, weight)
    partial = merge(own, oth).reshape(heads, 32, 128)
    partial, to_right, to_left = lax.optimization_barrier((partial, to_right, to_left))
    before = lax.ppermute(to_right, BLK, along(BLK, 1))
    after = lax.ppermute(to_left, BLK, along(BLK, -1))
    parts = lax.all_to_all(partial, HEAD, split_axis=0, concat_axis=0, tiled=True)
    return head_sum(parts), (toks, mids, before, after)


def shards(
    query_vectors,
    key_vectors,
    value_vectors,
    weight_head,
    noisy_latent,
    noise_level,
    latent_mean,
    latent_scale,
    cache_in,
    weight_in,
    bias_in,
    norm_gain,
    cache_mid,
    weight_mid,
    bias_mid,
):
    (mine, near, apart), (toks, mids, before, after) = attention(
        query_vectors,
        key_vectors,
        value_vectors,
        weight_head,
        (noisy_latent, cache_in, cache_mid),
    )

    count = lax.axis_size(SEQ)
    near = lax.ppermute(near, SEQ, [(i, i ^ 1) for i in range(count)])
    pairs = [(i, i + 1) for i in range(1, count - 1, 2)]
    pairs += [(j, i) for i, j in pairs]
    apart = lax.ppermute(apart, SEQ, pairs)
    denoised, features = tail(
        near,
        mine,
        apart,
        toks,
        mids,
        before,
        after,
        noise_level,
        latent_scale,
        latent_mean,
        weight_in,
        bias_in,
        norm_gain,
        weight_mid.reshape(9, 3 * C1, C1),
        bias_mid,
    )
    return denoised.transpose(0, 2, 1, 3), features.transpose(0, 2, 1, 3)


def solution(mesh):
    inner = Mesh(mesh.devices.reshape(4, 4, 2, 2, 4), SHARD)
    tokens, tile = P(SHARD, None), P(None, SEQ, BLK, None)
    in_specs = (
        tokens,
        tokens,
        tokens,
        P(),
        tile,
        P(),
        P(),
        P(),
        tile,
        P(),
        P(),
        P(),
        tile,
        P(),
        P(),
    )
    return jax.shard_map(
        shards, mesh=inner, in_specs=in_specs, out_specs=(tile, tile), check_vma=False
    )
```

```python
import functools
import math

import jax
import jax.numpy as jnp
from jax import lax
from jax.experimental import pallas as pl
from jax.experimental.pallas import tpu as pltpu
from jax.sharding import Mesh
from jax.sharding import PartitionSpec as P

HEAD_DIM = 128
LAT = 16
C1 = 384
F = 4
EPSILON = 1e-06

SEQ = ("y", "zh", "core")
BLK = ("zl", "x")
HEAD = ("zh", "zl", "x")
SHARD = SEQ + BLK

TILE = 1536
SUB = 256
CHUNK = 768
NT = (((1,), (1,)), ((), ()))


def mesh_index(axes):
    index = 0
    for axis in axes:
        index = index * lax.axis_size(axis) + lax.axis_index(axis)
    return index


def lane_max(s):
    t = s[:, :128]
    for j in range(1, s.shape[1] // 128):
        t = jnp.maximum(t, s[:, j * 128 : (j + 1) * 128])
    return jnp.max(t, axis=1, keepdims=True)


def flash_kernel(first, last, n_kv, half, *refs):
    q_ref, refs = refs[0], refs[1:]
    if not last:
        qx_ref, refs = refs[0], refs[1:]
    kv_refs, refs = refs[:n_kv], refs[n_kv:]
    if not first:
        st_ref, refs = refs[0], refs[1:]
    if last:
        w_ref, u_ref = refs
        query = q_ref[...]
        own = w_ref[:, pl.ds(pl.multiple_of(mesh_index(HEAD) * HEAD_DIM, HEAD_DIM), HEAD_DIM)]
        weight = jnp.concatenate([own, jnp.zeros_like(own)], axis=0)
    else:
        (so_ref,) = refs
        query = jnp.where(pl.program_id(0) < half, q_ref[...], qx_ref[...])
    scale = math.log2(math.e) / math.sqrt(HEAD_DIM)
    qf = query.astype(jnp.float32) * scale
    q_hi = qf.astype(jnp.bfloat16)
    q_lo = (qf - q_hi.astype(jnp.float32)).astype(jnp.bfloat16)
    q = jnp.concatenate([q_hi, q_lo], axis=1)
    subs = TILE // SUB
    tops, accs = [], []
    for r in range(subs):
        if first:
            tops.append(jnp.full((SUB, 128), -1e30, jnp.float32))
            accs.append(jnp.zeros((SUB, 256), jnp.float32))
        else:
            st = st_ref[pl.ds(r * SUB, SUB), :]
            acc_l = st[:, 128:]
            lane = lax.broadcasted_iota(jnp.int32, (SUB, 128), 1)
            total = jnp.max(jnp.where(lane < 64, acc_l, -1e30), axis=1, keepdims=True)
            top = jnp.max(jnp.where(lane < 64, -1e30, acc_l), axis=1, keepdims=True)
            tops.append(jnp.broadcast_to(top, (SUB, 128)))
            accs.append(
                jnp.concatenate([st[:, :128], jnp.broadcast_to(total, (SUB, 128))], axis=1)
            )
    items = [
        (r, b, c)
        for r in range(subs)
        for b in range(n_kv)
        for c in range(kv_refs[b].shape[0] // CHUNK)
    ]
    ones = jnp.ones((CHUNK, 128), jnp.bfloat16)

    def score(item):
        r, b, c = item
        k = kv_refs[b][pl.ds(c * CHUNK, CHUNK), :128]
        return lax.dot_general(
            q[r * SUB : (r + 1) * SUB],
            jnp.concatenate([k, k], axis=1),
            NT,
            preferred_element_type=jnp.float32,
        )

    s = score(items[0])
    for n, (r, b, c) in enumerate(items):
        following = score(items[n + 1]) if n + 1 < len(items) else None
        top = jnp.maximum(tops[r], lane_max(s))
        p = jnp.exp2(s - top[:, :1]).astype(jnp.bfloat16)
        fade = jnp.exp2(tops[r] - top)
        v = jnp.concatenate([kv_refs[b][pl.ds(c * CHUNK, CHUNK), 128:], ones], axis=1)
        accs[r] = accs[r] * jnp.concatenate([fade, fade], axis=1) + jnp.dot(
            p, v, preferred_element_type=jnp.float32
        )
        tops[r] = top
        s = following
    lane = lax.broadcasted_iota(jnp.int32, (SUB, 128), 1)
    for r in range(subs):
        if last:
            total = accs[r][:, 128:]
            mixed = (accs[r][:, :128] / total).astype(jnp.bfloat16)
            u = lax.dot_general(mixed, weight, NT, preferred_element_type=jnp.float32)
            u_ref[pl.ds(r * SUB, SUB), :] = jnp.where(lane < 64, u, tops[r] + jnp.log2(total))
        else:
            so_ref[pl.ds(r * SUB, SUB), :] = jnp.concatenate(
                [accs[r][:, :128], jnp.where(lane < 64, accs[r][:, 128:], tops[r])], axis=1
            )


def flash(q_own, q_oth, kvs, state=None):
    rows = q_oth.shape[0]
    half = rows // TILE
    keys = sum(kv.shape[0] for kv in kvs)
    in_specs = [
        pl.BlockSpec((TILE, 128), lambda i: (jnp.minimum(i, half - 1), 2)),
        pl.BlockSpec((TILE, 128), lambda i: (jnp.maximum(i - half, 0), 0)),
    ]
    in_specs += [pl.BlockSpec((kv.shape[0], 256), lambda i: (0, 0)) for kv in kvs]
    args = [q_own, q_oth, *kvs]
    if state is not None:
        in_specs.append(pl.BlockSpec((TILE, 256), lambda i: (i, 0)))
        args.append(state)
    return pl.pallas_call(
        functools.partial(flash_kernel, state is None, False, len(kvs), half),
        grid=(2 * half,),
        in_specs=in_specs,
        out_specs=pl.BlockSpec((TILE, 256), lambda i: (i, 0)),
        out_shape=jax.ShapeDtypeStruct((2 * rows, 256), jnp.float32),
        compiler_params=pltpu.CompilerParams(vmem_limit_bytes=20 << 20),
        cost_estimate=flash_cost(2 * rows, keys),
    )(*args)


def flash_last(query, lane_block, kvs, state, half_at, weight):
    rows = query.shape[0]
    half = rows // TILE
    keys = sum(kv.shape[0] for kv in kvs)
    in_specs = [pl.BlockSpec((TILE, 128), lambda i: (i, lane_block))]
    in_specs += [pl.BlockSpec((kv.shape[0], 256), lambda i: (0, 0)) for kv in kvs]
    in_specs += [
        pl.BlockSpec((TILE, 256), lambda i: (i + half_at * half, 0)),
        pl.BlockSpec(weight.shape, lambda i: (0, 0)),
    ]
    return pl.pallas_call(
        functools.partial(flash_kernel, False, True, len(kvs), half),
        grid=(half,),
        in_specs=in_specs,
        out_specs=pl.BlockSpec((TILE, 128), lambda i: (i, 0)),
        out_shape=jax.ShapeDtypeStruct((rows, 128), jnp.float32),
        compiler_params=pltpu.CompilerParams(vmem_limit_bytes=20 << 20),
        cost_estimate=flash_cost(rows, keys),
    )(query, *kvs, state, weight)


def flash_cost(rows, keys):
    return pl.CostEstimate(
        flops=rows * keys * 1024, bytes_accessed=rows * 2048, transcendentals=rows * keys
    )


def inside(at, low, high, before, after):
    return ((at > low) | before) & ((at < high) | after)


def tail_kernel(
    near_ref,
    mine_ref,
    apart_ref,
    toks,
    mids,
    before_ref,
    after_ref,
    level_ref,
    scale_ref,
    mean_ref,
    w1_ref,
    b1_ref,
    gain_ref,
    w2_ref,
    b2_ref,
    den_ref,
    out_ref,
    vel,
    lat,
    den,
    first,
    act,
    wide,
    done,
    vecs,
    cells_ref,
    mid_ref,
    w1_buf,
    w2_buf,
    sems,
):
    for tap in range(9):
        pltpu.make_async_copy(w2_ref.at[tap], w2_buf.at[tap], sems.at[tap]).start()
    window_weights(w1_ref, w1_buf)
    place(toks, mids, before_ref, after_ref, cells_ref, mid_ref)
    even = lax.axis_index("core") == 0
    at_row, at_col = mesh_index(SEQ), mesh_index(BLK)
    up, down = at_row > 0, at_row < lax.axis_size(SEQ) - 1
    before, after = at_col > 0, at_col < lax.axis_size(BLK) - 1
    above = jnp.where(even, apart_ref[...], near_ref[...])
    below = jnp.where(even, near_ref[...], apart_ref[...])
    for at, rows in enumerate((above, mine_ref[0:16, :], mine_ref[16:32, :], below)):
        turned = pltpu.roll(rows, 64, axis=1)
        for f in range(F):
            vel[f, at, 0:4, :] = rows[f * 4 : f * 4 + 4]
            vel[f, at, 4:8, :] = turned[f * 4 : f * 4 + 4]
    vecs[...] = jnp.zeros(vecs.shape, jnp.float32)
    vecs[0:1, 0:LAT] = scale_ref[...].reshape(1, LAT)
    vecs[8:9, 0:LAT] = mean_ref[...].reshape(1, LAT)
    base = vecs[...]
    tiled = base + pltpu.roll(base, LAT, axis=1)
    tiled = tiled + pltpu.roll(tiled, 2 * LAT, axis=1)
    scale, mean = tiled[0:1, 0:64], tiled[8:9, 0:64]
    denoised = cells_ref[2:6, :, :, 0:64] - level_ref[0] * vel[:, :, :, 0:64]
    row = lax.broadcasted_iota(jnp.int32, denoised.shape, 1)
    col = lax.broadcasted_iota(jnp.int32, denoised.shape, 2)
    kept = inside(row, 0, 3, up, down) & inside(col, 0, 7, before, after)
    latent = jnp.where(kept, denoised * scale + mean, 0.0)
    for k in range(4):
        part = jnp.concatenate([denoised, denoised], axis=3).reshape(F * 32, 128)
        part = pltpu.roll(part, 128 - LAT * k, axis=1) if k else part
        part = part.reshape(F, 4, 8, 128)
        for f in range(F):
            for r in range(2):
                rows = pl.ds(8 * (k % 2) + 2 * r + k // 2, 8, stride=16)
                den[f, rows, :] = part[f, r + 1]
    den_ref[...] = den[:, 16:112, :].reshape(F, 12, 8, 128)[:, :, 0:4, 0:LAT]
    lat[...] = jnp.zeros(lat.shape, jnp.float32)
    lat[0:2, :, 0:8, 0:64] = cells_ref[0:2, :, :, 0:64]
    lat[2:6, :, 0:8, 0:64] = latent.astype(jnp.bfloat16).astype(jnp.float32)
    here = lat[:, :, 0:8, :].reshape(192, 128)
    right = pltpu.roll(lat[:, :, 1:9, :].reshape(192, 128), 64, axis=1)
    lane = lax.broadcasted_iota(jnp.int32, (192, 128), 1)
    pair = jnp.where(lane < 64, here, right).reshape(6, 4, 8, 128)
    lower = jnp.concatenate([pair[:, 1:4], pair[:, 3:4]], axis=1)
    window = jnp.concatenate([pair, lower], axis=3).reshape(192, 256).astype(jnp.bfloat16)
    parts = C1 // 128
    for k in range(parts):
        act[k, 0:2, :, 0:16, :] = mid_ref[:, :, :, pl.ds(k * 128, 128)]
    gain = gain_ref[...].reshape(1, C1)
    for p in range(2):
        for q in range(2):
            lanes = pl.ds((2 * p + q) * C1, C1)
            value = b1_ref[...].reshape(1, C1)
            for t in range(3):
                value = value + jnp.dot(
                    window[t * 32 : t * 32 + 128],
                    w1_buf[t, :, lanes],
                    preferred_element_type=jnp.float32,
                )
            power = jnp.mean(value * value, axis=1, keepdims=True)
            normed = value * lax.rsqrt(power + EPSILON) * gain
            active = (normed / (1.0 + jnp.exp(-normed))).reshape(F, 32, C1)
            at = lax.broadcasted_iota(jnp.int32, (32, C1), 0)
            kept = inside(2 * (at // 8) + p, 0, 5, up, down)
            kept = kept & inside(2 * (at % 8) + q, 0, 13, before, after)
            active = jnp.where(kept, active, 0.0)
            value = value.reshape(F, 4, 8, C1)
            active = active.reshape(F, 4, 8, C1)
            for r in range(3):
                cols = pl.ds(q, 8, stride=2)
                for k in range(parts):
                    part = slice(k * 128, k * 128 + 128)
                    for f in range(F):
                        first[k, f, 2 * r + p, cols, :] = value[f, r, :, part]
                        act[k, f + 2, 2 * r + p, cols, :] = active[f, r, :, part]
    for v in range(3):
        for k in range(parts):
            wide[:, :, :, pl.ds(v * C1 + k * 128, 128)] = act[k, :, :, pl.ds(v, 16), :].astype(
                jnp.bfloat16
            )
    middle = [first[k, :, 1:5, pl.ds(1, 16), :].reshape(256, 128) for k in range(parts)]
    total = jnp.concatenate(middle, axis=1) + b2_ref[...].reshape(1, C1)
    for tap in range(9):
        t, u = divmod(tap, 3)
        rows = wide[t : t + 4, u : u + 4].reshape(256, 3 * C1)
        pltpu.make_async_copy(w2_ref.at[tap], w2_buf.at[tap], sems.at[tap]).wait()
        total = total + jnp.dot(rows, w2_buf[tap], preferred_element_type=jnp.float32)
    for k in range(parts):
        for f in range(F):
            for i in range(4):
                at = f * 64 + i * 16
                done[k, f, pl.ds(i, 16, stride=8), :] = total[at : at + 16, k * 128 : k * 128 + 128]
        cells = done[k, :, 0:96, :].reshape(F, 12, 8, 128)[:, :, 0:4]
        out_ref[:, :, :, pl.ds(k * 128, 128)] = cells.astype(jnp.bfloat16)


def tail(*args):
    specs = [pl.BlockSpec(memory_space=pltpu.VMEM)] * len(args)
    specs[7] = pl.BlockSpec(memory_space=pltpu.SMEM)
    specs[13] = pl.BlockSpec(memory_space=pl.ANY)
    return pl.pallas_call(
        tail_kernel,
        in_specs=specs,
        out_specs=[pl.BlockSpec(memory_space=pltpu.VMEM)] * 2,
        out_shape=[
            jax.ShapeDtypeStruct((F, 12, 4, LAT), jnp.float32),
            jax.ShapeDtypeStruct((F, 12, 4, C1), jnp.bfloat16),
        ],
        scratch_shapes=[
            pltpu.VMEM((F, 4, 8, 128), jnp.float32),
            pltpu.VMEM((6, 4, 16, 128), jnp.float32),
            pltpu.VMEM((F, 144, 128), jnp.float32),
            pltpu.VMEM((C1 // 128, F, 6, 24, 128), jnp.float32),
            pltpu.VMEM((C1 // 128, 6, 6, 24, 128), jnp.float32),
            pltpu.VMEM((6, 6, 16, 3 * C1), jnp.bfloat16),
            pltpu.VMEM((C1 // 128, F, 136, 128), jnp.float32),
            pltpu.VMEM((16, 128), jnp.float32),
            pltpu.VMEM((6, 4, 8, 128), jnp.float32),
            pltpu.VMEM((2, 6, 16, C1), jnp.float32),
            pltpu.VMEM((3, 16 * LAT, 4 * C1), jnp.bfloat16),
            pltpu.VMEM((9, 3 * C1, C1), jnp.bfloat16),
            pltpu.SemaphoreType.DMA((9,)),
        ],
        compiler_params=pltpu.CompilerParams(vmem_limit_bytes=53 << 20),
    )(*args)


def window_weights(w_ref, out_ref):
    out_ref[...] = jnp.zeros(out_ref.shape, out_ref.dtype)
    for t in range(3):
        for u in range(3):
            for v in range(3):
                taps = w_ref[t, u, v]
                for p in range(2):
                    for q in range(2):
                        (dr, a), (dc, b) = divmod(p + u, 2), divmod(q + v, 2)
                        at = dr * 128 + dc * 64 + a * 32 + b * 16
                        out_ref[t, pl.ds(at, LAT), pl.ds((2 * p + q) * C1, C1)] = taps


def put_frames(ref, rows, tokens):
    count = tokens[0].shape[0]
    low = lax.broadcasted_iota(jnp.int32, (count, 128), 1) < 64
    for i in range(2):
        for h in range(2):
            one = tokens[i + 2 * h]
            two = pltpu.roll(tokens[i + 4], 64, axis=1) if h == 0 else jnp.zeros_like(one)
            ref[i, pl.ds(rows + h * count, count), 384:512] = jnp.where(low, one, two)


def get_frames(ref, rows, count):
    out = {}
    for i in range(2):
        for h in range(2):
            both = ref[i, pl.ds(rows + h * count, count), 384:512]
            out[i + 2 * h] = both
            if h == 0:
                out[i + 4] = pltpu.roll(both, 64, axis=1)
    return [out[f] for f in range(6)]


def edge_rows_kernel(noisy_ref, cache_ref, mid_ref, tok_ref, down_ref, up_ref, cells):
    cells[...] = jnp.zeros(cells.shape, jnp.float32)
    cells[0:2, :, 0:12, 0:LAT] = cache_ref[...].astype(jnp.float32)
    cells[2:6, :, 0:12, 0:LAT] = noisy_ref[...]
    lane = lax.broadcasted_iota(jnp.int32, (8, 128), 1)
    tokens = {}
    for r in range(2):
        for f in range(6):
            token = jnp.zeros((8, 128), jnp.float32)
            for k in range(4):
                part = cells[f, 2 * r + k // 2, pl.ds(k % 2, 8, stride=2), :]
                part = pltpu.roll(part, LAT * k, axis=1) if k else part
                token = jnp.where((lane >= LAT * k) & (lane < LAT * k + LAT), part, token)
            tok_ref[f, r] = token
            tokens[f, r] = token
    for ref, row, r in ((down_ref, 3, 1), (up_ref, 0, 0)):
        ref[...] = jnp.zeros(ref.shape, jnp.float32)
        ref[:, 0:12, 0:C1] = mid_ref[:, row].astype(jnp.float32)
        put_frames(ref, 0, [tokens[f, r] for f in range(6)])


def edge_cols_kernel(tok_ref, mid_ref, above_ref, below_ref, toks, mids, right_ref, left_ref):
    above, below = get_frames(above_ref, 0, 8), get_frames(below_ref, 0, 8)
    for f in range(6):
        toks[f, 0] = above[f]
        toks[f, 1] = tok_ref[f, 0]
        toks[f, 2] = tok_ref[f, 1]
        toks[f, 3] = below[f]
    mids[...] = jnp.zeros(mids.shape, jnp.float32)
    mids[:, 0, 0:12, :] = above_ref[:, 0:12, 0:C1]
    mids[:, 1:5, 0:12, :] = mid_ref[...].astype(jnp.float32)
    mids[:, 5, 0:12, :] = below_ref[:, 0:12, 0:C1]
    for ref, token, col in ((right_ref, 5, 11), (left_ref, 0, 0)):
        ref[...] = jnp.zeros(ref.shape, jnp.float32)
        for i in range(2):
            for row in range(6):
                ref[i, pl.ds(row, 1), 0:C1] = mids[i, row, pl.ds(col, 1), :]
        for r in range(4):
            put_rows(ref, r, [toks[f, r, pl.ds(token, 1), :] for f in range(6)])


def put_rows(ref, r, tokens):
    low = lax.broadcasted_iota(jnp.int32, (1, 128), 1) < 64
    for i in range(2):
        for h in range(2):
            one = tokens[i + 2 * h]
            two = pltpu.roll(tokens[i + 4], 64, axis=1) if h == 0 else jnp.zeros_like(one)
            ref[i, pl.ds(4 * h + r, 1), 384:512] = jnp.where(low, one, two)


def place(toks, mids, left_ref, right_ref, cells_ref, cache_ref):
    cells_ref[...] = jnp.zeros(cells_ref.shape, jnp.float32)
    cache_ref[...] = jnp.zeros(cache_ref.shape, jnp.float32)
    for f in range(6):
        for r in range(4):
            cells_ref[f, r, 1:7, :] = toks[f, r, 0:6, :]
    cache_ref[:, :, 1:13, :] = mids[:, :, 0:12, :]
    for ref, token, col in ((left_ref, 0, 0), (right_ref, 7, 13)):
        frames = get_frames(ref, 0, 4)
        for f in range(6):
            for r in range(4):
                cells_ref[f, r, pl.ds(token, 1), :] = frames[f][r : r + 1]
        for i in range(2):
            for row in range(6):
                cache_ref[i, row, pl.ds(col, 1), :] = ref[i, pl.ds(row, 1), 0:C1]


def small_call(kernel, shapes, scratch=()):
    return pl.pallas_call(
        kernel,
        out_shape=[jax.ShapeDtypeStruct(shape, jnp.float32) for shape in shapes],
        scratch_shapes=[pltpu.VMEM(shape, jnp.float32) for shape in scratch],
        compiler_params=pltpu.CompilerParams(vmem_limit_bytes=8 << 20),
    )


def along(axis, step):
    count = lax.axis_size(axis)
    return [(i, i + step) for i in range(count) if 0 <= i + step < count]


def halo_rows(noisy, cache_in, cache_mid):
    edge = (2, 16, 512)
    toks, down, up = small_call(
        edge_rows_kernel, [(6, 2, 8, 128), edge, edge], [(6, 4, 24, 128)]
    )(noisy, cache_in, cache_mid)
    above = lax.ppermute(down, SEQ, along(SEQ, 1))
    below = lax.ppermute(up, SEQ, along(SEQ, -1))
    side = (2, 8, 512)
    return small_call(edge_cols_kernel, [(6, 4, 8, 128), (2, 6, 16, C1), side, side])(
        toks, cache_mid, above, below
    )


def pack_kernel(q_ref, k_ref, v_ref, out_ref):
    for h in range(out_ref.shape[0]):
        lanes = pl.ds(h * HEAD_DIM, HEAD_DIM)
        out_ref[h, :, 0:128] = k_ref[:, lanes]
        out_ref[h, :, 128:256] = v_ref[:, lanes]
        out_ref[h, :, 256:384] = q_ref[:, lanes]


def pack(query_vectors, key_vectors, value_vectors):
    tokens, width = query_vectors.shape
    heads = width // HEAD_DIM
    block = pl.BlockSpec((tokens, width // 2), lambda i: (0, i))
    return pl.pallas_call(
        pack_kernel,
        grid=(2,),
        in_specs=[block] * 3,
        out_specs=pl.BlockSpec((heads // 2, tokens, 3 * HEAD_DIM), lambda i: (i, 0, 0)),
        out_shape=jax.ShapeDtypeStruct((heads, tokens, 3 * HEAD_DIM), jnp.bfloat16),
    )(query_vectors, key_vectors, value_vectors)


def merge_kernel(own_ref, oth_ref, out_ref, vel_ref, piece_ref):
    own, oth = own_ref[...], oth_ref[...]
    gap = pltpu.roll(oth - own, 64, axis=1)
    share = 1.0 / (1.0 + jnp.exp2(gap))
    vel = own * share + oth * (1.0 - share)
    lane = lax.broadcasted_iota(jnp.int32, vel.shape, 1)
    vel_ref[0 : vel.shape[0], :] = jnp.where(lane < 64, vel, pltpu.roll(vel, 64, axis=1))
    low = lax.broadcasted_iota(jnp.int32, (16, 128), 1) < 64
    zero = jnp.zeros((16, 128), jnp.float32)

    def column(r, at):
        if at < 0 or at >= 48:
            return zero
        return vel_ref[pl.ds(r * 48 + at, 16, stride=96), :]

    for b in range(8):
        for r in range(2):
            for c in range(4):
                at = 6 * b - 1 + c
                both = jnp.where(low, column(r, at), column(r, at + 4))
                for y in range(4):
                    piece_ref[y, b, pl.ds(r * 16 + c, 4, stride=4), :] = both[y * 4 : y * 4 + 4]
    out_ref[...] = piece_ref[:, :, 0:32, :].astype(jnp.bfloat16)


def merge(own, oth):
    rows = own.shape[0]
    whole = pl.BlockSpec((rows, 128), lambda: (0, 0))
    shape = (4, 8, 32, 128)
    return pl.pallas_call(
        merge_kernel,
        in_specs=[whole, whole],
        out_specs=pl.BlockSpec(shape, lambda: (0, 0, 0, 0)),
        out_shape=jax.ShapeDtypeStruct(shape, jnp.bfloat16),
        scratch_shapes=[
            pltpu.VMEM((rows + 96, 128), jnp.float32),
            pltpu.VMEM((4, 8, 40, 128), jnp.float32),
        ],
        compiler_params=pltpu.CompilerParams(vmem_limit_bytes=24 << 20),
    )(own, oth)


def head_sum_kernel(parts_ref, mine_ref, near_ref, apart_ref):
    total = parts_ref[0].astype(jnp.float32)
    for h in range(1, parts_ref.shape[0]):
        total = total + parts_ref[h].astype(jnp.float32)
    mine_ref[...] = total
    even = lax.axis_index("core") == 0
    near_ref[...] = jnp.where(even, total[16:32], total[0:16])
    apart_ref[...] = jnp.where(even, total[0:16], total[16:32])


def head_sum(parts):
    return small_call(head_sum_kernel, [(32, 128), (16, 128), (16, 128)])(parts)


def attention(query_vectors, key_vectors, value_vectors, weight_head, inputs):
    packed = pack(query_vectors, key_vectors, value_vectors)
    packed, inputs = lax.optimization_barrier((packed, inputs))
    noisy, cache_in, cache_mid = inputs
    rows = halo_rows(noisy, cache_in, cache_mid)
    heads, tokens = packed.shape[:2]
    moved = lax.all_to_all(packed, HEAD, split_axis=0, concat_axis=0, tiled=True)
    moved = moved.reshape(heads * tokens, 3 * HEAD_DIM)
    swap = [(0, 1), (1, 0)]
    right = [(i, (i + 1) % 4) for i in range(4)]
    left = [((i + 1) % 4, i) for i in range(4)]
    mid = moved.shape[0] // 2
    a, b, q_own = moved[:mid, :256], moved[mid:, :256], moved[:, 256:]
    a, b, q_own, rows = lax.optimization_barrier((a, b, q_own, rows))
    left_a = lax.ppermute(a, "y", right)
    right_b = lax.ppermute(b, "y", left)
    q_oth = lax.ppermute(q_own, "core", swap)
    state = flash(moved, q_oth, [moved])
    toks, mids, to_right, to_left = rows
    state, a, b = lax.optimization_barrier((state, a, b))
    left_b = lax.ppermute(b, "y", right)
    right_a = lax.ppermute(a, "y", left)
    state = flash(moved, q_oth, [left_a, right_b], state)
    state, left_a, right_b = lax.optimization_barrier((state, left_a, right_b))
    far = [lax.ppermute(left_a, "y", right), lax.ppermute(right_b, "y", left)]
    state = flash(moved, q_oth, [left_b, right_a], state)
    weight = weight_head.T
    oth = flash_last(q_oth, 0, far, state, 1, weight)
    oth, state = lax.optimization_barrier((oth, state))
    oth = lax.ppermute(oth, "core", swap)
    own = flash_last(moved, 2, far, state, 0, weight)
    partial = merge(own, oth).reshape(heads, 32, 128)
    partial, to_right, to_left = lax.optimization_barrier((partial, to_right, to_left))
    before = lax.ppermute(to_right, BLK, along(BLK, 1))
    after = lax.ppermute(to_left, BLK, along(BLK, -1))
    parts = lax.all_to_all(partial, HEAD, split_axis=0, concat_axis=0, tiled=True)
    return head_sum(parts), (toks, mids, before, after)


def shards(
    query_vectors,
    key_vectors,
    value_vectors,
    weight_head,
    noisy_latent,
    noise_level,
    latent_mean,
    latent_scale,
    cache_in,
    weight_in,
    bias_in,
    norm_gain,
    cache_mid,
    weight_mid,
    bias_mid,
):
    (mine, near, apart), (toks, mids, before, after) = attention(
        query_vectors,
        key_vectors,
        value_vectors,
        weight_head,
        (noisy_latent, cache_in, cache_mid),
    )

    count = lax.axis_size(SEQ)
    near = lax.ppermute(near, SEQ, [(i, i ^ 1) for i in range(count)])
    pairs = [(i, i + 1) for i in range(1, count - 1, 2)]
    pairs += [(j, i) for i, j in pairs]
    apart = lax.ppermute(apart, SEQ, pairs)
    denoised, features = tail(
        near,
        mine,
        apart,
        toks,
        mids,
        before,
        after,
        noise_level,
        latent_scale,
        latent_mean,
        weight_in,
        bias_in,
        norm_gain,
        weight_mid.reshape(9, 3 * C1, C1),
        bias_mid,
    )
    return denoised.transpose(0, 2, 1, 3), features.transpose(0, 2, 1, 3)


def solution(mesh):
    inner = Mesh(mesh.devices.reshape(4, 4, 2, 2, 4), SHARD)
    tokens, tile = P(SHARD, None), P(None, SEQ, BLK, None)
    in_specs = (
        tokens,
        tokens,
        tokens,
        P(),
        tile,
        P(),
        P(),
        P(),
        tile,
        P(),
        P(),
        P(),
        tile,
        P(),
        P(),
    )
    return jax.shard_map(
        shards, mesh=inner, in_specs=in_specs, out_specs=(tile, tile), check_vma=False
    )
```
